32 devices in a mesh: grp: 1, zs: 32 (over z, y, x, core).
Axes of the slice: x: 2, y: 2, z: 4, core: 2. Of those that a mesh axis runs over, the one named last changes fastest.
Arguments:
- quark_up: bfloat16 [2, 3, 256, 384], P(None, None, 'zs', 'grp'), may hold values from -3 to 3
- quark_down: bfloat16 [2, 3, 256, 384], P(None, None, 'zs', 'grp'), may hold values from -3 to 3
- forward: bfloat16 [2, 3, 32, 6, 2, 256], P(None, None, 'zs', None, None, 'grp'), may hold values from -3 to 3
- gauge_links: bfloat16 [2, 3, 3, 32, 6, 2, 256], P(None, None, None, 'zs', None, None, 'grp'), may hold values from -2.5 to 2.5
- corner_weight: float32 [8], replicated, may hold values from 0.25 to 2
- corner_offset: int32 [8, 3], replicated, may hold values from 0 to 1, as said below
- lengths: int32 [1024], P('grp'), may hold values from 0 to 7
- separations: int32 [1024], P('grp'), may hold values from 0 to 7
- owner_map: int32 [1024, 1], P('grp'), may hold values from 0 to 31; in each aligned block of 1024 rows (0 to 1023, 1024 to 2047, ...) at most 96 rows name the same one
Outputs:
- seq_source: float32 [2, 3, 32, 6, 2, 256], P(None, None, 'zs', None, None, 'grp')
- elements: float32 [3072, 2], P('zs', 'grp')
The draws below stay inside these ranges and needn't reach their ends.
Inputs may be any that keep to these rules, and one draw needn't show every extreme that they name: `corner_offset`: the eight rows are the eight corners of the unit cube, each once. `owner_map`: every owner gets one request or more and at most 96; some owner gets exactly 96.
All inputs are finite; a program needn't handle non-finite values.
Results may differ from the reference program's by a relative error of at most 0.0004.
Values may be sent and summed in bfloat16 or wider, within the bound.
No kernel may reach another device: no remote copies, remote signals or barrier semaphores. Data moves between devices by JAX's collectives and lax.ppermute only.
A program may use at most 192 MiB of HBM per device.

```python
import math
import jax
import jax.numpy as jnp
import numpy as np
from jax import lax

NC = 3
NT = 8
LMAX = 8
PMOM = 3
G = 8
CZ = 6
XBLK = 2
NZB = 4
NZ = 24
NX = 16
NY = 32
NYT = 256
NZX = 384
NBLK = 32
NREQ = 1024
MOST = 96
SLOTS = 3072
N_ZS = 32


def draw_corner_offset(key, part):
    key = jax.random.fold_in(key, 7)
    order = jax.random.permutation(key, 8).astype(jnp.int32)
    return jnp.stack([order // 4, order // 2 % 2, order % 2], axis=1).astype(jnp.int32)


def plant(array, stream_key, smallest, top_value):
    spot = [jax.random.randint(jax.random.fold_in(stream_key, axis), (), 0, length) for axis, length in enumerate(array.shape)]
    main_axis = array.shape.index(max(array.shape))
    neighbour = spot[:main_axis] + [(spot[main_axis] + 1) % array.shape[main_axis]] + spot[main_axis + 1:]
    return array.at[tuple(spot)].set(smallest).at[tuple(neighbour)].set(top_value)


def level_of(own_key, extent, cuts, low, largest):
    level = 1.0
    for axis_at, parts in cuts:
        steps = jax.random.uniform(jax.random.fold_in(jax.random.fold_in(own_key, 6), axis_at), (parts,), jnp.float32, low / len(cuts), largest / len(cuts))
        level = level * jnp.repeat(jnp.exp(steps), extent[axis_at] // parts).reshape((-1,) + (1,) * (len(extent) - 1 - axis_at))
    return level


def deal_out(rng, own, number, rows, count, top, bound, slope):
    ranking = jax.random.permutation(rng, count)
    packed, ordinary = load_shares(count, rows * top, bound, slope, True), load_shares(count, rows * top, bound, slope, False)
    places = jnp.arange(count)

    def named(sizes, rotation):
        used = int((sizes > 0).sum())
        fixed = max(1, used // 4)
        passed = fixed + (places - fixed + rotation * (used - fixed)) % max(1, count - fixed)
        return jnp.zeros((count,), jnp.int32).at[ranking[jnp.where(places < fixed, places, passed)]].set(jnp.asarray(sizes, jnp.int32))

    sizes = jnp.where(number % 4 == 0, named(packed, number // 4), named(ordinary, number - number // 4 - 1))
    mixed = jax.random.permutation(jax.random.fold_in(own, 3), count)
    source_of, sink = mixed[0:count // 2 * 2:2], mixed[1:count // 2 * 2:2]
    slack = jnp.minimum(sizes[source_of] - 1, bound - sizes[sink]) // 2
    slack = jnp.where((source_of == ranking[0]) | (sink == ranking[0]) | (sizes[sink] == 0), 0, jnp.maximum(slack, 0))
    passed = jax.random.randint(jax.random.fold_in(own, 4), (count // 2,), 0, 1 << 20) % (slack + 1)
    sizes = sizes.at[source_of].add(-passed).at[sink].add(passed)
    members = jnp.searchsorted(jnp.cumsum(sizes), jnp.arange(rows * top), side="right").astype(jnp.int32)
    grid = members.reshape(top, rows).T
    grid = grid[jax.random.permutation(jax.random.fold_in(own, 1), rows)]
    rotation = jax.random.randint(jax.random.fold_in(own, 2), (rows, 1), 0, top)
    return jnp.take_along_axis(grid, (jnp.arange(top)[None, :] + rotation) % top, axis=1)


def load_shares(number_of, total, reach, slope, full):
    portions = [(1 << 20) // math.isqrt(standing ** slope) + 1 for standing in range(1, number_of + 1)]
    largest = reach if full else min(reach, max(-(-total // number_of), total * portions[0] // sum(portions)))
    least = 1 if total - largest >= number_of - 1 else 0
    given, spare = [largest] + [least] * (number_of - 1), total - largest - least * (number_of - 1)
    while spare > 0:
        movable = [i for i in range(1, number_of) if given[i] < largest] or [i for i in range(1, number_of) if given[i] < reach]
        pool, remaining = sum([portions[i] for i in movable]), spare
        for i in movable:
            addition = min(reach - given[i], max(1, remaining * portions[i] // pool), spare)
            given[i] = given[i] + addition
            spare = spare - addition
    return np.array(given)


def centred(rng, dims, scale, most, cuts=(), kind=jnp.bfloat16):
    factor_of = level_of(rng, dims, cuts, -0.22, 0.18) if cuts else 1.0
    drawn = jax.random.normal(rng, dims, jnp.float32) * scale * factor_of
    return jnp.minimum(jnp.maximum(drawn, -most), most).astype(kind)


def setup_inputs(seed: int = 0, part: int = 0) -> dict:
    arg_keys = jax.random.split(jax.random.key(seed), 10)
    own_keys = jax.random.split(jax.random.fold_in(arg_keys[9], part), 10)
    quark_up = centred(own_keys[0], (2, NC, NYT, NZX), 0.5, 3.0, ((2, 32),))
    quark_down = centred(own_keys[1], (2, NC, NYT, NZX), 0.5, 3.0, ((2, 32),))
    forward = centred(own_keys[2], (2, NC, NBLK, CZ, XBLK, NYT), 0.5, 3.0, ((2, 32),))
    gauge_links = centred(own_keys[3], (2, NC, NC, NBLK, CZ, XBLK, NYT), 0.408, 2.5, ((3, 32),))
    corner_weight = jnp.clip(jnp.exp(jax.random.uniform(arg_keys[4], (8,), jnp.float32, math.log(0.25), math.log(2.0))), 0.25, 2.0)
    corner_offset = draw_corner_offset(jax.random.fold_in(arg_keys[9], 71), part)
    lengths = plant(jax.random.randint(own_keys[6], (NREQ,), 0, LMAX), jax.random.fold_in(own_keys[6], 1), 0, LMAX - 1).astype(jnp.int32)
    separations = plant(jax.random.randint(own_keys[7], (NREQ,), 0, NT), jax.random.fold_in(own_keys[7], 1), 0, NT - 1).astype(jnp.int32)
    owner_map_keys = jax.random.split(jax.random.fold_in(own_keys[8], 1), NREQ // NREQ)
    owner_map_turns = jax.random.permutation(jax.random.fold_in(own_keys[8], 3), NREQ // NREQ)
    owner_map = jax.vmap(lambda own, number: deal_out(jax.random.fold_in(own_keys[8], 2), own, number, NREQ, N_ZS, 1, MOST, 2))(owner_map_keys, owner_map_turns).reshape((NREQ, 1))
    return {"quark_up": quark_up, "quark_down": quark_down, "forward": forward, "gauge_links": gauge_links, "corner_weight": corner_weight, "corner_offset": corner_offset, "lengths": lengths, "separations": separations, "owner_map": owner_map}


def cross_three(lhs_vec, rhs_vec):
    return jnp.stack([lhs_vec[1] * rhs_vec[2] - lhs_vec[2] * rhs_vec[1], lhs_vec[2] * rhs_vec[0] - lhs_vec[0] * rhs_vec[2], lhs_vec[0] * rhs_vec[1] - lhs_vec[1] * rhs_vec[0]])

def cross_colour(first_vec, second_vec):
    real_part = cross_three(first_vec[0], second_vec[0]) - cross_three(first_vec[1], second_vec[1])
    imag_part = cross_three(first_vec[0], second_vec[1]) + cross_three(first_vec[1], second_vec[0])
    return jnp.stack([real_part, imag_part])

def corner_table(weights, offsets):
    codes = offsets[:, 0] * 4 + offsets[:, 1] * 2 + offsets[:, 2]
    hits = codes[:, None] == jnp.arange(8, dtype=jnp.int32)[None, :]
    return lax.optimization_barrier(jnp.sum(jnp.where(hits, weights.astype(jnp.float32)[:, None], jnp.float32(0.0)), axis=0))

def smear_corners(lower, upper, weights, depth, width):
    summed = jnp.zeros(lower.shape[:3] + (depth, width), jnp.float32)
    for y_step, source_rows in ((0, lower), (1, upper)):
        lattice = source_rows.reshape(source_rows.shape[:3] + (depth, width))
        for z_step in (0, 1):
            z_moved = jnp.roll(lattice, -z_step, axis=3)
            for x_step in (0, 1):
                summed = summed + weights[4 * x_step + 2 * y_step + z_step] * jnp.roll(z_moved, -x_step, axis=4)
    return summed

def apply_links(link_field, vec_field):
    real_part = lax.optimization_barrier(jnp.sum(link_field[0] * vec_field[0][None] - link_field[1] * vec_field[1][None], axis=1))
    imag_part = lax.optimization_barrier(jnp.sum(link_field[0] * vec_field[1][None] + link_field[1] * vec_field[0][None], axis=1))
    return jnp.stack([real_part, imag_part])

def project(seq_field, vec_field, cos_z, sin_z, scale):
    corr_real = lax.optimization_barrier(jnp.sum(seq_field[0] * vec_field[0] + seq_field[1] * vec_field[1], axis=0))
    corr_imag = lax.optimization_barrier(jnp.sum(seq_field[0] * vec_field[1] - seq_field[1] * vec_field[0], axis=0))
    rot_real = corr_real * cos_z - corr_imag * sin_z
    rot_imag = corr_real * sin_z + corr_imag * cos_z
    return jnp.stack([lax.optimization_barrier(jnp.sum(rot_real.reshape(-1, NT), axis=0)), lax.optimization_barrier(jnp.sum(rot_imag.reshape(-1, NT), axis=0))]) * scale

def from_blocks(block_form):
    leading = block_form.shape[:-4]
    count = len(leading)
    shaped = block_form.reshape(leading + (NZB, G, CZ, XBLK, NYT))
    order = tuple(range(count)) + (count, count + 2, count + 1, count + 3, count + 4)
    return jnp.transpose(shaped, order).reshape(leading + (NZ, NX, NYT))

def reference(quark_up, quark_down, forward, gauge_links, corner_weight, corner_offset, lengths, separations, owner_map):
    planes = cross_colour(quark_up.astype(jnp.float32), quark_down.astype(jnp.float32))
    upper = jnp.roll(planes.reshape(2, NC, NY, NT, NZX), -1, axis=2).reshape(2, NC, NYT, NZX)
    weights = corner_table(corner_weight, corner_offset)
    smeared = smear_corners(planes, upper, weights, NZ, NX)
    shaped = smeared.reshape(2, NC, NYT, NZB, CZ, G, XBLK)
    seq_source = jnp.transpose(shaped, (0, 1, 3, 5, 4, 6, 2)).reshape(2, NC, NBLK, CZ, XBLK, NYT)
    seq_global = from_blocks(seq_source)
    field = from_blocks(forward).astype(jnp.float32)
    link_field = from_blocks(gauge_links).astype(jnp.float32)
    zpos = jnp.arange(NZ, dtype=jnp.int32)
    angle = (zpos * PMOM % NZ).astype(jnp.float32) * (2.0 * math.pi / NZ)
    cos_z = jnp.cos(angle)[:, None, None]
    sin_z = jnp.sin(angle)[:, None, None]
    scale = 1.0 / math.sqrt(NX * NY * NZ)
    partial_rows = []
    for length in range(LMAX):
        field = apply_links(link_field, jnp.roll(field, -1, axis=2))
        partial_rows.append(project(seq_global, field, cos_z, sin_z, scale))
    table = jnp.transpose(jnp.stack(partial_rows), (0, 2, 1))
    owner_ids = owner_map[:, 0]
    lanes = jnp.arange(N_ZS, dtype=jnp.int32)
    member = (owner_ids[:, None] == lanes[None, :]).astype(jnp.int32)
    earlier = jnp.cumsum(member, axis=0, dtype=jnp.int32) - member
    rank_in = lax.optimization_barrier(jnp.sum(earlier * member, axis=1, dtype=jnp.int32))
    slot_ids = owner_ids * MOST + rank_in
    values = table[lengths, separations]
    elements = jnp.zeros((SLOTS, 2), jnp.float32).at[slot_ids].set(values)
    return (seq_source, elements)
```

```python
import functools
import math

import jax
import jax.numpy as jnp
from jax import lax
from jax.experimental import pallas as pl
from jax.experimental.pallas import tpu as pltpu
from jax.sharding import PartitionSpec as P

NT = 8
LMAX = 8
PMOM = 3
G = 8
MOST = 96
LANES = 128
XH = 3
CROWS = 16

F32 = jnp.float32
BF16 = jnp.bfloat16
NT_DIMS = (((1,), (1,)), ((), ()))


def passed_along(block, axis, distance):
    devices = range(lax.axis_size(axis))
    route = [((i - distance) % len(devices), i) for i in devices]
    return lax.ppermute(block, axis, route)


def split_two(value):
    high = value.astype(BF16)
    return high, (value - high.astype(F32)).astype(BF16)


def iota(shape, axis):
    return lax.broadcasted_iota(jnp.int32, shape, axis)


def pack_kernel(block_z, block_x, up_ref, down_ref, links_ref, forward_ref, out_ref, edge_ref):
    edge_ref[0:18] = links_ref[:, 0]
    edge_ref[18:24] = forward_ref[:, 0]
    edge_ref[24:30] = forward_ref[:, 1]
    zh = block_z + 1
    slot_lanes = zh * XH
    width_x = block_x * G
    cells = up_ref.shape[3]
    z_blocks = cells // (block_z * width_x)
    up = up_ref[...].astype(F32)
    down = down_ref[...].astype(F32)

    def cross(a, b, c):
        d, e = (c + 1) % 3, (c + 2) % 3
        return up[a, d] * down[b, e] - up[a, e] * down[b, d]

    planes = [cross(0, 0, c) - cross(1, 1, c) for c in range(3)]
    planes += [cross(0, 1, c) + cross(1, 0, c) for c in range(3)]
    lane = iota((1, 2 * LANES), 1)
    half = lane // LANES
    within = lane % LANES
    slot = within // slot_lanes
    cell = within % slot_lanes
    source_row = iota((LANES, 2 * LANES), 0)
    results = []
    for comp in range(6):
        turned = (slot + 12 - comp - 4 * half) % 6
        source = (cell % zh) * width_x + (block_x * (turned + 4 * half) + cell // zh) % width_x
        source = jnp.where((turned < 4) & (slot < 6), source, -1)
        pick = jnp.where(source_row == source, 1.0, 0.0).astype(BF16)
        wide = jnp.concatenate([planes[comp], planes[comp][:, :LANES]], axis=1)
        rows = []
        for zb in range(z_blocks):
            begin = zb * block_z * width_x
            part = wide[:, begin : begin + LANES]
            high = part.astype(BF16).astype(F32)
            rows += [high, part - high]
        left = jnp.concatenate(rows, axis=0).astype(BF16)
        got = jnp.dot(left, pick, preferred_element_type=F32)
        got = got.reshape(z_blocks, 2, NT, 2 * LANES)
        results.append(got[:, 0] + got[:, 1])
    one_slot = iota((NT, LANES), 1) // slot_lanes
    for zb in range(z_blocks):
        for g in range(G):
            at = (g // 4) * LANES
            value = jnp.zeros((NT, LANES), F32)
            for comp in range(6):
                value = jnp.where(
                    one_slot == (comp + g) % 6, results[comp][zb, :, at : at + LANES], value
                )
            out_ref[zb * G + g] = value


def chain_kernel(
    depth_z,
    scale,
    block_z,
    block_x,
    weight_ref,
    offset_ref,
    links_ref,
    links_next_ref,
    forward_ref,
    forward_next_ref,
    edge_ref,
    lengths_ref,
    separations_ref,
    owners_ref,
    chain_ref,
    corner_ref,
    picked_ref,
    link_rows,
    field_rows,
):
    place = lax.axis_index("zs")
    rows_y = links_ref.shape[3]
    zh = block_z + 1
    slot_lanes = zh * XH
    count = block_z * block_x
    link_rows[...] = jnp.zeros_like(link_rows)
    field_rows[...] = jnp.zeros_like(field_rows)

    def fill_links(i, carry):
        for z in range(block_z):
            link_rows[i, block_x * z : block_x * (z + 1)] = links_ref[i, z].astype(F32)
            at = count + block_x * z
            link_rows[i, at : at + block_x] = links_next_ref[i, z].astype(F32)
        link_rows[i, 2 * count : 2 * count + block_x] = edge_ref[i].astype(F32)
        return carry

    def fill_field(i, carry):
        for z in range(block_z):
            field_rows[i, block_x * z : block_x * (z + 1)] = forward_ref[i, z].astype(F32)
            at = count + block_x * z
            field_rows[i, at : at + block_x] = forward_next_ref[i, z].astype(F32)
        field_rows[i, 2 * count : 2 * count + block_x] = edge_ref[18 + i].astype(F32)
        at = 2 * count + block_x
        field_rows[i, at : at + block_x] = edge_ref[24 + i].astype(F32)
        return carry

    lax.fori_loop(0, 18, fill_links, 0)
    lax.fori_loop(0, 6, fill_field, 0)

    row = iota((CROWS, LANES), 0)
    z_of_row = (place // G) * block_z + row // block_x
    angle = (z_of_row * PMOM % depth_z).astype(F32) * (2.0 * math.pi / depth_z)
    inside = row < count
    cos_z = jnp.where(inside, jnp.cos(angle) * scale, 0.0)[:, :1]
    sin_z = jnp.where(inside, jnp.sin(angle) * scale, 0.0)[:, :1]
    total_rows = link_rows.shape[1]

    def step(length, carry):
        for at in range(0, rows_y, LANES):
            lanes = slice(at, at + LANES)
            vec = [
                pltpu.roll(field_rows[c, :, lanes], total_rows - block_x, 0) for c in range(6)
            ]
            for a in range(3):
                real = None
                imag = None
                for b in range(3):
                    link_real = link_rows[a * 3 + b, :, lanes]
                    link_imag = link_rows[9 + a * 3 + b, :, lanes]
                    term_real = link_real * vec[b] - link_imag * vec[3 + b]
                    term_imag = link_real * vec[3 + b] + link_imag * vec[b]
                    real = term_real if real is None else real + term_real
                    imag = term_imag if imag is None else imag + term_imag
                field_rows[a, :, lanes] = real
                field_rows[3 + a, :, lanes] = imag
                top_real, top_imag = real[:CROWS], imag[:CROWS]
                chain_ref[length, a * CROWS : (a + 1) * CROWS, lanes] = (
                    top_real * cos_z - top_imag * sin_z
                )
                chain_ref[length, (3 + a) * CROWS : (4 + a) * CROWS, lanes] = (
                    top_real * sin_z + top_imag * cos_z
                )
        return carry

    lax.fori_loop(0, LMAX, step, 0)

    shape = (6 * CROWS, LANES)
    row = iota(shape, 0)
    lane = iota(shape, 1)
    comp = row // CROWS
    z_step = lane % slot_lanes % zh - row % CROWS // block_x
    x_step = lane % slot_lanes // zh - row % block_x
    here = (lane // slot_lanes == (comp + place % G) % 6) & (row % CROWS < count)
    sums = [jnp.zeros(shape, F32), jnp.zeros(shape, F32)]
    for k in range(8):
        match = here & (x_step == offset_ref[0, k]) & (z_step == offset_ref[2, k])
        for y_step in range(2):
            taken = jnp.where(offset_ref[1, k] == y_step, weight_ref[k], 0.0)
            sums[y_step] = sums[y_step] + jnp.where(match, taken, 0.0)
    for y_step in range(2):
        high, low = split_two(sums[y_step])
        corner_ref[0, y_step * 6 * CROWS : (y_step + 1) * 6 * CROWS] = high
        corner_ref[1, y_step * 6 * CROWS : (y_step + 1) * 6 * CROWS] = low

    mine = owners_ref[...] == place
    codes = (lengths_ref[...] * (2 * NT) + separations_ref[...]).astype(F32)
    member = jnp.where(mine, 1.0, 0.0)
    below = jnp.where(iota((LANES, LANES), 0) < iota((LANES, LANES), 1), 1.0, 0.0)
    earlier = jnp.dot(member.astype(BF16), below.astype(BF16), preferred_element_type=F32)
    running = jnp.zeros((1, 1), F32)
    picked = jnp.zeros((8, LANES), F32)
    slots = iota((LANES, LANES), 0).astype(F32)
    head = iota((8, LANES), 0) == 0
    for i in range(member.shape[0]):
        key = jnp.where(member[i : i + 1] > 0.5, earlier[i : i + 1] + running, -1.0)
        hits = jnp.where(slots == key, 1.0, 0.0).astype(BF16)
        left = jnp.where(head, codes[i : i + 1], 1.0).astype(BF16)
        picked = picked + lax.dot_general(left, hits, NT_DIMS, preferred_element_type=F32)
        running = running + jnp.sum(member[i : i + 1], axis=1, keepdims=True)
    lane_of = picked[0:1].astype(jnp.int32) + iota((8, LANES), 0) % 2 * NT
    picked_ref[...] = jnp.where(picked[1:2] > 0.5, lane_of, -1)


def meet_kernel(block_z, block_x, got_ref, corner_ref, chain_ref, seq_ref, table_ref):
    rows_y = got_ref.shape[0] * NT
    got = got_ref[...].reshape(rows_y, LANES)
    high, low = split_two(got)
    dot = functools.partial(
        lax.dot_general, dimension_numbers=NT_DIMS, preferred_element_type=F32
    )
    both = dot(corner_ref[0], high) + dot(corner_ref[0], low) + dot(corner_ref[1], high)
    size = 6 * CROWS
    seq = both[:size] + pltpu.roll(both[size:], rows_y - NT, 1)
    for comp in range(6):
        for z in range(block_z):
            at = comp * CROWS + z * block_x
            seq_ref[comp, z] = seq[at : at + block_x]
    turned = jnp.concatenate([-seq[3 * CROWS :], seq[: 3 * CROWS]], axis=0)
    sums = []
    for length in range(LMAX):
        chain = chain_ref[length]
        for field in (seq, turned):
            prod = field * chain
            part = prod[:8]
            for at in range(8, size, 8):
                part = part + prod[at : at + 8]
            narrow = part[:, :LANES]
            for at in range(LANES, rows_y, LANES):
                narrow = narrow + part[:, at : at + LANES]
            sums.append(jnp.sum(narrow, axis=0, keepdims=True))
    table = jnp.concatenate(sums, axis=0)
    for shift in (64, 32, 16, 8):
        table = table + pltpu.roll(table, shift, 1)
    mine = iota((2 * LMAX, LANES), 1) // NT == iota((2 * LMAX, LANES), 0)
    flat = jnp.sum(jnp.where(mine, table, 0.0), axis=0, keepdims=True)
    table_ref[...] = jnp.broadcast_to(flat, table_ref.shape)


def final_kernel(tables_ref, picked_ref, out_ref):
    total = jnp.sum(tables_ref[...], axis=0, keepdims=True)
    picked = picked_ref[...]
    value = jnp.take_along_axis(
        jnp.broadcast_to(total, picked.shape), jnp.maximum(picked, 0), axis=1
    )
    value = jnp.where(picked >= 0, value, 0.0)
    out_ref[...] = value[:2, : out_ref.shape[1]]


VMEM = pl.BlockSpec(memory_space=pltpu.VMEM)
SMEM = pl.BlockSpec(memory_space=pltpu.SMEM)


def cost(flops, moved):
    return pl.CostEstimate(flops=flops, bytes_accessed=moved, transcendentals=0)


def shards(
    quark_up,
    quark_down,
    forward,
    gauge_links,
    corner_weight,
    corner_offset,
    lengths,
    separations,
    owner_map,
):
    devices = lax.axis_size("zs")
    block_z, block_x, rows_y = forward.shape[3:]
    cells = quark_up.shape[3]
    depth_z = cells // (block_x * G)
    scale = 1.0 / math.sqrt(cells * (rows_y // NT))
    links = gauge_links.reshape(18, block_z, block_x, rows_y)
    field = forward.reshape(6, block_z, block_x, rows_y)

    links_next = passed_along(links, "zs", -G)
    field_next = passed_along(field, "zs", -G)
    payload, edge = pl.pallas_call(
        functools.partial(pack_kernel, block_z, block_x),
        out_shape=(
            jax.ShapeDtypeStruct((devices, NT, LANES), F32),
            jax.ShapeDtypeStruct((30, block_x, rows_y), BF16),
        ),
        grid=(1,),
        in_specs=[
            pl.BlockSpec(quark_up.shape, lambda i: (0, 0, 0, 0)),
            pl.BlockSpec(quark_down.shape, lambda i: (0, 0, 0, 0)),
            pl.BlockSpec((18, 1, block_x, rows_y), lambda i: (0, 0, 0, 0)),
            pl.BlockSpec((6, 2, block_x, rows_y), lambda i: (0, 0, 0, 0)),
        ],
        out_specs=(
            pl.BlockSpec((devices, NT, LANES), lambda i: (0, 0, 0)),
            pl.BlockSpec((30, block_x, rows_y), lambda i: (0, 0, 0)),
        ),
        cost_estimate=cost(10_000_000, 400_000),
        name="pack",
    )(quark_up, quark_down, links, field)
    edge_next = passed_along(edge, "zs", -2 * G)
    got = lax.all_to_all(payload, "zs", split_axis=0, concat_axis=0, tiled=True)

    requests = (lengths.shape[0] // LANES, LANES)
    chain, corner, picked = pl.pallas_call(
        functools.partial(chain_kernel, depth_z, scale, block_z, block_x),
        out_shape=(
            jax.ShapeDtypeStruct((LMAX, 6 * CROWS, rows_y), F32),
            jax.ShapeDtypeStruct((2, 12 * CROWS, LANES), BF16),
            jax.ShapeDtypeStruct((8, LANES), jnp.int32),
        ),
        in_specs=[SMEM, SMEM] + [VMEM] * 8,
        out_specs=(VMEM, VMEM, VMEM),
        scratch_shapes=[
            pltpu.VMEM((18, 32, rows_y), F32),
            pltpu.VMEM((6, 32, rows_y), F32),
        ],
        cost_estimate=cost(20_000_000, 2_000_000),
        name="chain",
    )(
        corner_weight,
        corner_offset.T,
        links,
        links_next,
        field,
        field_next,
        edge_next,
        lengths.reshape(requests),
        separations.reshape(requests),
        owner_map.reshape(requests),
    )

    seq, table = pl.pallas_call(
        functools.partial(meet_kernel, block_z, block_x),
        out_shape=(
            jax.ShapeDtypeStruct((6, block_z, block_x, rows_y), F32),
            jax.ShapeDtypeStruct((devices, LANES), F32),
        ),
        in_specs=[VMEM] * 3,
        out_specs=(VMEM, VMEM),
        cost_estimate=cost(20_000_000, 1_000_000),
        name="meet",
    )(got, corner, chain)
    tables = lax.all_to_all(
        table.reshape(devices, 1, LANES), "zs", split_axis=0, concat_axis=0, tiled=True
    )
    owned = pl.pallas_call(
        final_kernel,
        out_shape=jax.ShapeDtypeStruct((2, MOST), F32),
        in_specs=[VMEM] * 2,
        out_specs=VMEM,
        name="final",
    )(tables.reshape(devices, LANES), picked)
    return (seq.reshape(2, 3, 1, block_z, block_x, rows_y), owned.T)


def solution(mesh):
    in_specs = (
        P(None, None, "zs", "grp"),
        P(None, None, "zs", "grp"),
        P(None, None, "zs", None, None, "grp"),
        P(None, None, None, "zs", None, None, "grp"),
        P(),
        P(),
        P("grp"),
        P("grp"),
        P("grp", None),
    )
    out_specs = (P(None, None, "zs", None, None, "grp"), P("zs", "grp"))
    return jax.shard_map(shards, mesh=mesh, in_specs=in_specs, out_specs=out_specs, check_vma=False)
```

```python
import functools
import math

import jax
import jax.numpy as jnp
from jax import lax
from jax.experimental import pallas as pl
from jax.experimental.pallas import tpu as pltpu
from jax.sharding import PartitionSpec as P

NT = 8
LMAX = 8
PMOM = 3
G = 8
MOST = 96
LANES = 128
XH = 3
CROWS = 16

F32 = jnp.float32
BF16 = jnp.bfloat16
NT_DIMS = (((1,), (1,)), ((), ()))


def passed_along(block, axis, distance):
    devices = range(lax.axis_size(axis))
    route = [((i - distance) % len(devices), i) for i in devices]
    return lax.ppermute(block, axis, route)


def split_two(value):
    high = value.astype(BF16)
    return high, (value - high.astype(F32)).astype(BF16)


def iota(shape, axis):
    return lax.broadcasted_iota(jnp.int32, shape, axis)


def pack_kernel(block_z, block_x, up_ref, down_ref, links_ref, forward_ref, out_ref, edge_ref):
    edge_ref[0:18] = links_ref[:, 0]
    edge_ref[18:24] = forward_ref[:, 0]
    edge_ref[24:30] = forward_ref[:, 1]
    zh = block_z + 1
    slot_lanes = zh * XH
    width_x = block_x * G
    cells = up_ref.shape[3]
    z_blocks = cells // (block_z * width_x)
    up = up_ref[...].astype(F32)
    down = down_ref[...].astype(F32)

    def cross(a, b, c):
        d, e = (c + 1) % 3, (c + 2) % 3
        return up[a, d] * down[b, e] - up[a, e] * down[b, d]

    planes = [cross(0, 0, c) - cross(1, 1, c) for c in range(3)]
    planes += [cross(0, 1, c) + cross(1, 0, c) for c in range(3)]
    lane = iota((1, 2 * LANES), 1)
    half = lane // LANES
    within = lane % LANES
    slot = within // slot_lanes
    cell = within % slot_lanes
    source_row = iota((LANES, 2 * LANES), 0)
    results = []
    for comp in range(6):
        turned = (slot + 12 - comp - 4 * half) % 6
        source = (cell % zh) * width_x + (block_x * (turned + 4 * half) + cell // zh) % width_x
        source = jnp.where((turned < 4) & (slot < 6), source, -1)
        pick = jnp.where(source_row == source, 1.0, 0.0).astype(BF16)
        wide = jnp.concatenate([planes[comp], planes[comp][:, :LANES]], axis=1)
        rows = []
        for zb in range(z_blocks):
            begin = zb * block_z * width_x
            part = wide[:, begin : begin + LANES]
            high = part.astype(BF16).astype(F32)
            rows += [high, part - high]
        left = jnp.concatenate(rows, axis=0).astype(BF16)
        got = jnp.dot(left, pick, preferred_element_type=F32)
        got = got.reshape(z_blocks, 2, NT, 2 * LANES)
        results.append(got[:, 0] + got[:, 1])
    one_slot = iota((NT, LANES), 1) // slot_lanes
    for zb in range(z_blocks):
        for g in range(G):
            at = (g // 4) * LANES
            value = jnp.zeros((NT, LANES), F32)
            for comp in range(6):
                value = jnp.where(
                    one_slot == (comp + g) % 6, results[comp][zb, :, at : at + LANES], value
                )
            out_ref[zb * G + g] = value


def chain_kernel(
    depth_z,
    scale,
    block_z,
    block_x,
    weight_ref,
    offset_ref,
    links_ref,
    links_next_ref,
    forward_ref,
    forward_next_ref,
    edge_ref,
    lengths_ref,
    separations_ref,
    owners_ref,
    chain_ref,
    corner_ref,
    picked_ref,
    link_rows,
    field_rows,
):
    place = lax.axis_index("zs")
    rows_y = links_ref.shape[3]
    zh = block_z + 1
    slot_lanes = zh * XH
    count = block_z * block_x
    link_rows[...] = jnp.zeros_like(link_rows)
    field_rows[...] = jnp.zeros_like(field_rows)

    def fill_links(i, carry):
        for z in range(block_z):
            link_rows[i, block_x * z : block_x * (z + 1)] = links_ref[i, z].astype(F32)
            at = count + block_x * z
            link_rows[i, at : at + block_x] = links_next_ref[i, z].astype(F32)
        link_rows[i, 2 * count : 2 * count + block_x] = edge_ref[i].astype(F32)
        return carry

    def fill_field(i, carry):
        for z in range(block_z):
            field_rows[i, block_x * z : block_x * (z + 1)] = forward_ref[i, z].astype(F32)
            at = count + block_x * z
            field_rows[i, at : at + block_x] = forward_next_ref[i, z].astype(F32)
        field_rows[i, 2 * count : 2 * count + block_x] = edge_ref[18 + i].astype(F32)
        at = 2 * count + block_x
        field_rows[i, at : at + block_x] = edge_ref[24 + i].astype(F32)
        return carry

    lax.fori_loop(0, 18, fill_links, 0)
    lax.fori_loop(0, 6, fill_field, 0)

    row = iota((CROWS, LANES), 0)
    z_of_row = (place // G) * block_z + row // block_x
    angle = (z_of_row * PMOM % depth_z).astype(F32) * (2.0 * math.pi / depth_z)
    inside = row < count
    cos_z = jnp.where(inside, jnp.cos(angle) * scale, 0.0)[:, :1]
    sin_z = jnp.where(inside, jnp.sin(angle) * scale, 0.0)[:, :1]
    total_rows = link_rows.shape[1]

    def step(length, carry):
        for at in range(0, rows_y, LANES):
            lanes = slice(at, at + LANES)
            vec = [
                pltpu.roll(field_rows[c, :, lanes], total_rows - block_x, 0) for c in range(6)
            ]
            for a in range(3):
                real = None
                imag = None
                for b in range(3):
                    link_real = link_rows[a * 3 + b, :, lanes]
                    link_imag = link_rows[9 + a * 3 + b, :, lanes]
                    term_real = link_real * vec[b] - link_imag * vec[3 + b]
                    term_imag = link_real * vec[3 + b] + link_imag * vec[b]
                    real = term_real if real is None else real + term_real
                    imag = term_imag if imag is None else imag + term_imag
                field_rows[a, :, lanes] = real
                field_rows[3 + a, :, lanes] = imag
                top_real, top_imag = real[:CROWS], imag[:CROWS]
                chain_ref[length, a * CROWS : (a + 1) * CROWS, lanes] = (
                    top_real * cos_z - top_imag * sin_z
                )
                chain_ref[length, (3 + a) * CROWS : (4 + a) * CROWS, lanes] = (
                    top_real * sin_z + top_imag * cos_z
                )
        return carry

    lax.fori_loop(0, LMAX, step, 0)

    shape = (6 * CROWS, LANES)
    row = iota(shape, 0)
    lane = iota(shape, 1)
    comp = row // CROWS
    z_step = lane % slot_lanes % zh - row % CROWS // block_x
    x_step = lane % slot_lanes // zh - row % block_x
    here = (lane // slot_lanes == (comp + place % G) % 6) & (row % CROWS < count)
    sums = [jnp.zeros(shape, F32), jnp.zeros(shape, F32)]
    for k in range(8):
        match = here & (x_step == offset_ref[0, k]) & (z_step == offset_ref[2, k])
        for y_step in range(2):
            taken = jnp.where(offset_ref[1, k] == y_step, weight_ref[k], 0.0)
            sums[y_step] = sums[y_step] + jnp.where(match, taken, 0.0)
    for y_step in range(2):
        high, low = split_two(sums[y_step])
        corner_ref[0, y_step * 6 * CROWS : (y_step + 1) * 6 * CROWS] = high
        corner_ref[1, y_step * 6 * CROWS : (y_step + 1) * 6 * CROWS] = low

    mine = owners_ref[...] == place
    codes = (lengths_ref[...] * (2 * NT) + separations_ref[...]).astype(F32)
    member = jnp.where(mine, 1.0, 0.0)
    below = jnp.where(iota((LANES, LANES), 0) < iota((LANES, LANES), 1), 1.0, 0.0)
    earlier = jnp.dot(member.astype(BF16), below.astype(BF16), preferred_element_type=F32)
    running = jnp.zeros((1, 1), F32)
    picked = jnp.zeros((8, LANES), F32)
    slots = iota((LANES, LANES), 0).astype(F32)
    head = iota((8, LANES), 0) == 0
    for i in range(member.shape[0]):
        key = jnp.where(member[i : i + 1] > 0.5, earlier[i : i + 1] + running, -1.0)
        hits = jnp.where(slots == key, 1.0, 0.0).astype(BF16)
        left = jnp.where(head, codes[i : i + 1], 1.0).astype(BF16)
        picked = picked + lax.dot_general(left, hits, NT_DIMS, preferred_element_type=F32)
        running = running + jnp.sum(member[i : i + 1], axis=1, keepdims=True)
    lane_of = picked[0:1].astype(jnp.int32) + iota((8, LANES), 0) % 2 * NT
    picked_ref[...] = jnp.where(picked[1:2] > 0.5, lane_of, -1)


def meet_kernel(block_z, block_x, got_ref, corner_ref, chain_ref, seq_ref, table_ref):
    rows_y = got_ref.shape[0] * NT
    got = got_ref[...].reshape(rows_y, LANES)
    high, low = split_two(got)
    dot = functools.partial(
        lax.dot_general, dimension_numbers=NT_DIMS, preferred_element_type=F32
    )
    both = dot(corner_ref[0], high) + dot(corner_ref[0], low) + dot(corner_ref[1], high)
    size = 6 * CROWS
    seq = both[:size] + pltpu.roll(both[size:], rows_y - NT, 1)
    for comp in range(6):
        for z in range(block_z):
            at = comp * CROWS + z * block_x
            seq_ref[comp, z] = seq[at : at + block_x]
    turned = jnp.concatenate([-seq[3 * CROWS :], seq[: 3 * CROWS]], axis=0)
    sums = []
    for length in range(LMAX):
        chain = chain_ref[length]
        for field in (seq, turned):
            prod = field * chain
            part = prod[:8]
            for at in range(8, size, 8):
                part = part + prod[at : at + 8]
            narrow = part[:, :LANES]
            for at in range(LANES, rows_y, LANES):
                narrow = narrow + part[:, at : at + LANES]
            sums.append(jnp.sum(narrow, axis=0, keepdims=True))
    table = jnp.concatenate(sums, axis=0)
    for shift in (64, 32, 16, 8):
        table = table + pltpu.roll(table, shift, 1)
    mine = iota((2 * LMAX, LANES), 1) // NT == iota((2 * LMAX, LANES), 0)
    flat = jnp.sum(jnp.where(mine, table, 0.0), axis=0, keepdims=True)
    table_ref[...] = flat


def final_kernel(total_ref, picked_ref, out_ref):
    total = total_ref[...]
    picked = picked_ref[...]
    value = jnp.take_along_axis(
        jnp.broadcast_to(total, picked.shape), jnp.maximum(picked, 0), axis=1
    )
    value = jnp.where(picked >= 0, value, 0.0)
    out_ref[...] = value[:2, : out_ref.shape[1]]


VMEM = pl.BlockSpec(memory_space=pltpu.VMEM)
SMEM = pl.BlockSpec(memory_space=pltpu.SMEM)


def cost(flops, moved):
    return pl.CostEstimate(flops=flops, bytes_accessed=moved, transcendentals=0)


PARAMS = pltpu.CompilerParams(vmem_limit_bytes=16 * 1024 * 1024)
WIDE_PARAMS = pltpu.CompilerParams(vmem_limit_bytes=60 * 1024 * 1024)


def shards(
    quark_up,
    quark_down,
    forward,
    gauge_links,
    corner_weight,
    corner_offset,
    lengths,
    separations,
    owner_map,
):
    devices = lax.axis_size("zs")
    block_z, block_x, rows_y = forward.shape[3:]
    cells = quark_up.shape[3]
    depth_z = cells // (block_x * G)
    scale = 1.0 / math.sqrt(cells * (rows_y // NT))
    links = gauge_links.reshape(18, block_z, block_x, rows_y)
    field = forward.reshape(6, block_z, block_x, rows_y)

    links_next = passed_along(links, "zs", -G)
    field_next = passed_along(field, "zs", -G)
    payload, edge = pl.pallas_call(
        functools.partial(pack_kernel, block_z, block_x),
        out_shape=(
            jax.ShapeDtypeStruct((devices, NT, LANES), F32),
            jax.ShapeDtypeStruct((30, block_x, rows_y), BF16),
        ),
        grid=(1,),
        in_specs=[
            pl.BlockSpec(quark_up.shape, lambda i: (0, 0, 0, 0)),
            pl.BlockSpec(quark_down.shape, lambda i: (0, 0, 0, 0)),
            pl.BlockSpec((18, 1, block_x, rows_y), lambda i: (0, 0, 0, 0)),
            pl.BlockSpec((6, 2, block_x, rows_y), lambda i: (0, 0, 0, 0)),
        ],
        out_specs=(
            pl.BlockSpec((devices, NT, LANES), lambda i: (0, 0, 0)),
            pl.BlockSpec((30, block_x, rows_y), lambda i: (0, 0, 0)),
        ),
        compiler_params=WIDE_PARAMS,
        cost_estimate=cost(2_000_000_000, 400_000),
        name="pack",
    )(quark_up, quark_down, links, field)
    edge_next = passed_along(edge, "zs", -2 * G)
    got = lax.all_to_all(payload, "zs", split_axis=0, concat_axis=0, tiled=True)

    requests = (lengths.shape[0] // LANES, LANES)
    chain, corner, picked = pl.pallas_call(
        functools.partial(chain_kernel, depth_z, scale, block_z, block_x),
        out_shape=(
            jax.ShapeDtypeStruct((LMAX, 6 * CROWS, rows_y), F32),
            jax.ShapeDtypeStruct((2, 12 * CROWS, LANES), BF16),
            jax.ShapeDtypeStruct((8, LANES), jnp.int32),
        ),
        in_specs=[SMEM, SMEM] + [VMEM] * 8,
        out_specs=(VMEM, VMEM, VMEM),
        scratch_shapes=[
            pltpu.VMEM((18, 32, rows_y), F32),
            pltpu.VMEM((6, 32, rows_y), F32),
        ],
        compiler_params=PARAMS,
        cost_estimate=cost(3_000_000_000, 2_000_000),
        name="chain",
    )(
        corner_weight,
        corner_offset.T,
        links,
        links_next,
        field,
        field_next,
        edge_next,
        lengths.reshape(requests),
        separations.reshape(requests),
        owner_map.reshape(requests),
    )

    seq, table = pl.pallas_call(
        functools.partial(meet_kernel, block_z, block_x),
        out_shape=(
            jax.ShapeDtypeStruct((6, block_z, block_x, rows_y), F32),
            jax.ShapeDtypeStruct((1, LANES), F32),
        ),
        in_specs=[VMEM] * 3,
        out_specs=(VMEM, VMEM),
        compiler_params=PARAMS,
        cost_estimate=cost(2_000_000_000, 1_000_000),
        name="meet",
    )(got, corner, chain)
    total = lax.psum(table, "zs")
    owned = pl.pallas_call(
        final_kernel,
        out_shape=jax.ShapeDtypeStruct((2, MOST), F32),
        in_specs=[VMEM] * 2,
        out_specs=VMEM,
        compiler_params=PARAMS,
        name="final",
    )(total, picked)
    return (seq.reshape(2, 3, 1, block_z, block_x, rows_y), owned.T)


def solution(mesh):
    in_specs = (
        P(None, None, "zs", "grp"),
        P(None, None, "zs", "grp"),
        P(None, None, "zs", None, None, "grp"),
        P(None, None, None, "zs", None, None, "grp"),
        P(),
        P(),
        P("grp"),
        P("grp"),
        P("grp", None),
    )
    out_specs = (P(None, None, "zs", None, None, "grp"), P("zs", "grp"))
    return jax.shard_map(shards, mesh=mesh, in_specs=in_specs, out_specs=out_specs, check_vma=False)
```

```python
import functools
import math

import jax
import jax.numpy as jnp
from jax import lax
from jax.experimental import pallas as pl
from jax.experimental.pallas import tpu as pltpu
from jax.sharding import PartitionSpec as P

NT = 8
LMAX = 8
PMOM = 3
G = 8
MOST = 96
LANES = 128
XH = 3
CROWS = 16

F32 = jnp.float32
BF16 = jnp.bfloat16
NT_DIMS = (((1,), (1,)), ((), ()))


def passed_along(block, axis, distance):
    devices = range(lax.axis_size(axis))
    route = [((i - distance) % len(devices), i) for i in devices]
    return lax.ppermute(block, axis, route)


def within_group(block, axis, distance):
    devices = range(lax.axis_size(axis))
    route = [(i, i // G * G + (i % G + distance) % G) for i in devices]
    return lax.ppermute(block, axis, route)


def split_two(value):
    high = value.astype(BF16)
    return high, (value - high.astype(F32)).astype(BF16)


def iota(shape, axis):
    return lax.broadcasted_iota(jnp.int32, shape, axis)


def pack_kernel(block_z, block_x, up_ref, down_ref, links_ref, forward_ref, *refs):
    out_refs, edge_ref, result_rows = refs[:G], refs[G], refs[G + 1]
    edge_ref[0:18] = links_ref[:, 0]
    edge_ref[18:24] = forward_ref[:, 0]
    edge_ref[24:30] = forward_ref[:, 1]
    zh = block_z + 1
    slot_lanes = zh * XH
    width_x = block_x * G
    cells = up_ref.shape[3]
    z_blocks = cells // (block_z * width_x)
    up = up_ref[...].astype(F32)
    down = down_ref[...].astype(F32)

    def cross(a, b, c):
        d, e = (c + 1) % 3, (c + 2) % 3
        return up[a, d] * down[b, e] - up[a, e] * down[b, d]

    planes = [cross(0, 0, c) - cross(1, 1, c) for c in range(3)]
    planes += [cross(0, 1, c) + cross(1, 0, c) for c in range(3)]
    lane = iota((1, 2 * LANES), 1)
    half = lane // LANES
    within = lane % LANES
    slot = within // slot_lanes
    cell = within % slot_lanes
    source_row = iota((LANES, 2 * LANES), 0)
    for comp in range(6):
        turned = (slot + 12 - comp - 4 * half) % 6
        source = (cell % zh) * width_x + (block_x * (turned + 4 * half) + cell // zh) % width_x
        source = jnp.where((turned < 4) & (slot < 6), source, -1)
        pick = jnp.where(source_row == source, 1.0, 0.0).astype(BF16)
        wide = jnp.concatenate([planes[comp], planes[comp][:, :LANES]], axis=1)
        rows = []
        for zb in range(z_blocks):
            begin = zb * block_z * width_x
            part = wide[:, begin : begin + LANES]
            high = part.astype(BF16).astype(F32)
            rows += [high, part - high]
        left = jnp.concatenate(rows, axis=0).astype(BF16)
        got = jnp.dot(left, pick, preferred_element_type=F32)
        got = got.reshape(z_blocks, 2, NT, 2 * LANES)
        got = got[:, 0] + got[:, 1]
        result_rows[0, comp] = got[..., :LANES]
        result_rows[1, comp] = got[..., LANES:]
    one_slot = iota((NT, LANES), 1) // slot_lanes
    place = lax.axis_index("zs") % G
    for step in range(G):
        g = (place + step) % G
        value = jnp.zeros((z_blocks, NT, LANES), F32)
        for comp in range(6):
            mask = (one_slot == (comp + g) % 6)[None]
            value = jnp.where(mask, result_rows[g // 4, comp], value)
        out_refs[step][...] = value


def regroup_kernel(*refs):
    z_blocks = refs[0].shape[0]
    place = lax.axis_index("zs")
    for j in range(z_blocks):
        for step in range(G):
            refs[G + j][(place + G - step) % G] = refs[step][(place // G + j) % z_blocks]


def chain_kernel(
    depth_z,
    scale,
    block_z,
    block_x,
    weight_ref,
    offset_ref,
    links_ref,
    links_next_ref,
    forward_ref,
    forward_next_ref,
    edge_ref,
    lengths_ref,
    separations_ref,
    owners_ref,
    chain_ref,
    corner_ref,
    picked_ref,
    link_rows,
    field_rows,
):
    place = lax.axis_index("zs")
    rows_y = links_ref.shape[3]
    zh = block_z + 1
    slot_lanes = zh * XH
    count = block_z * block_x
    link_rows[...] = jnp.zeros_like(link_rows)
    field_rows[...] = jnp.zeros_like(field_rows)

    def fill_links(i, carry):
        for z in range(block_z):
            link_rows[i, block_x * z : block_x * (z + 1)] = links_ref[i, z].astype(F32)
            at = count + block_x * z
            link_rows[i, at : at + block_x] = links_next_ref[i, z].astype(F32)
        link_rows[i, 2 * count : 2 * count + block_x] = edge_ref[i].astype(F32)
        return carry

    def fill_field(i, carry):
        for z in range(block_z):
            field_rows[i, block_x * z : block_x * (z + 1)] = forward_ref[i, z].astype(F32)
            at = count + block_x * z
            field_rows[i, at : at + block_x] = forward_next_ref[i, z].astype(F32)
        field_rows[i, 2 * count : 2 * count + block_x] = edge_ref[18 + i].astype(F32)
        at = 2 * count + block_x
        field_rows[i, at : at + block_x] = edge_ref[24 + i].astype(F32)
        return carry

    lax.fori_loop(0, 18, fill_links, 0)
    lax.fori_loop(0, 6, fill_field, 0)

    row = iota((CROWS, LANES), 0)
    z_of_row = (place // G) * block_z + row // block_x
    angle = (z_of_row * PMOM % depth_z).astype(F32) * (2.0 * math.pi / depth_z)
    inside = row < count
    cos_z = jnp.where(inside, jnp.cos(angle) * scale, 0.0)[:, :1]
    sin_z = jnp.where(inside, jnp.sin(angle) * scale, 0.0)[:, :1]
    total_rows = link_rows.shape[1]

    def step(length, carry):
        for at in range(0, rows_y, LANES):
            lanes = slice(at, at + LANES)
            vec = [
                pltpu.roll(field_rows[c, :, lanes], total_rows - block_x, 0) for c in range(6)
            ]
            for a in range(3):
                real = None
                imag = None
                for b in range(3):
                    link_real = link_rows[a * 3 + b, :, lanes]
                    link_imag = link_rows[9 + a * 3 + b, :, lanes]
                    term_real = link_real * vec[b] - link_imag * vec[3 + b]
                    term_imag = link_real * vec[3 + b] + link_imag * vec[b]
                    real = term_real if real is None else real + term_real
                    imag = term_imag if imag is None else imag + term_imag
                field_rows[a, :, lanes] = real
                field_rows[3 + a, :, lanes] = imag
                top_real, top_imag = real[:CROWS], imag[:CROWS]
                chain_ref[length, a * CROWS : (a + 1) * CROWS, lanes] = (
                    top_real * cos_z - top_imag * sin_z
                )
                chain_ref[length, (3 + a) * CROWS : (4 + a) * CROWS, lanes] = (
                    top_real * sin_z + top_imag * cos_z
                )
        return carry

    lax.fori_loop(0, LMAX, step, 0)

    shape = (6 * CROWS, LANES)
    row = iota(shape, 0)
    lane = iota(shape, 1)
    comp = row // CROWS
    z_step = lane % slot_lanes % zh - row % CROWS // block_x
    x_step = lane % slot_lanes // zh - row % block_x
    here = (lane // slot_lanes == (comp + place % G) % 6) & (row % CROWS < count)
    sums = [jnp.zeros(shape, F32), jnp.zeros(shape, F32)]
    for k in range(8):
        match = here & (x_step == offset_ref[0, k]) & (z_step == offset_ref[2, k])
        for y_step in range(2):
            taken = jnp.where(offset_ref[1, k] == y_step, weight_ref[k], 0.0)
            sums[y_step] = sums[y_step] + jnp.where(match, taken, 0.0)
    for y_step in range(2):
        high, low = split_two(sums[y_step])
        corner_ref[0, y_step * 6 * CROWS : (y_step + 1) * 6 * CROWS] = high
        corner_ref[1, y_step * 6 * CROWS : (y_step + 1) * 6 * CROWS] = low

    mine = owners_ref[...] == place
    codes = (lengths_ref[...] * (2 * NT) + separations_ref[...]).astype(F32)
    member = jnp.where(mine, 1.0, 0.0)
    below = jnp.where(iota((LANES, LANES), 0) < iota((LANES, LANES), 1), 1.0, 0.0)
    earlier = jnp.dot(member.astype(BF16), below.astype(BF16), preferred_element_type=F32)
    running = jnp.zeros((1, 1), F32)
    picked = jnp.zeros((8, LANES), F32)
    slots = iota((LANES, LANES), 0).astype(F32)
    head = iota((8, LANES), 0) == 0
    for i in range(member.shape[0]):
        key = jnp.where(member[i : i + 1] > 0.5, earlier[i : i + 1] + running, -1.0)
        hits = jnp.where(slots == key, 1.0, 0.0).astype(BF16)
        left = jnp.where(head, codes[i : i + 1], 1.0).astype(BF16)
        picked = picked + lax.dot_general(left, hits, NT_DIMS, preferred_element_type=F32)
        running = running + jnp.sum(member[i : i + 1], axis=1, keepdims=True)
    lane_of = picked[0:1].astype(jnp.int32) + iota((8, LANES), 0) % 2 * NT
    picked_ref[...] = jnp.where(picked[1:2] > 0.5, lane_of, -1)


def meet_kernel(block_z, block_x, z_blocks, *refs):
    corner_ref, chain_ref, seq_ref, table_ref, got_rows = refs[z_blocks:]
    group = lax.axis_index("zs") // G
    for j in range(z_blocks):
        got_rows[(group + z_blocks - j) % z_blocks] = refs[j][...]
    rows_y = z_blocks * G * NT
    got = got_rows[...].reshape(rows_y, LANES)
    high, low = split_two(got)
    dot = functools.partial(
        lax.dot_general, dimension_numbers=NT_DIMS, preferred_element_type=F32
    )
    both = dot(corner_ref[0], high) + dot(corner_ref[0], low) + dot(corner_ref[1], high)
    size = 6 * CROWS
    seq = both[:size] + pltpu.roll(both[size:], rows_y - NT, 1)
    for comp in range(6):
        for z in range(block_z):
            at = comp * CROWS + z * block_x
            seq_ref[comp, z] = seq[at : at + block_x]
    turned = jnp.concatenate([-seq[3 * CROWS :], seq[: 3 * CROWS]], axis=0)
    sums = []
    for length in range(LMAX):
        chain = chain_ref[length]
        for field in (seq, turned):
            prod = field * chain
            part = prod[:8]
            for at in range(8, size, 8):
                part = part + prod[at : at + 8]
            narrow = part[:, :LANES]
            for at in range(LANES, rows_y, LANES):
                narrow = narrow + part[:, at : at + LANES]
            sums.append(jnp.sum(narrow, axis=0, keepdims=True))
    table = jnp.concatenate(sums, axis=0)
    for shift in (64, 32, 16, 8):
        table = table + pltpu.roll(table, shift, 1)
    mine = iota((2 * LMAX, LANES), 1) // NT == iota((2 * LMAX, LANES), 0)
    flat = jnp.sum(jnp.where(mine, table, 0.0), axis=0, keepdims=True)
    table_ref[...] = flat


def sum_kernel(*refs):
    total = refs[0][...]
    for ref in refs[1:-1]:
        total = total + ref[...]
    refs[-1][...] = total


def final_kernel(*refs):
    picked_ref, out_ref = refs[-2:]
    total = refs[0][...]
    for ref in refs[1:-2]:
        total = total + ref[...]
    picked = picked_ref[...]
    value = jnp.take_along_axis(
        jnp.broadcast_to(total, picked.shape), jnp.maximum(picked, 0), axis=1
    )
    value = jnp.where(picked >= 0, value, 0.0)
    out_ref[...] = value[:2, : out_ref.shape[1]]


VMEM = pl.BlockSpec(memory_space=pltpu.VMEM)
SMEM = pl.BlockSpec(memory_space=pltpu.SMEM)


def cost(flops, moved):
    return pl.CostEstimate(flops=flops, bytes_accessed=moved, transcendentals=0)


PARAMS = pltpu.CompilerParams(vmem_limit_bytes=16 * 1024 * 1024)
WIDE_PARAMS = pltpu.CompilerParams(vmem_limit_bytes=60 * 1024 * 1024)


def shards(
    quark_up,
    quark_down,
    forward,
    gauge_links,
    corner_weight,
    corner_offset,
    lengths,
    separations,
    owner_map,
):
    devices = lax.axis_size("zs")
    block_z, block_x, rows_y = forward.shape[3:]
    cells = quark_up.shape[3]
    depth_z = cells // (block_x * G)
    scale = 1.0 / math.sqrt(cells * (rows_y // NT))
    links = gauge_links.reshape(18, block_z, block_x, rows_y)
    field = forward.reshape(6, block_z, block_x, rows_y)

    links_next = passed_along(links, "zs", -G)
    field_next = passed_along(field, "zs", -G)
    z_blocks = devices // G
    part = (z_blocks, NT, LANES)
    *payload, edge = pl.pallas_call(
        functools.partial(pack_kernel, block_z, block_x),
        out_shape=(jax.ShapeDtypeStruct(part, F32),) * G
        + (jax.ShapeDtypeStruct((30, block_x, rows_y), BF16),),
        grid=(1,),
        in_specs=[
            pl.BlockSpec(quark_up.shape, lambda i: (0, 0, 0, 0)),
            pl.BlockSpec(quark_down.shape, lambda i: (0, 0, 0, 0)),
            pl.BlockSpec((18, 1, block_x, rows_y), lambda i: (0, 0, 0, 0)),
            pl.BlockSpec((6, 2, block_x, rows_y), lambda i: (0, 0, 0, 0)),
        ],
        out_specs=(pl.BlockSpec(part, lambda i: (0, 0, 0)),) * G
        + (pl.BlockSpec((30, block_x, rows_y), lambda i: (0, 0, 0)),),
        scratch_shapes=[pltpu.VMEM((2, 6) + part, F32)],
        compiler_params=WIDE_PARAMS,
        cost_estimate=cost(2_000_000_000, 400_000),
        name="pack",
    )(quark_up, quark_down, links, field)
    edge_next = passed_along(edge, "zs", -2 * G)
    came = [payload[0]] + [within_group(payload[k], "zs", k) for k in range(1, G)]
    parts = pl.pallas_call(
        regroup_kernel,
        out_shape=(jax.ShapeDtypeStruct((G, NT, LANES), F32),) * z_blocks,
        in_specs=[VMEM] * G,
        out_specs=(VMEM,) * z_blocks,
        compiler_params=PARAMS,
        cost_estimate=cost(500_000_000, 300_000),
        name="regroup",
    )(*came)
    got = [parts[0]] + [passed_along(parts[j], "zs", j * G) for j in range(1, z_blocks)]

    requests = (lengths.shape[0] // LANES, LANES)
    chain, corner, picked = pl.pallas_call(
        functools.partial(chain_kernel, depth_z, scale, block_z, block_x),
        out_shape=(
            jax.ShapeDtypeStruct((LMAX, 6 * CROWS, rows_y), F32),
            jax.ShapeDtypeStruct((2, 12 * CROWS, LANES), BF16),
            jax.ShapeDtypeStruct((8, LANES), jnp.int32),
        ),
        in_specs=[SMEM, SMEM] + [VMEM] * 8,
        out_specs=(VMEM, VMEM, VMEM),
        scratch_shapes=[
            pltpu.VMEM((18, 32, rows_y), F32),
            pltpu.VMEM((6, 32, rows_y), F32),
        ],
        compiler_params=PARAMS,
        cost_estimate=cost(3_000_000_000, 2_000_000),
        name="chain",
    )(
        corner_weight,
        corner_offset.T,
        links,
        links_next,
        field,
        field_next,
        edge_next,
        lengths.reshape(requests),
        separations.reshape(requests),
        owner_map.reshape(requests),
    )

    seq, table = pl.pallas_call(
        functools.partial(meet_kernel, block_z, block_x, z_blocks),
        out_shape=(
            jax.ShapeDtypeStruct((6, block_z, block_x, rows_y), F32),
            jax.ShapeDtypeStruct((1, LANES), F32),
        ),
        in_specs=[VMEM] * (z_blocks + 2),
        out_specs=(VMEM, VMEM),
        scratch_shapes=[pltpu.VMEM((z_blocks, G, NT, LANES), F32)],
        compiler_params=PARAMS,
        cost_estimate=cost(2_000_000_000, 1_000_000),
        name="meet",
    )(*got, corner, chain)
    tables = [table] + [within_group(table, "zs", k) for k in range(1, G)]
    table = pl.pallas_call(
        sum_kernel,
        out_shape=jax.ShapeDtypeStruct((1, LANES), F32),
        in_specs=[VMEM] * G,
        out_specs=VMEM,
        compiler_params=PARAMS,
        name="sum",
    )(*tables)
    tables = [table] + [passed_along(table, "zs", j * G) for j in range(1, z_blocks)]
    owned = pl.pallas_call(
        final_kernel,
        out_shape=jax.ShapeDtypeStruct((2, MOST), F32),
        in_specs=[VMEM] * (z_blocks + 1),
        out_specs=VMEM,
        compiler_params=PARAMS,
        name="final",
    )(*tables, picked)
    return (seq.reshape(2, 3, 1, block_z, block_x, rows_y), owned.T)


def solution(mesh):
    in_specs = (
        P(None, None, "zs", "grp"),
        P(None, None, "zs", "grp"),
        P(None, None, "zs", None, None, "grp"),
        P(None, None, None, "zs", None, None, "grp"),
        P(),
        P(),
        P("grp"),
        P("grp"),
        P("grp", None),
    )
    out_specs = (P(None, None, "zs", None, None, "grp"), P("zs", "grp"))
    return jax.shard_map(shards, mesh=mesh, in_specs=in_specs, out_specs=out_specs, check_vma=False)
```

```python
import functools
import math

import jax
import jax.numpy as jnp
from jax import lax
from jax.experimental import pallas as pl
from jax.experimental.pallas import tpu as pltpu
from jax.sharding import PartitionSpec as P

NT = 8
LMAX = 8
PMOM = 3
G = 8
MOST = 96
LANES = 128
XH = 3
CROWS = 16

F32 = jnp.float32
BF16 = jnp.bfloat16
NT_DIMS = (((1,), (1,)), ((), ()))


def passed_along(block, axis, distance):
    devices = range(lax.axis_size(axis))
    route = [((i - distance) % len(devices), i) for i in devices]
    return lax.ppermute(block, axis, route)


def swapped_within(block, axis):
    count = lax.axis_size(axis)
    groups = [[first + k for k in range(G)] for first in range(0, count, G)]
    return lax.all_to_all(block, axis, 0, 0, tiled=True, axis_index_groups=groups)


def swapped_between(block, axis):
    count = lax.axis_size(axis)
    groups = [list(range(first, count, G)) for first in range(G)]
    return lax.all_to_all(block, axis, 0, 0, tiled=True, axis_index_groups=groups)


def split_two(value):
    high = value.astype(BF16)
    return high, (value - high.astype(F32)).astype(BF16)


def iota(shape, axis):
    return lax.broadcasted_iota(jnp.int32, shape, axis)


def pack_kernel(block_z, block_x, up_ref, down_ref, links_ref, forward_ref, out_ref, edge_ref):
    edge_ref[0:18] = links_ref[:, 0]
    edge_ref[18:24] = forward_ref[:, 0]
    edge_ref[24:30] = forward_ref[:, 1]
    zh = block_z + 1
    slot_lanes = zh * XH
    width_x = block_x * G
    cells = up_ref.shape[3]
    z_blocks = cells // (block_z * width_x)
    up = up_ref[...].astype(F32)
    down = down_ref[...].astype(F32)

    def cross(a, b, c):
        d, e = (c + 1) % 3, (c + 2) % 3
        return up[a, d] * down[b, e] - up[a, e] * down[b, d]

    planes = [cross(0, 0, c) - cross(1, 1, c) for c in range(3)]
    planes += [cross(0, 1, c) + cross(1, 0, c) for c in range(3)]
    lane = iota((1, 2 * LANES), 1)
    half = lane // LANES
    within = lane % LANES
    slot = within // slot_lanes
    cell = within % slot_lanes
    source_row = iota((LANES, 2 * LANES), 0)
    results = []
    for comp in range(6):
        turned = (slot + 12 - comp - 4 * half) % 6
        source = (cell % zh) * width_x + (block_x * (turned + 4 * half) + cell // zh) % width_x
        source = jnp.where((turned < 4) & (slot < 6), source, -1)
        pick = jnp.where(source_row == source, 1.0, 0.0).astype(BF16)
        wide = jnp.concatenate([planes[comp], planes[comp][:, :LANES]], axis=1)
        rows = []
        for zb in range(z_blocks):
            begin = zb * block_z * width_x
            part = wide[:, begin : begin + LANES]
            high = part.astype(BF16).astype(F32)
            rows += [high, part - high]
        left = jnp.concatenate(rows, axis=0).astype(BF16)
        got = jnp.dot(left, pick, preferred_element_type=F32)
        got = got.reshape(z_blocks, 2, NT, 2 * LANES)
        results.append(got[:, 0] + got[:, 1])
    one_slot = iota((NT, LANES), 1) // slot_lanes
    for zb in range(z_blocks):
        for g in range(G):
            at = (g // 4) * LANES
            value = jnp.zeros((NT, LANES), F32)
            for comp in range(6):
                value = jnp.where(
                    one_slot == (comp + g) % 6, results[comp][zb, :, at : at + LANES], value
                )
            out_ref[g, zb] = value


def regroup_kernel(came_ref, out_ref):
    for g in range(came_ref.shape[0]):
        for zb in range(came_ref.shape[1]):
            out_ref[zb, g] = came_ref[g, zb]


def chain_kernel(
    depth_z,
    scale,
    block_z,
    block_x,
    weight_ref,
    offset_ref,
    links_ref,
    links_next_ref,
    forward_ref,
    forward_next_ref,
    edge_ref,
    lengths_ref,
    separations_ref,
    owners_ref,
    chain_ref,
    corner_ref,
    picked_ref,
    link_rows,
    field_rows,
):
    place = lax.axis_index("zs")
    rows_y = links_ref.shape[3]
    zh = block_z + 1
    slot_lanes = zh * XH
    count = block_z * block_x
    link_rows[...] = jnp.zeros_like(link_rows)
    field_rows[...] = jnp.zeros_like(field_rows)

    def fill_links(i, carry):
        for z in range(block_z):
            link_rows[i, block_x * z : block_x * (z + 1)] = links_ref[i, z].astype(F32)
            at = count + block_x * z
            link_rows[i, at : at + block_x] = links_next_ref[i, z].astype(F32)
        link_rows[i, 2 * count : 2 * count + block_x] = edge_ref[i].astype(F32)
        return carry

    def fill_field(i, carry):
        for z in range(block_z):
            field_rows[i, block_x * z : block_x * (z + 1)] = forward_ref[i, z].astype(F32)
            at = count + block_x * z
            field_rows[i, at : at + block_x] = forward_next_ref[i, z].astype(F32)
        field_rows[i, 2 * count : 2 * count + block_x] = edge_ref[18 + i].astype(F32)
        at = 2 * count + block_x
        field_rows[i, at : at + block_x] = edge_ref[24 + i].astype(F32)
        return carry

    lax.fori_loop(0, 18, fill_links, 0)
    lax.fori_loop(0, 6, fill_field, 0)

    row = iota((CROWS, LANES), 0)
    z_of_row = (place // G) * block_z + row // block_x
    angle = (z_of_row * PMOM % depth_z).astype(F32) * (2.0 * math.pi / depth_z)
    inside = row < count
    cos_z = jnp.where(inside, jnp.cos(angle) * scale, 0.0)[:, :1]
    sin_z = jnp.where(inside, jnp.sin(angle) * scale, 0.0)[:, :1]
    total_rows = link_rows.shape[1]

    def step(length, carry):
        for at in range(0, rows_y, LANES):
            lanes = slice(at, at + LANES)
            vec = [
                pltpu.roll(field_rows[c, :, lanes], total_rows - block_x, 0) for c in range(6)
            ]
            for a in range(3):
                real = None
                imag = None
                for b in range(3):
                    link_real = link_rows[a * 3 + b, :, lanes]
                    link_imag = link_rows[9 + a * 3 + b, :, lanes]
                    term_real = link_real * vec[b] - link_imag * vec[3 + b]
                    term_imag = link_real * vec[3 + b] + link_imag * vec[b]
                    real = term_real if real is None else real + term_real
                    imag = term_imag if imag is None else imag + term_imag
                field_rows[a, :, lanes] = real
                field_rows[3 + a, :, lanes] = imag
                top_real, top_imag = real[:CROWS], imag[:CROWS]
                chain_ref[length, a * CROWS : (a + 1) * CROWS, lanes] = (
                    top_real * cos_z - top_imag * sin_z
                )
                chain_ref[length, (3 + a) * CROWS : (4 + a) * CROWS, lanes] = (
                    top_real * sin_z + top_imag * cos_z
                )
        return carry

    lax.fori_loop(0, LMAX, step, 0)

    shape = (6 * CROWS, LANES)
    row = iota(shape, 0)
    lane = iota(shape, 1)
    comp = row // CROWS
    z_step = lane % slot_lanes % zh - row % CROWS // block_x
    x_step = lane % slot_lanes // zh - row % block_x
    here = (lane // slot_lanes == (comp + place % G) % 6) & (row % CROWS < count)
    sums = [jnp.zeros(shape, F32), jnp.zeros(shape, F32)]
    for k in range(8):
        match = here & (x_step == offset_ref[0, k]) & (z_step == offset_ref[2, k])
        for y_step in range(2):
            taken = jnp.where(offset_ref[1, k] == y_step, weight_ref[k], 0.0)
            sums[y_step] = sums[y_step] + jnp.where(match, taken, 0.0)
    for y_step in range(2):
        high, low = split_two(sums[y_step])
        corner_ref[0, y_step * 6 * CROWS : (y_step + 1) * 6 * CROWS] = high
        corner_ref[1, y_step * 6 * CROWS : (y_step + 1) * 6 * CROWS] = low

    mine = owners_ref[...] == place
    codes = (lengths_ref[...] * (2 * NT) + separations_ref[...]).astype(F32)
    member = jnp.where(mine, 1.0, 0.0)
    below = jnp.where(iota((LANES, LANES), 0) < iota((LANES, LANES), 1), 1.0, 0.0)
    earlier = jnp.dot(member.astype(BF16), below.astype(BF16), preferred_element_type=F32)
    running = jnp.zeros((1, 1), F32)
    picked = jnp.zeros((8, LANES), F32)
    slots = iota((LANES, LANES), 0).astype(F32)
    head = iota((8, LANES), 0) == 0
    for i in range(member.shape[0]):
        key = jnp.where(member[i : i + 1] > 0.5, earlier[i : i + 1] + running, -1.0)
        hits = jnp.where(slots == key, 1.0, 0.0).astype(BF16)
        left = jnp.where(head, codes[i : i + 1], 1.0).astype(BF16)
        picked = picked + lax.dot_general(left, hits, NT_DIMS, preferred_element_type=F32)
        running = running + jnp.sum(member[i : i + 1], axis=1, keepdims=True)
    lane_of = picked[0:1].astype(jnp.int32) + iota((8, LANES), 0) % 2 * NT
    picked_ref[...] = jnp.where(picked[1:2] > 0.5, lane_of, -1)


def meet_kernel(block_z, block_x, got_ref, corner_ref, chain_ref, seq_ref, table_ref):
    rows_y = got_ref.shape[0] * NT
    got = got_ref[...].reshape(rows_y, LANES)
    high, low = split_two(got)
    dot = functools.partial(
        lax.dot_general, dimension_numbers=NT_DIMS, preferred_element_type=F32
    )
    both = dot(corner_ref[0], high) + dot(corner_ref[0], low) + dot(corner_ref[1], high)
    size = 6 * CROWS
    seq = both[:size] + pltpu.roll(both[size:], rows_y - NT, 1)
    for comp in range(6):
        for z in range(block_z):
            at = comp * CROWS + z * block_x
            seq_ref[comp, z] = seq[at : at + block_x]
    turned = jnp.concatenate([-seq[3 * CROWS :], seq[: 3 * CROWS]], axis=0)
    sums = []
    for length in range(LMAX):
        chain = chain_ref[length]
        for field in (seq, turned):
            prod = field * chain
            part = prod[:8]
            for at in range(8, size, 8):
                part = part + prod[at : at + 8]
            narrow = part[:, :LANES]
            for at in range(LANES, rows_y, LANES):
                narrow = narrow + part[:, at : at + LANES]
            sums.append(jnp.sum(narrow, axis=0, keepdims=True))
    table = jnp.concatenate(sums, axis=0)
    for shift in (64, 32, 16, 8):
        table = table + pltpu.roll(table, shift, 1)
    mine = iota((2 * LMAX, LANES), 1) // NT == iota((2 * LMAX, LANES), 0)
    flat = jnp.sum(jnp.where(mine, table, 0.0), axis=0, keepdims=True)
    table_ref[...] = jnp.broadcast_to(flat, table_ref.shape)


def sum_kernel(tables_ref, out_ref):
    total = jnp.sum(tables_ref[...], axis=0, keepdims=True)
    out_ref[...] = jnp.broadcast_to(total, out_ref.shape)


def final_kernel(tables_ref, picked_ref, out_ref):
    total = jnp.sum(tables_ref[...], axis=0, keepdims=True)
    picked = picked_ref[...]
    value = jnp.take_along_axis(
        jnp.broadcast_to(total, picked.shape), jnp.maximum(picked, 0), axis=1
    )
    value = jnp.where(picked >= 0, value, 0.0)
    out_ref[...] = value[:2, : out_ref.shape[1]]


VMEM = pl.BlockSpec(memory_space=pltpu.VMEM)
SMEM = pl.BlockSpec(memory_space=pltpu.SMEM)


def cost(flops, moved):
    return pl.CostEstimate(flops=flops, bytes_accessed=moved, transcendentals=0)


PARAMS = pltpu.CompilerParams(vmem_limit_bytes=16 * 1024 * 1024)
WIDE_PARAMS = pltpu.CompilerParams(vmem_limit_bytes=60 * 1024 * 1024)


def shards(
    quark_up,
    quark_down,
    forward,
    gauge_links,
    corner_weight,
    corner_offset,
    lengths,
    separations,
    owner_map,
):
    devices = lax.axis_size("zs")
    block_z, block_x, rows_y = forward.shape[3:]
    cells = quark_up.shape[3]
    depth_z = cells // (block_x * G)
    scale = 1.0 / math.sqrt(cells * (rows_y // NT))
    links = gauge_links.reshape(18, block_z, block_x, rows_y)
    field = forward.reshape(6, block_z, block_x, rows_y)

    links_next = passed_along(links, "zs", -G)
    field_next = passed_along(field, "zs", -G)
    z_blocks = devices // G
    payload, edge = pl.pallas_call(
        functools.partial(pack_kernel, block_z, block_x),
        out_shape=(
            jax.ShapeDtypeStruct((G, z_blocks, NT, LANES), F32),
            jax.ShapeDtypeStruct((30, block_x, rows_y), BF16),
        ),
        grid=(1,),
        in_specs=[
            pl.BlockSpec(quark_up.shape, lambda i: (0, 0, 0, 0)),
            pl.BlockSpec(quark_down.shape, lambda i: (0, 0, 0, 0)),
            pl.BlockSpec((18, 1, block_x, rows_y), lambda i: (0, 0, 0, 0)),
            pl.BlockSpec((6, 2, block_x, rows_y), lambda i: (0, 0, 0, 0)),
        ],
        out_specs=(
            pl.BlockSpec((G, z_blocks, NT, LANES), lambda i: (0, 0, 0, 0)),
            pl.BlockSpec((30, block_x, rows_y), lambda i: (0, 0, 0)),
        ),
        compiler_params=WIDE_PARAMS,
        cost_estimate=cost(2_000_000_000, 400_000),
        name="pack",
    )(quark_up, quark_down, links, field)
    edge_next = passed_along(edge, "zs", -2 * G)
    parts = pl.pallas_call(
        regroup_kernel,
        out_shape=jax.ShapeDtypeStruct((z_blocks, G, NT, LANES), F32),
        in_specs=[VMEM],
        out_specs=VMEM,
        compiler_params=PARAMS,
        cost_estimate=cost(500_000_000, 300_000),
        name="regroup",
    )(swapped_within(payload, "zs"))
    got = swapped_between(parts, "zs").reshape(devices, NT, LANES)

    requests = (lengths.shape[0] // LANES, LANES)
    chain, corner, picked = pl.pallas_call(
        functools.partial(chain_kernel, depth_z, scale, block_z, block_x),
        out_shape=(
            jax.ShapeDtypeStruct((LMAX, 6 * CROWS, rows_y), F32),
            jax.ShapeDtypeStruct((2, 12 * CROWS, LANES), BF16),
            jax.ShapeDtypeStruct((8, LANES), jnp.int32),
        ),
        in_specs=[SMEM, SMEM] + [VMEM] * 8,
        out_specs=(VMEM, VMEM, VMEM),
        scratch_shapes=[
            pltpu.VMEM((18, 32, rows_y), F32),
            pltpu.VMEM((6, 32, rows_y), F32),
        ],
        compiler_params=PARAMS,
        cost_estimate=cost(3_000_000_000, 2_000_000),
        name="chain",
    )(
        corner_weight,
        corner_offset.T,
        links,
        links_next,
        field,
        field_next,
        edge_next,
        lengths.reshape(requests),
        separations.reshape(requests),
        owner_map.reshape(requests),
    )

    seq, table = pl.pallas_call(
        functools.partial(meet_kernel, block_z, block_x),
        out_shape=(
            jax.ShapeDtypeStruct((6, block_z, block_x, rows_y), F32),
            jax.ShapeDtypeStruct((G, LANES), F32),
        ),
        in_specs=[VMEM] * 3,
        out_specs=(VMEM, VMEM),
        compiler_params=PARAMS,
        cost_estimate=cost(2_000_000_000, 1_000_000),
        name="meet",
    )(got, corner, chain)
    tables = swapped_within(table.reshape(G, 1, LANES), "zs").reshape(G, LANES)
    table = pl.pallas_call(
        sum_kernel,
        out_shape=jax.ShapeDtypeStruct((z_blocks, LANES), F32),
        in_specs=[VMEM],
        out_specs=VMEM,
        compiler_params=PARAMS,
        name="sum",
    )(tables)
    tables = swapped_between(table.reshape(z_blocks, 1, LANES), "zs").reshape(z_blocks, LANES)
    owned = pl.pallas_call(
        final_kernel,
        out_shape=jax.ShapeDtypeStruct((2, MOST), F32),
        in_specs=[VMEM] * 2,
        out_specs=VMEM,
        compiler_params=PARAMS,
        name="final",
    )(tables, picked)
    return (seq.reshape(2, 3, 1, block_z, block_x, rows_y), owned.T)


def solution(mesh):
    in_specs = (
        P(None, None, "zs", "grp"),
        P(None, None, "zs", "grp"),
        P(None, None, "zs", None, None, "grp"),
        P(None, None, None, "zs", None, None, "grp"),
        P(),
        P(),
        P("grp"),
        P("grp"),
        P("grp", None),
    )
    out_specs = (P(None, None, "zs", None, None, "grp"), P("zs", "grp"))
    return jax.shard_map(shards, mesh=mesh, in_specs=in_specs, out_specs=out_specs, check_vma=False)
```

```python
import functools
import math

import jax
import jax.numpy as jnp
from jax import lax
from jax.experimental import pallas as pl
from jax.experimental.pallas import tpu as pltpu
from jax.sharding import PartitionSpec as P

NT = 8
LMAX = 8
PMOM = 3
G = 8
MOST = 96
LANES = 128
XH = 3
CROWS = 16

F32 = jnp.float32
BF16 = jnp.bfloat16
NT_DIMS = (((1,), (1,)), ((), ()))


def passed_along(block, axis, distance):
    devices = range(lax.axis_size(axis))
    route = [((i - distance) % len(devices), i) for i in devices]
    return lax.ppermute(block, axis, route)


def split_two(value):
    high = value.astype(BF16)
    return high, (value - high.astype(F32)).astype(BF16)


def iota(shape, axis):
    return lax.broadcasted_iota(jnp.int32, shape, axis)


def pack_kernel(block_z, block_x, up_ref, down_ref, out_ref):
    zh = block_z + 1
    slot_lanes = zh * XH
    width_x = block_x * G
    cells = up_ref.shape[3]
    z_blocks = cells // (block_z * width_x)
    up = up_ref[...].astype(F32)
    down = down_ref[...].astype(F32)

    def cross(a, b, c):
        d, e = (c + 1) % 3, (c + 2) % 3
        return up[a, d] * down[b, e] - up[a, e] * down[b, d]

    planes = [cross(0, 0, c) - cross(1, 1, c) for c in range(3)]
    planes += [cross(0, 1, c) + cross(1, 0, c) for c in range(3)]
    lane = iota((1, 2 * LANES), 1)
    half = lane // LANES
    within = lane % LANES
    slot = within // slot_lanes
    cell = within % slot_lanes
    source_row = iota((LANES, 2 * LANES), 0)
    results = []
    for comp in range(6):
        turned = (slot + 12 - comp - 4 * half) % 6
        source = (cell % zh) * width_x + (block_x * (turned + 4 * half) + cell // zh) % width_x
        source = jnp.where((turned < 4) & (slot < 6), source, -1)
        pick = jnp.where(source_row == source, 1.0, 0.0).astype(BF16)
        wide = jnp.concatenate([planes[comp], planes[comp][:, :LANES]], axis=1)
        rows = []
        for zb in range(z_blocks):
            begin = zb * block_z * width_x
            part = wide[:, begin : begin + LANES]
            high = part.astype(BF16).astype(F32)
            rows += [high, part - high]
        left = jnp.concatenate(rows, axis=0).astype(BF16)
        got = jnp.dot(left, pick, preferred_element_type=F32)
        got = got.reshape(z_blocks, 2, NT, 2 * LANES)
        results.append(got[:, 0] + got[:, 1])
    one_slot = iota((NT, LANES), 1) // slot_lanes
    for zb in range(z_blocks):
        for g in range(G):
            at = (g // 4) * LANES
            value = jnp.zeros((NT, LANES), F32)
            for comp in range(6):
                value = jnp.where(
                    one_slot == (comp + g) % 6, results[comp][zb, :, at : at + LANES], value
                )
            out_ref[zb * G + g] = value


def phases(group, depth_z, block_z, block_x, scale):
    row = iota((CROWS, LANES), 0)
    angle = ((group * block_z + row // block_x) * PMOM % depth_z).astype(F32)
    angle = angle * (2.0 * math.pi / depth_z)
    inside = row < block_z * block_x
    cos_z = jnp.where(inside, jnp.cos(angle) * scale, 0.0)[:, :1]
    sin_z = jnp.where(inside, jnp.sin(angle) * scale, 0.0)[:, :1]
    return cos_z, sin_z


def chain_kernel(
    depth_z,
    scale,
    block_z,
    block_x,
    weight_ref,
    offset_ref,
    links_ref,
    links_next_ref,
    forward_ref,
    forward_next_ref,
    lengths_ref,
    separations_ref,
    owners_ref,
    chain_ref,
    corner_ref,
    picked_ref,
    tail_ref,
    link_rows,
    field_rows,
    tails,
):
    place = lax.axis_index("zs")
    rows_y = links_ref.shape[3]
    zh = block_z + 1
    slot_lanes = zh * XH
    count = block_z * block_x
    no_plane = jnp.zeros((block_x, rows_y), F32)

    def fill_links(i, carry):
        for z in range(block_z):
            link_rows[i, block_x * z : block_x * (z + 1)] = links_ref[i, z].astype(F32)
            at = count + block_x * z
            last = z == block_z - 1
            plane = no_plane if last else links_next_ref[i, z].astype(F32)
            link_rows[i, at : at + block_x] = plane
        return carry

    def fill_field(i, carry):
        for z in range(block_z):
            field_rows[i, block_x * z : block_x * (z + 1)] = forward_ref[i, z].astype(F32)
            at = count + block_x * z
            field_rows[i, at : at + block_x] = forward_next_ref[i, z].astype(F32)
        return carry

    lax.fori_loop(0, 18, fill_links, 0)
    lax.fori_loop(0, 6, fill_field, 0)

    cos_z, sin_z = phases(place // G, depth_z, block_z, block_x, scale)
    total_rows = link_rows.shape[1]

    def step(length, carry):
        for at in range(0, rows_y, LANES):
            lanes = slice(at, at + LANES)
            vec = [
                pltpu.roll(field_rows[c, :, lanes], total_rows - block_x, 0) for c in range(6)
            ]
            for a in range(3):
                real = None
                imag = None
                for b in range(3):
                    link_real = link_rows[a * 3 + b, :, lanes]
                    link_imag = link_rows[9 + a * 3 + b, :, lanes]
                    term_real = link_real * vec[b] - link_imag * vec[3 + b]
                    term_imag = link_real * vec[3 + b] + link_imag * vec[b]
                    real = term_real if real is None else real + term_real
                    imag = term_imag if imag is None else imag + term_imag
                field_rows[a, :, lanes] = real
                field_rows[3 + a, :, lanes] = imag
                kept = jnp.clip(length + 1 - block_z, 0, LMAX - block_z)
                tails[kept, a, :, lanes] = real[:block_x]
                tails[kept, 3 + a, :, lanes] = imag[:block_x]
                top_real, top_imag = real[:CROWS], imag[:CROWS]
                chain_ref[length, a * CROWS : (a + 1) * CROWS, lanes] = (
                    top_real * cos_z - top_imag * sin_z
                )
                chain_ref[length, (3 + a) * CROWS : (4 + a) * CROWS, lanes] = (
                    top_real * sin_z + top_imag * cos_z
                )
        return carry

    lax.fori_loop(0, LMAX, step, 0)
    tail_ref[...] = tails[: LMAX - block_z]

    shape = (6 * CROWS, LANES)
    row = iota(shape, 0)
    lane = iota(shape, 1)
    comp = row // CROWS
    z_step = lane % slot_lanes % zh - row % CROWS // block_x
    x_step = lane % slot_lanes // zh - row % block_x
    here = (lane // slot_lanes == (comp + place % G) % 6) & (row % CROWS < count)
    sums = [jnp.zeros(shape, F32), jnp.zeros(shape, F32)]
    for k in range(8):
        match = here & (x_step == offset_ref[0, k]) & (z_step == offset_ref[2, k])
        for y_step in range(2):
            taken = jnp.where(offset_ref[1, k] == y_step, weight_ref[k], 0.0)
            sums[y_step] = sums[y_step] + jnp.where(match, taken, 0.0)
    for y_step in range(2):
        high, low = split_two(sums[y_step])
        corner_ref[0, y_step * 6 * CROWS : (y_step + 1) * 6 * CROWS] = high
        corner_ref[1, y_step * 6 * CROWS : (y_step + 1) * 6 * CROWS] = low

    mine = owners_ref[...] == place
    codes = (lengths_ref[...] * (2 * NT) + separations_ref[...]).astype(F32)
    member = jnp.where(mine, 1.0, 0.0)
    below = jnp.where(iota((LANES, LANES), 0) < iota((LANES, LANES), 1), 1.0, 0.0)
    earlier = jnp.dot(member.astype(BF16), below.astype(BF16), preferred_element_type=F32)
    running = jnp.zeros((1, 1), F32)
    picked = jnp.zeros((8, LANES), F32)
    slots = iota((LANES, LANES), 0).astype(F32)
    head = iota((8, LANES), 0) == 0
    for i in range(member.shape[0]):
        key = jnp.where(member[i : i + 1] > 0.5, earlier[i : i + 1] + running, -1.0)
        hits = jnp.where(slots == key, 1.0, 0.0).astype(BF16)
        left = jnp.where(head, codes[i : i + 1], 1.0).astype(BF16)
        picked = picked + lax.dot_general(left, hits, NT_DIMS, preferred_element_type=F32)
        running = running + jnp.sum(member[i : i + 1], axis=1, keepdims=True)
    lane_of = picked[0:1].astype(jnp.int32) + iota((8, LANES), 0) % 2 * NT
    picked_ref[...] = jnp.where(picked[1:2] > 0.5, lane_of, -1)


def tail_kernel(depth_z, scale, block_z, block_x, links_ref, tail_ref, extra_ref):
    cos_z, sin_z = phases(lax.axis_index("zs") // G, depth_z, block_z, block_x, scale)
    extra_ref[...] = jnp.zeros_like(extra_ref)
    past = LMAX - block_z
    vecs = [[tail_ref[k, c] for c in range(6)] for k in range(past)]
    for z in range(block_z - 1, block_z - 1 - past, -1):
        links = [links_ref[i, z].astype(F32) for i in range(18)]
        at = z * block_x
        cos_at, sin_at = cos_z[at : at + block_x], sin_z[at : at + block_x]
        moved = []
        for k in range(past - (block_z - 1 - z)):
            vec = vecs[k]
            real, imag = [], []
            for a in range(3):
                row = [(links[3 * a + b], links[9 + 3 * a + b]) for b in range(3)]
                real.append(sum(row[b][0] * vec[b] - row[b][1] * vec[3 + b] for b in range(3)))
                imag.append(sum(row[b][0] * vec[3 + b] + row[b][1] * vec[b] for b in range(3)))
            moved.append(real + imag)
            kept = k + block_z - 1 - z
            for a in range(3):
                first = a * CROWS + at
                extra_ref[kept, first : first + block_x] = real[a] * cos_at - imag[a] * sin_at
                first = (3 + a) * CROWS + at
                extra_ref[kept, first : first + block_x] = real[a] * sin_at + imag[a] * cos_at
        vecs = moved


def meet_kernel(block_z, block_x, got_ref, corner_ref, chain_ref, extra_ref, seq_ref, table_ref):
    rows_y = got_ref.shape[0] * NT
    got = got_ref[...].reshape(rows_y, LANES)
    high, low = split_two(got)
    dot = functools.partial(
        lax.dot_general, dimension_numbers=NT_DIMS, preferred_element_type=F32
    )
    both = dot(corner_ref[0], high) + dot(corner_ref[0], low) + dot(corner_ref[1], high)
    size = 6 * CROWS
    seq = both[:size] + pltpu.roll(both[size:], rows_y - NT, 1)
    for comp in range(6):
        for z in range(block_z):
            at = comp * CROWS + z * block_x
            seq_ref[comp, z] = seq[at : at + block_x]
    turned = jnp.concatenate([-seq[3 * CROWS :], seq[: 3 * CROWS]], axis=0)
    sums = []
    for length in range(LMAX):
        chain = chain_ref[length]
        if length >= block_z:
            chain = chain + extra_ref[length - block_z]
        for field in (seq, turned):
            prod = field * chain
            part = prod[:8]
            for at in range(8, size, 8):
                part = part + prod[at : at + 8]
            narrow = part[:, :LANES]
            for at in range(LANES, rows_y, LANES):
                narrow = narrow + part[:, at : at + LANES]
            sums.append(jnp.sum(narrow, axis=0, keepdims=True))
    table = jnp.concatenate(sums, axis=0)
    for shift in (64, 32, 16, 8):
        table = table + pltpu.roll(table, shift, 1)
    mine = iota((2 * LMAX, LANES), 1) // NT == iota((2 * LMAX, LANES), 0)
    flat = jnp.sum(jnp.where(mine, table, 0.0), axis=0, keepdims=True)
    table_ref[...] = flat


def final_kernel(tables_ref, picked_ref, out_ref):
    total = jnp.sum(tables_ref[...], axis=0, keepdims=True)
    picked = picked_ref[...]
    value = jnp.take_along_axis(
        jnp.broadcast_to(total, picked.shape), jnp.maximum(picked, 0), axis=1
    )
    value = jnp.where(picked >= 0, value, 0.0)
    out_ref[...] = value[:2, : out_ref.shape[1]]


VMEM = pl.BlockSpec(memory_space=pltpu.VMEM)
SMEM = pl.BlockSpec(memory_space=pltpu.SMEM)


def cost(flops, moved):
    return pl.CostEstimate(flops=flops, bytes_accessed=moved, transcendentals=0)


PARAMS = pltpu.CompilerParams(vmem_limit_bytes=16 * 1024 * 1024)
WIDE_PARAMS = pltpu.CompilerParams(vmem_limit_bytes=60 * 1024 * 1024)


def shards(
    quark_up,
    quark_down,
    forward,
    gauge_links,
    corner_weight,
    corner_offset,
    lengths,
    separations,
    owner_map,
):
    devices = lax.axis_size("zs")
    block_z, block_x, rows_y = forward.shape[3:]
    cells = quark_up.shape[3]
    depth_z = cells // (block_x * G)
    scale = 1.0 / math.sqrt(cells * (rows_y // NT))
    links = gauge_links.reshape(18, block_z, block_x, rows_y)
    field = forward.reshape(6, block_z, block_x, rows_y)

    links_next = passed_along(links, "zs", -G)
    field_next = passed_along(field, "zs", -G)
    payload = pl.pallas_call(
        functools.partial(pack_kernel, block_z, block_x),
        out_shape=jax.ShapeDtypeStruct((devices, NT, LANES), F32),
        grid=(1,),
        in_specs=[pl.BlockSpec(quark_up.shape, lambda i: (0, 0, 0, 0))] * 2,
        out_specs=pl.BlockSpec((devices, NT, LANES), lambda i: (0, 0, 0)),
        compiler_params=WIDE_PARAMS,
        cost_estimate=cost(2_000_000_000, 400_000),
        name="pack",
    )(quark_up, quark_down)
    got = lax.all_to_all(payload, "zs", split_axis=0, concat_axis=0, tiled=True)

    requests = (lengths.shape[0] // LANES, LANES)
    past = LMAX - block_z
    chain, corner, picked, tail = pl.pallas_call(
        functools.partial(chain_kernel, depth_z, scale, block_z, block_x),
        out_shape=(
            jax.ShapeDtypeStruct((LMAX, 6 * CROWS, rows_y), F32),
            jax.ShapeDtypeStruct((2, 12 * CROWS, LANES), BF16),
            jax.ShapeDtypeStruct((8, LANES), jnp.int32),
            jax.ShapeDtypeStruct((past, 6, block_x, rows_y), F32),
        ),
        in_specs=[SMEM, SMEM] + [VMEM] * 7,
        out_specs=(VMEM,) * 4,
        scratch_shapes=[
            pltpu.VMEM((18, 2 * block_z * block_x, rows_y), F32),
            pltpu.VMEM((6, 2 * block_z * block_x, rows_y), F32),
            pltpu.VMEM((past + 1, 6, block_x, rows_y), F32),
        ],
        compiler_params=PARAMS,
        cost_estimate=cost(3_000_000_000, 200_000),
        name="chain",
    )(
        corner_weight,
        corner_offset.T,
        links,
        links_next,
        field,
        field_next,
        lengths.reshape(requests),
        separations.reshape(requests),
        owner_map.reshape(requests),
    )

    extra = pl.pallas_call(
        functools.partial(tail_kernel, depth_z, scale, block_z, block_x),
        out_shape=jax.ShapeDtypeStruct((past, 6 * CROWS, rows_y), F32),
        in_specs=[VMEM] * 2,
        out_specs=VMEM,
        compiler_params=PARAMS,
        cost_estimate=cost(100_000_000, 200_000),
        name="tail",
    )(links, passed_along(tail, "zs", -G))

    seq, table = pl.pallas_call(
        functools.partial(meet_kernel, block_z, block_x),
        out_shape=(
            jax.ShapeDtypeStruct((6, block_z, block_x, rows_y), F32),
            jax.ShapeDtypeStruct((1, LANES), F32),
        ),
        in_specs=[VMEM] * 4,
        out_specs=(VMEM, VMEM),
        compiler_params=PARAMS,
        cost_estimate=cost(2_000_000_000, 1_000_000),
        name="meet",
    )(got, corner, chain, extra)
    tables = lax.all_gather(table, "zs", axis=0, tiled=True)
    owned = pl.pallas_call(
        final_kernel,
        out_shape=jax.ShapeDtypeStruct((2, MOST), F32),
        in_specs=[VMEM] * 2,
        out_specs=VMEM,
        compiler_params=PARAMS,
        name="final",
    )(tables, picked)
    return (seq.reshape(2, 3, 1, block_z, block_x, rows_y), owned.T)


def solution(mesh):
    in_specs = (
        P(None, None, "zs", "grp"),
        P(None, None, "zs", "grp"),
        P(None, None, "zs", None, None, "grp"),
        P(None, None, None, "zs", None, None, "grp"),
        P(),
        P(),
        P("grp"),
        P("grp"),
        P("grp", None),
    )
    out_specs = (P(None, None, "zs", None, None, "grp"), P("zs", "grp"))
    return jax.shard_map(shards, mesh=mesh, in_specs=in_specs, out_specs=out_specs, check_vma=False)
```

```python
import functools
import math

import jax
import jax.numpy as jnp
from jax import lax
from jax.experimental import pallas as pl
from jax.experimental.pallas import tpu as pltpu
from jax.sharding import PartitionSpec as P

NT = 8
LMAX = 8
PMOM = 3
G = 8
MOST = 96
LANES = 128
XH = 3
CROWS = 16

F32 = jnp.float32
BF16 = jnp.bfloat16
NT_DIMS = (((1,), (1,)), ((), ()))


def passed_along(block, axis, distance):
    devices = range(lax.axis_size(axis))
    route = [((i - distance) % len(devices), i) for i in devices]
    return lax.ppermute(block, axis, route)


def split_two(value):
    high = value.astype(BF16)
    return high, (value - high.astype(F32)).astype(BF16)


def iota(shape, axis):
    return lax.broadcasted_iota(jnp.int32, shape, axis)


def pack_kernel(block_z, block_x, up_ref, down_ref, links_ref, forward_ref, out_ref, edge_ref):
    edge_ref[0:18] = links_ref[:, 0]
    edge_ref[18:24] = forward_ref[:, 0]
    edge_ref[24:30] = forward_ref[:, 1]
    zh = block_z + 1
    slot_lanes = zh * XH
    width_x = block_x * G
    cells = up_ref.shape[3]
    z_blocks = cells // (block_z * width_x)
    up = up_ref[...].astype(F32)
    down = down_ref[...].astype(F32)

    def cross(a, b, c):
        d, e = (c + 1) % 3, (c + 2) % 3
        return up[a, d] * down[b, e] - up[a, e] * down[b, d]

    planes = [cross(0, 0, c) - cross(1, 1, c) for c in range(3)]
    planes += [cross(0, 1, c) + cross(1, 0, c) for c in range(3)]
    lane = iota((1, 2 * LANES), 1)
    half = lane // LANES
    within = lane % LANES
    slot = within // slot_lanes
    cell = within % slot_lanes
    source_row = iota((LANES, 2 * LANES), 0)
    results = []
    for comp in range(6):
        turned = (slot + 12 - comp - 4 * half) % 6
        source = (cell % zh) * width_x + (block_x * (turned + 4 * half) + cell // zh) % width_x
        source = jnp.where((turned < 4) & (slot < 6), source, -1)
        pick = jnp.where(source_row == source, 1.0, 0.0).astype(BF16)
        wide = jnp.concatenate([planes[comp], planes[comp][:, :LANES]], axis=1)
        rows = []
        for zb in range(z_blocks):
            begin = zb * block_z * width_x
            part = wide[:, begin : begin + LANES]
            high = part.astype(BF16).astype(F32)
            rows += [high, part - high]
        left = jnp.concatenate(rows, axis=0).astype(BF16)
        got = jnp.dot(left, pick, preferred_element_type=F32)
        got = got.reshape(z_blocks, 2, NT, 2 * LANES)
        results.append(got[:, 0] + got[:, 1])
    one_slot = iota((NT, LANES), 1) // slot_lanes
    for zb in range(z_blocks):
        for g in range(G):
            at = (g // 4) * LANES
            value = jnp.zeros((NT, LANES), F32)
            for comp in range(6):
                value = jnp.where(
                    one_slot == (comp + g) % 6, results[comp][zb, :, at : at + LANES], value
                )
            out_ref[zb * G + g] = value


def phases(group, depth_z, block_z, block_x, scale):
    row = iota((CROWS, LANES), 0)
    angle = ((group * block_z + row // block_x) * PMOM % depth_z).astype(F32)
    angle = angle * (2.0 * math.pi / depth_z)
    inside = row < block_z * block_x
    cos_z = jnp.where(inside, jnp.cos(angle) * scale, 0.0)[:, :1]
    sin_z = jnp.where(inside, jnp.sin(angle) * scale, 0.0)[:, :1]
    return cos_z, sin_z


def chain_kernel(
    depth_z,
    scale,
    block_z,
    block_x,
    weight_ref,
    offset_ref,
    links_ref,
    links_next_ref,
    forward_ref,
    forward_next_ref,
    lengths_ref,
    separations_ref,
    owners_ref,
    chain_ref,
    corner_ref,
    picked_ref,
    link_rows,
    field_rows,
    index_rows,
    index_done,
):
    sources = (lengths_ref, separations_ref, owners_ref)
    copies = [
        pltpu.make_async_copy(sources[i], index_rows.at[i], index_done.at[i]) for i in range(3)
    ]
    for copy in copies:
        copy.start()
    place = lax.axis_index("zs")
    rows_y = links_ref.shape[3]
    zh = block_z + 1
    slot_lanes = zh * XH
    count = block_z * block_x
    no_plane = jnp.zeros((block_x, rows_y), F32)

    def fill_links(i, carry):
        for z in range(block_z):
            link_rows[i, block_x * z : block_x * (z + 1)] = links_ref[i, z].astype(F32)
            at = count + block_x * z
            last = z == block_z - 1
            plane = no_plane if last else links_next_ref[i, z].astype(F32)
            link_rows[i, at : at + block_x] = plane
        return carry

    def fill_field(i, carry):
        for z in range(block_z):
            field_rows[i, block_x * z : block_x * (z + 1)] = forward_ref[i, z].astype(F32)
            at = count + block_x * z
            field_rows[i, at : at + block_x] = forward_next_ref[i, z].astype(F32)
        return carry

    lax.fori_loop(0, 18, fill_links, 0)
    lax.fori_loop(0, 6, fill_field, 0)

    cos_z, sin_z = phases(place // G, depth_z, block_z, block_x, scale)
    total_rows = link_rows.shape[1]

    def step(length, carry):
        for at in range(0, rows_y, LANES):
            lanes = slice(at, at + LANES)
            vec = [
                pltpu.roll(field_rows[c, :, lanes], total_rows - block_x, 0) for c in range(6)
            ]
            for a in range(3):
                real = None
                imag = None
                for b in range(3):
                    link_real = link_rows[a * 3 + b, :, lanes]
                    link_imag = link_rows[9 + a * 3 + b, :, lanes]
                    term_real = link_real * vec[b] - link_imag * vec[3 + b]
                    term_imag = link_real * vec[3 + b] + link_imag * vec[b]
                    real = term_real if real is None else real + term_real
                    imag = term_imag if imag is None else imag + term_imag
                field_rows[a, :, lanes] = real
                field_rows[3 + a, :, lanes] = imag
                top_real, top_imag = real[:CROWS], imag[:CROWS]
                chain_ref[length, a * CROWS : (a + 1) * CROWS, lanes] = (
                    top_real * cos_z - top_imag * sin_z
                )
                chain_ref[length, (3 + a) * CROWS : (4 + a) * CROWS, lanes] = (
                    top_real * sin_z + top_imag * cos_z
                )
        return carry

    lax.fori_loop(0, LMAX, step, 0)

    shape = (6 * CROWS, LANES)
    row = iota(shape, 0)
    lane = iota(shape, 1)
    comp = row // CROWS
    z_step = lane % slot_lanes % zh - row % CROWS // block_x
    x_step = lane % slot_lanes // zh - row % block_x
    here = (lane // slot_lanes == (comp + place % G) % 6) & (row % CROWS < count)
    sums = [jnp.zeros(shape, F32), jnp.zeros(shape, F32)]
    for k in range(8):
        match = here & (x_step == offset_ref[0, k]) & (z_step == offset_ref[2, k])
        for y_step in range(2):
            taken = jnp.where(offset_ref[1, k] == y_step, weight_ref[k], 0.0)
            sums[y_step] = sums[y_step] + jnp.where(match, taken, 0.0)
    for y_step in range(2):
        high, low = split_two(sums[y_step])
        corner_ref[0, y_step * 6 * CROWS : (y_step + 1) * 6 * CROWS] = high
        corner_ref[1, y_step * 6 * CROWS : (y_step + 1) * 6 * CROWS] = low

    for copy in copies:
        copy.wait()
    mine = index_rows[2] == place
    codes = (index_rows[0] * (2 * NT) + index_rows[1]).astype(F32)
    member = jnp.where(mine, 1.0, 0.0)
    below = jnp.where(iota((LANES, LANES), 0) < iota((LANES, LANES), 1), 1.0, 0.0)
    earlier = jnp.dot(member.astype(BF16), below.astype(BF16), preferred_element_type=F32)
    running = jnp.zeros((1, 1), F32)
    picked = jnp.zeros((8, LANES), F32)
    slots = iota((LANES, LANES), 0).astype(F32)
    head = iota((8, LANES), 0) == 0
    for i in range(member.shape[0]):
        key = jnp.where(member[i : i + 1] > 0.5, earlier[i : i + 1] + running, -1.0)
        hits = jnp.where(slots == key, 1.0, 0.0).astype(BF16)
        left = jnp.where(head, codes[i : i + 1], 1.0).astype(BF16)
        picked = picked + lax.dot_general(left, hits, NT_DIMS, preferred_element_type=F32)
        running = running + jnp.sum(member[i : i + 1], axis=1, keepdims=True)
    lane_of = picked[0:1].astype(jnp.int32) + iota((8, LANES), 0) % 2 * NT
    picked_ref[...] = jnp.where(picked[1:2] > 0.5, lane_of, -1)


def link_times(links, vec):
    real, imag = [], []
    for a in range(3):
        row = [(links[3 * a + b], links[9 + 3 * a + b]) for b in range(3)]
        real.append(sum(row[b][0] * vec[b] - row[b][1] * vec[3 + b] for b in range(3)))
        imag.append(sum(row[b][0] * vec[3 + b] + row[b][1] * vec[b] for b in range(3)))
    return real + imag


def tail_kernel(
    depth_z, scale, block_z, block_x, links_ref, links_next_ref, edge_ref, corner_ref, extra_ref
):
    cos_z, sin_z = phases(lax.axis_index("zs") // G, depth_z, block_z, block_x, scale)
    extra_ref[...] = jnp.zeros_like(extra_ref)
    planes = edge_ref[...].astype(F32)
    near = [planes[18 + c] for c in range(6)]
    far = link_times([planes[i] for i in range(18)], [planes[24 + c] for c in range(6)])
    vecs = [near, far]
    for z in range(2 * block_z - 1, block_z - 3, -1):
        ref = links_ref if z < block_z else links_next_ref
        links = [ref[i, z % block_z].astype(F32) for i in range(18)]
        vecs = [link_times(links, vec) for vec in vecs]
        if z < block_z:
            at = z * block_x
            cos_at, sin_at = cos_z[at : at + block_x], sin_z[at : at + block_x]
            for k, vec in enumerate(vecs):
                kept = k + block_z - 1 - z
                for a in range(3):
                    real, imag = vec[a], vec[3 + a]
                    first = a * CROWS + at
                    extra_ref[kept, first : first + block_x] = real * cos_at - imag * sin_at
                    first = (3 + a) * CROWS + at
                    extra_ref[kept, first : first + block_x] = real * sin_at + imag * cos_at
            vecs = vecs[:-1]


def meet_kernel(block_z, block_x, got_ref, corner_ref, chain_ref, extra_ref, seq_ref, table_ref):
    rows_y = got_ref.shape[0] * NT
    got = got_ref[...].reshape(rows_y, LANES)
    high, low = split_two(got)
    dot = functools.partial(
        lax.dot_general, dimension_numbers=NT_DIMS, preferred_element_type=F32
    )
    both = dot(corner_ref[0], high) + dot(corner_ref[0], low) + dot(corner_ref[1], high)
    size = 6 * CROWS
    seq = both[:size] + pltpu.roll(both[size:], rows_y - NT, 1)
    for comp in range(6):
        for z in range(block_z):
            at = comp * CROWS + z * block_x
            seq_ref[comp, z] = seq[at : at + block_x]
    turned = jnp.concatenate([-seq[3 * CROWS :], seq[: 3 * CROWS]], axis=0)
    sums = []
    for length in range(LMAX):
        chain = chain_ref[length]
        if length >= block_z:
            chain = chain + extra_ref[length - block_z]
        for field in (seq, turned):
            prod = field * chain
            part = prod[:8]
            for at in range(8, size, 8):
                part = part + prod[at : at + 8]
            narrow = part[:, :LANES]
            for at in range(LANES, rows_y, LANES):
                narrow = narrow + part[:, at : at + LANES]
            sums.append(jnp.sum(narrow, axis=0, keepdims=True))
    table = jnp.concatenate(sums, axis=0)
    for shift in (64, 32, 16, 8):
        table = table + pltpu.roll(table, shift, 1)
    mine = iota((2 * LMAX, LANES), 1) // NT == iota((2 * LMAX, LANES), 0)
    flat = jnp.sum(jnp.where(mine, table, 0.0), axis=0, keepdims=True)
    table_ref[...] = jnp.broadcast_to(flat, table_ref.shape)


def final_kernel(tables_ref, picked_ref, out_ref):
    total = jnp.sum(tables_ref[...], axis=0, keepdims=True)
    picked = picked_ref[...]
    value = jnp.take_along_axis(
        jnp.broadcast_to(total, picked.shape), jnp.maximum(picked, 0), axis=1
    )
    value = jnp.where(picked >= 0, value, 0.0)
    out_ref[...] = value[:2, : out_ref.shape[1]]


VMEM = pl.BlockSpec(memory_space=pltpu.VMEM)
SMEM = pl.BlockSpec(memory_space=pltpu.SMEM)


def cost(flops, moved):
    return pl.CostEstimate(flops=flops, bytes_accessed=moved, transcendentals=0)


PARAMS = pltpu.CompilerParams(vmem_limit_bytes=16 * 1024 * 1024)
WIDE_PARAMS = pltpu.CompilerParams(vmem_limit_bytes=60 * 1024 * 1024)


def shards(
    quark_up,
    quark_down,
    forward,
    gauge_links,
    corner_weight,
    corner_offset,
    lengths,
    separations,
    owner_map,
):
    devices = lax.axis_size("zs")
    block_z, block_x, rows_y = forward.shape[3:]
    cells = quark_up.shape[3]
    depth_z = cells // (block_x * G)
    scale = 1.0 / math.sqrt(cells * (rows_y // NT))
    links = gauge_links.reshape(18, block_z, block_x, rows_y)
    field = forward.reshape(6, block_z, block_x, rows_y)

    links_next = passed_along(links, "zs", -G)
    field_next = passed_along(field, "zs", -G)
    payload, edge = pl.pallas_call(
        functools.partial(pack_kernel, block_z, block_x),
        out_shape=(
            jax.ShapeDtypeStruct((devices, NT, LANES), F32),
            jax.ShapeDtypeStruct((30, block_x, rows_y), BF16),
        ),
        grid=(1,),
        in_specs=[
            pl.BlockSpec(quark_up.shape, lambda i: (0, 0, 0, 0)),
            pl.BlockSpec(quark_down.shape, lambda i: (0, 0, 0, 0)),
            pl.BlockSpec((18, 1, block_x, rows_y), lambda i: (0, 0, 0, 0)),
            pl.BlockSpec((6, 2, block_x, rows_y), lambda i: (0, 0, 0, 0)),
        ],
        out_specs=(
            pl.BlockSpec((devices, NT, LANES), lambda i: (0, 0, 0)),
            pl.BlockSpec((30, block_x, rows_y), lambda i: (0, 0, 0)),
        ),
        compiler_params=WIDE_PARAMS,
        cost_estimate=cost(2_000_000_000, 400_000),
        name="pack",
    )(quark_up, quark_down, links, field)
    got = lax.all_to_all(payload, "zs", split_axis=0, concat_axis=0, tiled=True)

    requests = (lengths.shape[0] // LANES, LANES)
    past = LMAX - block_z
    edge, links_next = lax.optimization_barrier((edge, links_next))
    edge_next = passed_along(edge, "zs", -2 * G)
    chain, corner, picked = pl.pallas_call(
        functools.partial(chain_kernel, depth_z, scale, block_z, block_x),
        out_shape=(
            jax.ShapeDtypeStruct((LMAX, 6 * CROWS, rows_y), F32),
            jax.ShapeDtypeStruct((2, 12 * CROWS, LANES), BF16),
            jax.ShapeDtypeStruct((8, LANES), jnp.int32),
        ),
        in_specs=[SMEM, SMEM] + [VMEM] * 4 + [pl.BlockSpec(memory_space=pl.ANY)] * 3,
        out_specs=(VMEM,) * 3,
        scratch_shapes=[
            pltpu.VMEM((18, 2 * block_z * block_x, rows_y), F32),
            pltpu.VMEM((6, 2 * block_z * block_x, rows_y), F32),
            pltpu.VMEM((3,) + requests, jnp.int32),
            pltpu.SemaphoreType.DMA((3,)),
        ],
        compiler_params=PARAMS,
        cost_estimate=cost(3_000_000_000, 200_000),
        name="chain",
    )(
        corner_weight,
        corner_offset.T,
        links,
        links_next,
        field,
        field_next,
        lengths.reshape(requests),
        separations.reshape(requests),
        owner_map.reshape(requests),
    )

    extra = pl.pallas_call(
        functools.partial(tail_kernel, depth_z, scale, block_z, block_x),
        out_shape=jax.ShapeDtypeStruct((past, 6 * CROWS, rows_y), F32),
        in_specs=[VMEM] * 3 + [pl.BlockSpec(memory_space=pl.ANY)],
        out_specs=VMEM,
        compiler_params=PARAMS,
        cost_estimate=cost(400_000_000, 200_000),
        name="tail",
    )(links, links_next, edge_next, corner)

    seq, table = pl.pallas_call(
        functools.partial(meet_kernel, block_z, block_x),
        out_shape=(
            jax.ShapeDtypeStruct((6, block_z, block_x, rows_y), F32),
            jax.ShapeDtypeStruct((devices, LANES), F32),
        ),
        in_specs=[VMEM] * 4,
        out_specs=(VMEM, VMEM),
        compiler_params=PARAMS,
        cost_estimate=cost(2_000_000_000, 1_000_000),
        name="meet",
    )(got, corner, chain, extra)
    tables = lax.all_to_all(
        table.reshape(devices, 1, LANES), "zs", split_axis=0, concat_axis=0, tiled=True
    ).reshape(devices, LANES)
    owned = pl.pallas_call(
        final_kernel,
        out_shape=jax.ShapeDtypeStruct((2, MOST), F32),
        in_specs=[VMEM] * 2,
        out_specs=VMEM,
        compiler_params=PARAMS,
        name="final",
    )(tables, picked)
    return (seq.reshape(2, 3, 1, block_z, block_x, rows_y), owned.T)


def solution(mesh):
    in_specs = (
        P(None, None, "zs", "grp"),
        P(None, None, "zs", "grp"),
        P(None, None, "zs", None, None, "grp"),
        P(None, None, None, "zs", None, None, "grp"),
        P(),
        P(),
        P("grp"),
        P("grp"),
        P("grp", None),
    )
    out_specs = (P(None, None, "zs", None, None, "grp"), P("zs", "grp"))
    return jax.shard_map(shards, mesh=mesh, in_specs=in_specs, out_specs=out_specs, check_vma=False)
```

```python
import functools
import math

import jax
import jax.numpy as jnp
from jax import lax
from jax.experimental import pallas as pl
from jax.experimental.pallas import tpu as pltpu
from jax.sharding import PartitionSpec as P

NT = 8
LMAX = 8
PMOM = 3
G = 8
MOST = 96
LANES = 128
XH = 3
CROWS = 16

F32 = jnp.float32
BF16 = jnp.bfloat16
NT_DIMS = (((1,), (1,)), ((), ()))


def passed_along(block, axis, distance):
    devices = range(lax.axis_size(axis))
    route = [((i - distance) % len(devices), i) for i in devices]
    return lax.ppermute(block, axis, route)


def split_two(value):
    high = value.astype(BF16)
    return high, (value - high.astype(F32)).astype(BF16)


def iota(shape, axis):
    return lax.broadcasted_iota(jnp.int32, shape, axis)


def pack_kernel(
    block_z,
    block_x,
    weight_ref,
    offset_ref,
    up_ref,
    down_ref,
    lengths_ref,
    separations_ref,
    owners_ref,
    out_ref,
    request_ref,
    table_ref,
):
    codes = lengths_ref[...] * (2 * NT) + separations_ref[...]
    request_ref[...] = owners_ref[...] * LANES + codes
    lane = iota((8, LANES), 1)
    table = jnp.zeros((8, LANES), F32)
    for k in range(8):
        corner = offset_ref[0, k] * 4 + offset_ref[1, k] * 2 + offset_ref[2, k]
        table = jnp.where(lane == corner, weight_ref[k], table)
    table_ref[...] = table
    zh = block_z + 1
    slot_lanes = zh * XH
    width_x = block_x * G
    cells = up_ref.shape[3]
    z_blocks = cells // (block_z * width_x)
    up = up_ref[...].astype(F32)
    down = down_ref[...].astype(F32)

    def cross(a, b, c):
        d, e = (c + 1) % 3, (c + 2) % 3
        return up[a, d] * down[b, e] - up[a, e] * down[b, d]

    planes = [cross(0, 0, c) - cross(1, 1, c) for c in range(3)]
    planes += [cross(0, 1, c) + cross(1, 0, c) for c in range(3)]
    lane = iota((1, 2 * LANES), 1)
    half = lane // LANES
    within = lane % LANES
    slot = within // slot_lanes
    cell = within % slot_lanes
    source_row = iota((LANES, 2 * LANES), 0)
    results = []
    for comp in range(6):
        turned = (slot + 12 - comp - 4 * half) % 6
        source = (cell % zh) * width_x + (block_x * (turned + 4 * half) + cell // zh) % width_x
        source = jnp.where((turned < 4) & (slot < 6), source, -1)
        pick = jnp.where(source_row == source, 1.0, 0.0).astype(BF16)
        wide = jnp.concatenate([planes[comp], planes[comp][:, :LANES]], axis=1)
        rows = []
        for zb in range(z_blocks):
            begin = zb * block_z * width_x
            part = wide[:, begin : begin + LANES]
            high = part.astype(BF16).astype(F32)
            rows += [high, part - high]
        left = jnp.concatenate(rows, axis=0).astype(BF16)
        got = jnp.dot(left, pick, preferred_element_type=F32)
        got = got.reshape(z_blocks, 2, NT, 2 * LANES)
        results.append(got[:, 0] + got[:, 1])
    one_slot = iota((NT, LANES), 1) // slot_lanes
    for zb in range(z_blocks):
        for g in range(G):
            at = (g // 4) * LANES
            value = jnp.zeros((NT, LANES), F32)
            for comp in range(6):
                value = jnp.where(
                    one_slot == (comp + g) % 6, results[comp][zb, :, at : at + LANES], value
                )
            out_ref[zb * G + g] = value


def edge_kernel(links_ref, forward_ref, ready_ref, edge_ref):
    edge_ref[0:18] = links_ref[:, 0]
    edge_ref[18:24] = forward_ref[:, 0]
    edge_ref[24:30] = forward_ref[:, 1]


def phases(group, depth_z, block_z, block_x, scale):
    row = iota((CROWS, LANES), 0)
    angle = ((group * block_z + row // block_x) * PMOM % depth_z).astype(F32)
    angle = angle * (2.0 * math.pi / depth_z)
    inside = row < block_z * block_x
    cos_z = jnp.where(inside, jnp.cos(angle) * scale, 0.0)[:, :1]
    sin_z = jnp.where(inside, jnp.sin(angle) * scale, 0.0)[:, :1]
    return cos_z, sin_z


def chain_kernel(
    depth_z,
    scale,
    block_z,
    block_x,
    table_ref,
    request_ref,
    links_ref,
    links_next_ref,
    forward_ref,
    forward_next_ref,
    chain_ref,
    corner_ref,
    picked_ref,
    link_rows,
    field_rows,
):
    place = lax.axis_index("zs")
    rows_y = links_ref.shape[3]
    zh = block_z + 1
    slot_lanes = zh * XH
    count = block_z * block_x
    no_plane = jnp.zeros((block_x, rows_y), F32)

    def fill_links(i, carry):
        for z in range(block_z):
            link_rows[i, block_x * z : block_x * (z + 1)] = links_ref[i, z].astype(F32)
            at = count + block_x * z
            last = z == block_z - 1
            plane = no_plane if last else links_next_ref[i, z].astype(F32)
            link_rows[i, at : at + block_x] = plane
        return carry

    def fill_field(i, carry):
        for z in range(block_z):
            field_rows[i, block_x * z : block_x * (z + 1)] = forward_ref[i, z].astype(F32)
            at = count + block_x * z
            field_rows[i, at : at + block_x] = forward_next_ref[i, z].astype(F32)
        return carry

    lax.fori_loop(0, 18, fill_links, 0)
    lax.fori_loop(0, 6, fill_field, 0)

    cos_z, sin_z = phases(place // G, depth_z, block_z, block_x, scale)
    total_rows = link_rows.shape[1]

    def step(length, carry):
        for at in range(0, rows_y, LANES):
            lanes = slice(at, at + LANES)
            vec = [
                pltpu.roll(field_rows[c, :, lanes], total_rows - block_x, 0) for c in range(6)
            ]
            for a in range(3):
                real = None
                imag = None
                for b in range(3):
                    link_real = link_rows[a * 3 + b, :, lanes]
                    link_imag = link_rows[9 + a * 3 + b, :, lanes]
                    term_real = link_real * vec[b] - link_imag * vec[3 + b]
                    term_imag = link_real * vec[3 + b] + link_imag * vec[b]
                    real = term_real if real is None else real + term_real
                    imag = term_imag if imag is None else imag + term_imag
                field_rows[a, :, lanes] = real
                field_rows[3 + a, :, lanes] = imag
                top_real, top_imag = real[:CROWS], imag[:CROWS]
                chain_ref[length, a * CROWS : (a + 1) * CROWS, lanes] = (
                    top_real * cos_z - top_imag * sin_z
                )
                chain_ref[length, (3 + a) * CROWS : (4 + a) * CROWS, lanes] = (
                    top_real * sin_z + top_imag * cos_z
                )
        return carry

    lax.fori_loop(0, LMAX, step, 0)

    shape = (6 * CROWS, LANES)
    row = iota(shape, 0)
    lane = iota(shape, 1)
    comp = row // CROWS
    z_step = lane % slot_lanes % zh - row % CROWS // block_x
    x_step = lane % slot_lanes // zh - row % block_x
    here = (lane // slot_lanes == (comp + place % G) % 6) & (row % CROWS < count)
    here = here & (x_step >= 0) & (x_step < 2) & (z_step >= 0) & (z_step < 2)
    table = jnp.broadcast_to(table_ref[0:1], shape)
    for y_step in range(2):
        corner = jnp.where(here, 4 * x_step + 2 * y_step + z_step, 0)
        weights = jnp.where(here, jnp.take_along_axis(table, corner, axis=1), 0.0)
        high, low = split_two(weights)
        corner_ref[0, y_step * 6 * CROWS : (y_step + 1) * 6 * CROWS] = high
        corner_ref[1, y_step * 6 * CROWS : (y_step + 1) * 6 * CROWS] = low

    request = request_ref[...]
    mine = request // LANES == place
    codes = (request % LANES).astype(F32)
    member = jnp.where(mine, 1.0, 0.0)
    below = jnp.where(iota((LANES, LANES), 0) < iota((LANES, LANES), 1), 1.0, 0.0)
    earlier = jnp.dot(member.astype(BF16), below.astype(BF16), preferred_element_type=F32)
    running = jnp.zeros((1, 1), F32)
    picked = jnp.zeros((8, LANES), F32)
    slots = iota((LANES, LANES), 0).astype(F32)
    head = iota((8, LANES), 0) == 0
    for i in range(member.shape[0]):
        key = jnp.where(member[i : i + 1] > 0.5, earlier[i : i + 1] + running, -1.0)
        hits = jnp.where(slots == key, 1.0, 0.0).astype(BF16)
        left = jnp.where(head, codes[i : i + 1], 1.0).astype(BF16)
        picked = picked + lax.dot_general(left, hits, NT_DIMS, preferred_element_type=F32)
        running = running + jnp.sum(member[i : i + 1], axis=1, keepdims=True)
    lane_of = picked[0:1].astype(jnp.int32) + iota((8, LANES), 0) % 2 * NT
    picked_ref[...] = jnp.where(picked[1:2] > 0.5, lane_of, -1)


def link_times(links, vec):
    real, imag = [], []
    for a in range(3):
        row = [(links[3 * a + b], links[9 + 3 * a + b]) for b in range(3)]
        real.append(sum(row[b][0] * vec[b] - row[b][1] * vec[3 + b] for b in range(3)))
        imag.append(sum(row[b][0] * vec[3 + b] + row[b][1] * vec[b] for b in range(3)))
    return real + imag


def tail_kernel(
    depth_z, scale, block_z, block_x, links_ref, links_next_ref, edge_ref, corner_ref, extra_ref
):
    cos_z, sin_z = phases(lax.axis_index("zs") // G, depth_z, block_z, block_x, scale)
    extra_ref[...] = jnp.zeros_like(extra_ref)
    planes = edge_ref[...].astype(F32)
    near = [planes[18 + c] for c in range(6)]
    far = link_times([planes[i] for i in range(18)], [planes[24 + c] for c in range(6)])
    vecs = [near, far]
    for z in range(2 * block_z - 1, block_z - 3, -1):
        ref = links_ref if z < block_z else links_next_ref
        links = [ref[i, z % block_z].astype(F32) for i in range(18)]
        vecs = [link_times(links, vec) for vec in vecs]
        if z < block_z:
            at = z * block_x
            cos_at, sin_at = cos_z[at : at + block_x], sin_z[at : at + block_x]
            for k, vec in enumerate(vecs):
                kept = k + block_z - 1 - z
                for a in range(3):
                    real, imag = vec[a], vec[3 + a]
                    first = a * CROWS + at
                    extra_ref[kept, first : first + block_x] = real * cos_at - imag * sin_at
                    first = (3 + a) * CROWS + at
                    extra_ref[kept, first : first + block_x] = real * sin_at + imag * cos_at
            vecs = vecs[:-1]


def meet_kernel(block_z, block_x, got_ref, corner_ref, chain_ref, extra_ref, seq_ref, table_ref):
    rows_y = got_ref.shape[0] * NT
    got = got_ref[...].reshape(rows_y, LANES)
    high, low = split_two(got)
    dot = functools.partial(
        lax.dot_general, dimension_numbers=NT_DIMS, preferred_element_type=F32
    )
    both = dot(corner_ref[0], high) + dot(corner_ref[0], low) + dot(corner_ref[1], high)
    size = 6 * CROWS
    seq = both[:size] + pltpu.roll(both[size:], rows_y - NT, 1)
    for comp in range(6):
        for z in range(block_z):
            at = comp * CROWS + z * block_x
            seq_ref[comp, z] = seq[at : at + block_x]
    turned = jnp.concatenate([-seq[3 * CROWS :], seq[: 3 * CROWS]], axis=0)
    sums = []
    for length in range(LMAX):
        chain = chain_ref[length]
        if length >= block_z:
            chain = chain + extra_ref[length - block_z]
        for field in (seq, turned):
            prod = field * chain
            part = prod[:8]
            for at in range(8, size, 8):
                part = part + prod[at : at + 8]
            narrow = part[:, :LANES]
            for at in range(LANES, rows_y, LANES):
                narrow = narrow + part[:, at : at + LANES]
            sums.append(jnp.sum(narrow, axis=0, keepdims=True))
    table = jnp.concatenate(sums, axis=0)
    for shift in (64, 32, 16, 8):
        table = table + pltpu.roll(table, shift, 1)
    mine = iota((2 * LMAX, LANES), 1) // NT == iota((2 * LMAX, LANES), 0)
    flat = jnp.sum(jnp.where(mine, table, 0.0), axis=0, keepdims=True)
    table_ref[...] = jnp.broadcast_to(flat, table_ref.shape)


def final_kernel(tables_ref, picked_ref, out_ref):
    total = jnp.sum(tables_ref[...], axis=0, keepdims=True)
    picked = picked_ref[...]
    value = jnp.take_along_axis(
        jnp.broadcast_to(total, picked.shape), jnp.maximum(picked, 0), axis=1
    )
    value = jnp.where(picked >= 0, value, 0.0)
    out_ref[...] = value[:2, : out_ref.shape[1]]


VMEM = pl.BlockSpec(memory_space=pltpu.VMEM)
SMEM = pl.BlockSpec(memory_space=pltpu.SMEM)


def cost(flops, moved):
    return pl.CostEstimate(flops=flops, bytes_accessed=moved, transcendentals=0)


PARAMS = pltpu.CompilerParams(vmem_limit_bytes=16 * 1024 * 1024)
WIDE_PARAMS = pltpu.CompilerParams(vmem_limit_bytes=60 * 1024 * 1024)


def shards(
    quark_up,
    quark_down,
    forward,
    gauge_links,
    corner_weight,
    corner_offset,
    lengths,
    separations,
    owner_map,
):
    devices = lax.axis_size("zs")
    block_z, block_x, rows_y = forward.shape[3:]
    cells = quark_up.shape[3]
    depth_z = cells // (block_x * G)
    scale = 1.0 / math.sqrt(cells * (rows_y // NT))
    links = gauge_links.reshape(18, block_z, block_x, rows_y)
    field = forward.reshape(6, block_z, block_x, rows_y)

    links_next = passed_along(links, "zs", -G)
    field_next = passed_along(field, "zs", -G)
    requests = (lengths.shape[0] // LANES, LANES)
    payload, request, table = pl.pallas_call(
        functools.partial(pack_kernel, block_z, block_x),
        out_shape=(
            jax.ShapeDtypeStruct((devices, NT, LANES), F32),
            jax.ShapeDtypeStruct(requests, jnp.int32),
            jax.ShapeDtypeStruct((8, LANES), F32),
        ),
        grid=(1,),
        in_specs=[SMEM] * 2
        + [pl.BlockSpec(quark_up.shape, lambda i: (0, 0, 0, 0))] * 2
        + [pl.BlockSpec(requests, lambda i: (0, 0))] * 3,
        out_specs=(
            pl.BlockSpec((devices, NT, LANES), lambda i: (0, 0, 0)),
            pl.BlockSpec(requests, lambda i: (0, 0)),
            pl.BlockSpec((8, LANES), lambda i: (0, 0)),
        ),
        compiler_params=WIDE_PARAMS,
        cost_estimate=cost(2_000_000_000, 400_000),
        name="pack",
    )(
        corner_weight,
        corner_offset.T,
        quark_up,
        quark_down,
        lengths.reshape(requests),
        separations.reshape(requests),
        owner_map.reshape(requests),
    )
    got = lax.all_to_all(payload, "zs", split_axis=0, concat_axis=0, tiled=True)

    past = LMAX - block_z
    edge = pl.pallas_call(
        edge_kernel,
        out_shape=jax.ShapeDtypeStruct((30, block_x, rows_y), BF16),
        in_specs=[VMEM] * 2 + [pl.BlockSpec(memory_space=pl.ANY)],
        out_specs=VMEM,
        compiler_params=PARAMS,
        cost_estimate=cost(50_000_000, 60_000),
        name="edge",
    )(links, field, links_next)
    edge_next = passed_along(edge, "zs", -2 * G)
    chain, corner, picked = pl.pallas_call(
        functools.partial(chain_kernel, depth_z, scale, block_z, block_x),
        out_shape=(
            jax.ShapeDtypeStruct((LMAX, 6 * CROWS, rows_y), F32),
            jax.ShapeDtypeStruct((2, 12 * CROWS, LANES), BF16),
            jax.ShapeDtypeStruct((8, LANES), jnp.int32),
        ),
        in_specs=[VMEM] * 6,
        out_specs=(VMEM,) * 3,
        scratch_shapes=[
            pltpu.VMEM((18, 2 * block_z * block_x, rows_y), F32),
            pltpu.VMEM((6, 2 * block_z * block_x, rows_y), F32),
        ],
        compiler_params=PARAMS,
        cost_estimate=cost(3_000_000_000, 200_000),
        name="chain",
    )(table, request, links, links_next, field, field_next)

    extra = pl.pallas_call(
        functools.partial(tail_kernel, depth_z, scale, block_z, block_x),
        out_shape=jax.ShapeDtypeStruct((past, 6 * CROWS, rows_y), F32),
        in_specs=[VMEM] * 3 + [pl.BlockSpec(memory_space=pl.ANY)],
        out_specs=VMEM,
        compiler_params=PARAMS,
        cost_estimate=cost(400_000_000, 200_000),
        name="tail",
    )(links, links_next, edge_next, corner)

    seq, partial = pl.pallas_call(
        functools.partial(meet_kernel, block_z, block_x),
        out_shape=(
            jax.ShapeDtypeStruct((6, block_z, block_x, rows_y), F32),
            jax.ShapeDtypeStruct((devices, LANES), F32),
        ),
        in_specs=[VMEM] * 4,
        out_specs=(VMEM, VMEM),
        compiler_params=PARAMS,
        cost_estimate=cost(2_000_000_000, 1_000_000),
        name="meet",
    )(got, corner, chain, extra)
    tables = lax.all_to_all(
        partial.reshape(devices, 1, LANES), "zs", split_axis=0, concat_axis=0, tiled=True
    ).reshape(devices, LANES)
    owned = pl.pallas_call(
        final_kernel,
        out_shape=jax.ShapeDtypeStruct((2, MOST), F32),
        in_specs=[VMEM] * 2,
        out_specs=VMEM,
        compiler_params=PARAMS,
        name="final",
    )(tables, picked)
    return (seq.reshape(2, 3, 1, block_z, block_x, rows_y), owned.T)


def solution(mesh):
    in_specs = (
        P(None, None, "zs", "grp"),
        P(None, None, "zs", "grp"),
        P(None, None, "zs", None, None, "grp"),
        P(None, None, None, "zs", None, None, "grp"),
        P(),
        P(),
        P("grp"),
        P("grp"),
        P("grp", None),
    )
    out_specs = (P(None, None, "zs", None, None, "grp"), P("zs", "grp"))
    return jax.shard_map(shards, mesh=mesh, in_specs=in_specs, out_specs=out_specs, check_vma=False)
```

```python
import functools
import math

import jax
import jax.numpy as jnp
from jax import lax
from jax.experimental import pallas as pl
from jax.experimental.pallas import tpu as pltpu
from jax.sharding import PartitionSpec as P

NT = 8
LMAX = 8
PMOM = 3
G = 8
MOST = 96
LANES = 128
XH = 3
CROWS = 16

F32 = jnp.float32
BF16 = jnp.bfloat16
NT_DIMS = (((1,), (1,)), ((), ()))


def passed_along(block, axis, distance):
    devices = range(lax.axis_size(axis))
    route = [((i - distance) % len(devices), i) for i in devices]
    return lax.ppermute(block, axis, route)


def split_two(value):
    high = value.astype(BF16)
    return high, (value - high.astype(F32)).astype(BF16)


def iota(shape, axis):
    return lax.broadcasted_iota(jnp.int32, shape, axis)


def pack_kernel(
    block_z,
    block_x,
    weight_ref,
    offset_ref,
    up_ref,
    down_ref,
    lengths_ref,
    separations_ref,
    owners_ref,
    out_ref,
    request_ref,
    table_ref,
):
    codes = lengths_ref[...] * (2 * NT) + separations_ref[...]
    request_ref[...] = owners_ref[...] * LANES + codes
    lane = iota((8, LANES), 1)
    table = jnp.zeros((8, LANES), F32)
    for k in range(8):
        corner = offset_ref[0, k] * 4 + offset_ref[1, k] * 2 + offset_ref[2, k]
        table = jnp.where(lane == corner, weight_ref[k], table)
    table_ref[...] = table
    zh = block_z + 1
    slot_lanes = zh * XH
    width_x = block_x * G
    cells = up_ref.shape[3]
    z_blocks = cells // (block_z * width_x)
    up = up_ref[...].astype(F32)
    down = down_ref[...].astype(F32)

    def cross(a, b, c):
        d, e = (c + 1) % 3, (c + 2) % 3
        return up[a, d] * down[b, e] - up[a, e] * down[b, d]

    planes = [cross(0, 0, c) - cross(1, 1, c) for c in range(3)]
    planes += [cross(0, 1, c) + cross(1, 0, c) for c in range(3)]
    lane = iota((1, 2 * LANES), 1)
    half = lane // LANES
    within = lane % LANES
    slot = within // slot_lanes
    cell = within % slot_lanes
    source_row = iota((LANES, 2 * LANES), 0)
    results = []
    for comp in range(6):
        turned = (slot + 12 - comp - 4 * half) % 6
        source = (cell % zh) * width_x + (block_x * (turned + 4 * half) + cell // zh) % width_x
        source = jnp.where((turned < 4) & (slot < 6), source, -1)
        pick = jnp.where(source_row == source, 1.0, 0.0).astype(BF16)
        wide = jnp.concatenate([planes[comp], planes[comp][:, :LANES]], axis=1)
        rows = []
        for zb in range(z_blocks):
            begin = zb * block_z * width_x
            part = wide[:, begin : begin + LANES]
            high = part.astype(BF16).astype(F32)
            rows += [high, part - high]
        left = jnp.concatenate(rows, axis=0).astype(BF16)
        got = jnp.dot(left, pick, preferred_element_type=F32)
        got = got.reshape(z_blocks, 2, NT, 2 * LANES)
        results.append(got[:, 0] + got[:, 1])
    one_slot = iota((NT, LANES), 1) // slot_lanes
    for zb in range(z_blocks):
        for g in range(G):
            at = (g // 4) * LANES
            value = jnp.zeros((NT, LANES), F32)
            for comp in range(6):
                value = jnp.where(
                    one_slot == (comp + g) % 6, results[comp][zb, :, at : at + LANES], value
                )
            out_ref[zb * G + g] = value


def link_times(links, vec):
    real, imag = [], []
    for a in range(3):
        row = [(links[3 * a + b], links[9 + 3 * a + b]) for b in range(3)]
        real.append(sum(row[b][0] * vec[b] - row[b][1] * vec[3 + b] for b in range(3)))
        imag.append(sum(row[b][0] * vec[3 + b] + row[b][1] * vec[b] for b in range(3)))
    return real + imag


def edge_kernel(links_ref, forward_ref, ready_ref, edge_ref):
    edge_ref[0:6] = forward_ref[:, 0]
    links = [links_ref[i, 0].astype(F32) for i in range(18)]
    after = [forward_ref[c, 1].astype(F32) for c in range(6)]
    for c, value in enumerate(link_times(links, after)):
        high, low = split_two(value)
        edge_ref[6 + c] = high
        edge_ref[12 + c] = low


def phases(group, depth_z, block_z, block_x, scale):
    row = iota((CROWS, LANES), 0)
    angle = ((group * block_z + row // block_x) * PMOM % depth_z).astype(F32)
    angle = angle * (2.0 * math.pi / depth_z)
    inside = row < block_z * block_x
    cos_z = jnp.where(inside, jnp.cos(angle) * scale, 0.0)[:, :1]
    sin_z = jnp.where(inside, jnp.sin(angle) * scale, 0.0)[:, :1]
    return cos_z, sin_z


def chain_kernel(
    depth_z,
    scale,
    block_z,
    block_x,
    table_ref,
    request_ref,
    links_ref,
    links_next_ref,
    forward_ref,
    forward_next_ref,
    chain_ref,
    corner_ref,
    picked_ref,
    link_rows,
    field_rows,
):
    place = lax.axis_index("zs")
    rows_y = links_ref.shape[3]
    zh = block_z + 1
    slot_lanes = zh * XH
    count = block_z * block_x
    no_plane = jnp.zeros((block_x, rows_y), F32)

    def fill_links(i, carry):
        for z in range(block_z):
            link_rows[i, block_x * z : block_x * (z + 1)] = links_ref[i, z].astype(F32)
            at = count + block_x * z
            last = z == block_z - 1
            plane = no_plane if last else links_next_ref[i, z].astype(F32)
            link_rows[i, at : at + block_x] = plane
        return carry

    def fill_field(i, carry):
        for z in range(block_z):
            field_rows[i, block_x * z : block_x * (z + 1)] = forward_ref[i, z].astype(F32)
            at = count + block_x * z
            field_rows[i, at : at + block_x] = forward_next_ref[i, z].astype(F32)
        return carry

    lax.fori_loop(0, 18, fill_links, 0)
    lax.fori_loop(0, 6, fill_field, 0)

    cos_z, sin_z = phases(place // G, depth_z, block_z, block_x, scale)
    total_rows = link_rows.shape[1]

    def step(length, carry):
        for at in range(0, rows_y, LANES):
            lanes = slice(at, at + LANES)
            vec = [
                pltpu.roll(field_rows[c, :, lanes], total_rows - block_x, 0) for c in range(6)
            ]
            for a in range(3):
                real = None
                imag = None
                for b in range(3):
                    link_real = link_rows[a * 3 + b, :, lanes]
                    link_imag = link_rows[9 + a * 3 + b, :, lanes]
                    term_real = link_real * vec[b] - link_imag * vec[3 + b]
                    term_imag = link_real * vec[3 + b] + link_imag * vec[b]
                    real = term_real if real is None else real + term_real
                    imag = term_imag if imag is None else imag + term_imag
                field_rows[a, :, lanes] = real
                field_rows[3 + a, :, lanes] = imag
                top_real, top_imag = real[:CROWS], imag[:CROWS]
                chain_ref[length, a * CROWS : (a + 1) * CROWS, lanes] = (
                    top_real * cos_z - top_imag * sin_z
                )
                chain_ref[length, (3 + a) * CROWS : (4 + a) * CROWS, lanes] = (
                    top_real * sin_z + top_imag * cos_z
                )
        return carry

    lax.fori_loop(0, LMAX, step, 0)

    shape = (6 * CROWS, LANES)
    row = iota(shape, 0)
    lane = iota(shape, 1)
    comp = row // CROWS
    z_step = lane % slot_lanes % zh - row % CROWS // block_x
    x_step = lane % slot_lanes // zh - row % block_x
    here = (lane // slot_lanes == (comp + place % G) % 6) & (row % CROWS < count)
    here = here & (x_step >= 0) & (x_step < 2) & (z_step >= 0) & (z_step < 2)
    table = jnp.broadcast_to(table_ref[0:1], shape)
    for y_step in range(2):
        corner = jnp.where(here, 4 * x_step + 2 * y_step + z_step, 0)
        weights = jnp.where(here, jnp.take_along_axis(table, corner, axis=1), 0.0)
        high, low = split_two(weights)
        corner_ref[0, y_step * 6 * CROWS : (y_step + 1) * 6 * CROWS] = high
        corner_ref[1, y_step * 6 * CROWS : (y_step + 1) * 6 * CROWS] = low

    request = request_ref[...]
    mine = request // LANES == place
    codes = (request % LANES).astype(F32)
    member = jnp.where(mine, 1.0, 0.0)
    below = jnp.where(iota((LANES, LANES), 0) < iota((LANES, LANES), 1), 1.0, 0.0)
    earlier = jnp.dot(member.astype(BF16), below.astype(BF16), preferred_element_type=F32)
    running = jnp.zeros((1, 1), F32)
    picked = jnp.zeros((8, LANES), F32)
    slots = iota((LANES, LANES), 0).astype(F32)
    head = iota((8, LANES), 0) == 0
    for i in range(member.shape[0]):
        key = jnp.where(member[i : i + 1] > 0.5, earlier[i : i + 1] + running, -1.0)
        hits = jnp.where(slots == key, 1.0, 0.0).astype(BF16)
        left = jnp.where(head, codes[i : i + 1], 1.0).astype(BF16)
        picked = picked + lax.dot_general(left, hits, NT_DIMS, preferred_element_type=F32)
        running = running + jnp.sum(member[i : i + 1], axis=1, keepdims=True)
    lane_of = picked[0:1].astype(jnp.int32) + iota((8, LANES), 0) % 2 * NT
    picked_ref[...] = jnp.where(picked[1:2] > 0.5, lane_of, -1)


def tail_kernel(
    depth_z, scale, block_z, block_x, links_ref, links_next_ref, edge_ref, corner_ref, extra_ref
):
    cos_z, sin_z = phases(lax.axis_index("zs") // G, depth_z, block_z, block_x, scale)
    extra_ref[...] = jnp.zeros_like(extra_ref)
    planes = edge_ref[...].astype(F32)
    near = [planes[c] for c in range(6)]
    far = [planes[6 + c] + planes[12 + c] for c in range(6)]
    vecs = [near, far]
    for z in range(2 * block_z - 1, block_z - 3, -1):
        ref = links_ref if z < block_z else links_next_ref
        links = [ref[i, z % block_z].astype(F32) for i in range(18)]
        vecs = [link_times(links, vec) for vec in vecs]
        if z < block_z:
            at = z * block_x
            cos_at, sin_at = cos_z[at : at + block_x], sin_z[at : at + block_x]
            for k, vec in enumerate(vecs):
                kept = k + block_z - 1 - z
                for a in range(3):
                    real, imag = vec[a], vec[3 + a]
                    first = a * CROWS + at
                    extra_ref[kept, first : first + block_x] = real * cos_at - imag * sin_at
                    first = (3 + a) * CROWS + at
                    extra_ref[kept, first : first + block_x] = real * sin_at + imag * cos_at
            vecs = vecs[:-1]


def meet_kernel(block_z, block_x, got_ref, corner_ref, chain_ref, extra_ref, seq_ref, table_ref):
    rows_y = got_ref.shape[0] * NT
    got = got_ref[...].reshape(rows_y, LANES)
    high, low = split_two(got)
    dot = functools.partial(
        lax.dot_general, dimension_numbers=NT_DIMS, preferred_element_type=F32
    )
    both = dot(corner_ref[0], high) + dot(corner_ref[0], low) + dot(corner_ref[1], high)
    size = 6 * CROWS
    seq = both[:size] + pltpu.roll(both[size:], rows_y - NT, 1)
    for comp in range(6):
        for z in range(block_z):
            at = comp * CROWS + z * block_x
            seq_ref[comp, z] = seq[at : at + block_x]
    turned = jnp.concatenate([-seq[3 * CROWS :], seq[: 3 * CROWS]], axis=0)
    sums = []
    for length in range(LMAX):
        chain = chain_ref[length]
        if length >= block_z:
            chain = chain + extra_ref[length - block_z]
        for field in (seq, turned):
            prod = field * chain
            part = prod[:8]
            for at in range(8, size, 8):
                part = part + prod[at : at + 8]
            narrow = part[:, :LANES]
            for at in range(LANES, rows_y, LANES):
                narrow = narrow + part[:, at : at + LANES]
            sums.append(jnp.sum(narrow, axis=0, keepdims=True))
    table = jnp.concatenate(sums, axis=0)
    for shift in (64, 32, 16, 8):
        table = table + pltpu.roll(table, shift, 1)
    mine = iota((2 * LMAX, LANES), 1) // NT == iota((2 * LMAX, LANES), 0)
    flat = jnp.sum(jnp.where(mine, table, 0.0), axis=0, keepdims=True)
    table_ref[...] = jnp.broadcast_to(flat, table_ref.shape)


def final_kernel(tables_ref, picked_ref, out_ref):
    total = jnp.sum(tables_ref[...], axis=0, keepdims=True)
    picked = picked_ref[...]
    value = jnp.take_along_axis(
        jnp.broadcast_to(total, picked.shape), jnp.maximum(picked, 0), axis=1
    )
    value = jnp.where(picked >= 0, value, 0.0)
    out_ref[...] = value[:2, : out_ref.shape[1]]


VMEM = pl.BlockSpec(memory_space=pltpu.VMEM)
SMEM = pl.BlockSpec(memory_space=pltpu.SMEM)


def cost(flops, moved):
    return pl.CostEstimate(flops=flops, bytes_accessed=moved, transcendentals=0)


PARAMS = pltpu.CompilerParams(vmem_limit_bytes=16 * 1024 * 1024)
WIDE_PARAMS = pltpu.CompilerParams(vmem_limit_bytes=60 * 1024 * 1024)


def shards(
    quark_up,
    quark_down,
    forward,
    gauge_links,
    corner_weight,
    corner_offset,
    lengths,
    separations,
    owner_map,
):
    devices = lax.axis_size("zs")
    block_z, block_x, rows_y = forward.shape[3:]
    cells = quark_up.shape[3]
    depth_z = cells // (block_x * G)
    scale = 1.0 / math.sqrt(cells * (rows_y // NT))
    links = gauge_links.reshape(18, block_z, block_x, rows_y)
    field = forward.reshape(6, block_z, block_x, rows_y)

    links_next = passed_along(links, "zs", -G)
    field_next = passed_along(field, "zs", -G)
    requests = (lengths.shape[0] // LANES, LANES)
    payload, request, table = pl.pallas_call(
        functools.partial(pack_kernel, block_z, block_x),
        out_shape=(
            jax.ShapeDtypeStruct((devices, NT, LANES), F32),
            jax.ShapeDtypeStruct(requests, jnp.int32),
            jax.ShapeDtypeStruct((8, LANES), F32),
        ),
        grid=(1,),
        in_specs=[SMEM] * 2
        + [pl.BlockSpec(quark_up.shape, lambda i: (0, 0, 0, 0))] * 2
        + [pl.BlockSpec(requests, lambda i: (0, 0))] * 3,
        out_specs=(
            pl.BlockSpec((devices, NT, LANES), lambda i: (0, 0, 0)),
            pl.BlockSpec(requests, lambda i: (0, 0)),
            pl.BlockSpec((8, LANES), lambda i: (0, 0)),
        ),
        compiler_params=WIDE_PARAMS,
        cost_estimate=cost(2_000_000_000, 400_000),
        name="pack",
    )(
        corner_weight,
        corner_offset.T,
        quark_up,
        quark_down,
        lengths.reshape(requests),
        separations.reshape(requests),
        owner_map.reshape(requests),
    )
    got = lax.all_to_all(payload, "zs", split_axis=0, concat_axis=0, tiled=True)

    past = LMAX - block_z
    edge = pl.pallas_call(
        edge_kernel,
        out_shape=jax.ShapeDtypeStruct((18, block_x, rows_y), BF16),
        in_specs=[VMEM] * 2 + [pl.BlockSpec(memory_space=pl.ANY)],
        out_specs=VMEM,
        compiler_params=PARAMS,
        cost_estimate=cost(50_000_000, 60_000),
        name="edge",
    )(links, field, links_next)
    edge_next = passed_along(edge, "zs", -2 * G)
    chain, corner, picked = pl.pallas_call(
        functools.partial(chain_kernel, depth_z, scale, block_z, block_x),
        out_shape=(
            jax.ShapeDtypeStruct((LMAX, 6 * CROWS, rows_y), F32),
            jax.ShapeDtypeStruct((2, 12 * CROWS, LANES), BF16),
            jax.ShapeDtypeStruct((8, LANES), jnp.int32),
        ),
        in_specs=[VMEM] * 6,
        out_specs=(VMEM,) * 3,
        scratch_shapes=[
            pltpu.VMEM((18, 2 * block_z * block_x, rows_y), F32),
            pltpu.VMEM((6, 2 * block_z * block_x, rows_y), F32),
        ],
        compiler_params=PARAMS,
        cost_estimate=cost(3_000_000_000, 200_000),
        name="chain",
    )(table, request, links, links_next, field, field_next)

    extra = pl.pallas_call(
        functools.partial(tail_kernel, depth_z, scale, block_z, block_x),
        out_shape=jax.ShapeDtypeStruct((past, 6 * CROWS, rows_y), F32),
        in_specs=[VMEM] * 3 + [pl.BlockSpec(memory_space=pl.ANY)],
        out_specs=VMEM,
        compiler_params=PARAMS,
        cost_estimate=cost(400_000_000, 200_000),
        name="tail",
    )(links, links_next, edge_next, corner)

    seq, partial = pl.pallas_call(
        functools.partial(meet_kernel, block_z, block_x),
        out_shape=(
            jax.ShapeDtypeStruct((6, block_z, block_x, rows_y), F32),
            jax.ShapeDtypeStruct((devices, LANES), F32),
        ),
        in_specs=[VMEM] * 4,
        out_specs=(VMEM, VMEM),
        compiler_params=PARAMS,
        cost_estimate=cost(2_000_000_000, 1_000_000),
        name="meet",
    )(got, corner, chain, extra)
    tables = lax.all_to_all(
        partial.reshape(devices, 1, LANES), "zs", split_axis=0, concat_axis=0, tiled=True
    ).reshape(devices, LANES)
    owned = pl.pallas_call(
        final_kernel,
        out_shape=jax.ShapeDtypeStruct((2, MOST), F32),
        in_specs=[VMEM] * 2,
        out_specs=VMEM,
        compiler_params=PARAMS,
        name="final",
    )(tables, picked)
    return (seq.reshape(2, 3, 1, block_z, block_x, rows_y), owned.T)


def solution(mesh):
    in_specs = (
        P(None, None, "zs", "grp"),
        P(None, None, "zs", "grp"),
        P(None, None, "zs", None, None, "grp"),
        P(None, None, None, "zs", None, None, "grp"),
        P(),
        P(),
        P("grp"),
        P("grp"),
        P("grp", None),
    )
    out_specs = (P(None, None, "zs", None, None, "grp"), P("zs", "grp"))
    return jax.shard_map(shards, mesh=mesh, in_specs=in_specs, out_specs=out_specs, check_vma=False)
```

```python
import functools
import math

import jax
import jax.numpy as jnp
from jax import lax
from jax.experimental import pallas as pl
from jax.experimental.pallas import tpu as pltpu
from jax.sharding import PartitionSpec as P

NT = 8
LMAX = 8
PMOM = 3
G = 8
MOST = 96
LANES = 128
XH = 3
CROWS = 16

F32 = jnp.float32
BF16 = jnp.bfloat16
NT_DIMS = (((1,), (1,)), ((), ()))


def passed_along(block, axis, distance):
    devices = range(lax.axis_size(axis))
    route = [((i - distance) % len(devices), i) for i in devices]
    return lax.ppermute(block, axis, route)


def split_two(value):
    high = value.astype(BF16)
    return high, (value - high.astype(F32)).astype(BF16)


def iota(shape, axis):
    return lax.broadcasted_iota(jnp.int32, shape, axis)


def pack_kernel(
    block_z,
    block_x,
    weight_ref,
    offset_ref,
    up_ref,
    down_ref,
    lengths_ref,
    separations_ref,
    owners_ref,
    out_ref,
    request_ref,
    table_ref,
):
    codes = lengths_ref[...] * (2 * NT) + separations_ref[...]
    request_ref[...] = owners_ref[...] * LANES + codes
    lane = iota((8, LANES), 1)
    table = jnp.zeros((8, LANES), F32)
    for k in range(8):
        corner = offset_ref[0, k] * 4 + offset_ref[1, k] * 2 + offset_ref[2, k]
        table = jnp.where(lane == corner, weight_ref[k], table)
    table_ref[...] = table
    zh = block_z + 1
    slot_lanes = zh * XH
    width_x = block_x * G
    cells = up_ref.shape[3]
    z_blocks = cells // (block_z * width_x)
    up = up_ref[...].astype(F32)
    down = down_ref[...].astype(F32)

    def cross(a, b, c):
        d, e = (c + 1) % 3, (c + 2) % 3
        return up[a, d] * down[b, e] - up[a, e] * down[b, d]

    planes = [cross(0, 0, c) - cross(1, 1, c) for c in range(3)]
    planes += [cross(0, 1, c) + cross(1, 0, c) for c in range(3)]
    lane = iota((1, 2 * LANES), 1)
    half = lane // LANES
    within = lane % LANES
    slot = within // slot_lanes
    cell = within % slot_lanes
    source_row = iota((LANES, 2 * LANES), 0)
    results = []
    for comp in range(6):
        turned = (slot + 12 - comp - 4 * half) % 6
        source = (cell % zh) * width_x + (block_x * (turned + 4 * half) + cell // zh) % width_x
        source = jnp.where((turned < 4) & (slot < 6), source, -1)
        pick = jnp.where(source_row == source, 1.0, 0.0).astype(BF16)
        wide = jnp.concatenate([planes[comp], planes[comp][:, :LANES]], axis=1)
        rows = []
        for zb in range(z_blocks):
            begin = zb * block_z * width_x
            part = wide[:, begin : begin + LANES]
            high = part.astype(BF16).astype(F32)
            rows += [high, part - high]
        left = jnp.concatenate(rows, axis=0).astype(BF16)
        got = jnp.dot(left, pick, preferred_element_type=F32)
        got = got.reshape(z_blocks, 2, NT, 2 * LANES)
        results.append(got[:, 0] + got[:, 1])
    one_slot = iota((NT, LANES), 1) // slot_lanes
    for zb in range(z_blocks):
        for g in range(G):
            at = (g // 4) * LANES
            value = jnp.zeros((NT, LANES), F32)
            for comp in range(6):
                value = jnp.where(
                    one_slot == (comp + g) % 6, results[comp][zb, :, at : at + LANES], value
                )
            out_ref[zb * G + g] = value


def link_times(links, vec):
    real, imag = [], []
    for a in range(3):
        row = [(links[3 * a + b], links[9 + 3 * a + b]) for b in range(3)]
        real.append(sum(row[b][0] * vec[b] - row[b][1] * vec[3 + b] for b in range(3)))
        imag.append(sum(row[b][0] * vec[3 + b] + row[b][1] * vec[b] for b in range(3)))
    return real + imag


def edge_kernel(links_ref, forward_ref, ready_ref, edge_ref):
    edge_ref[0:6] = forward_ref[:, 0]
    links = [links_ref[i, 0].astype(F32) for i in range(18)]
    after = [forward_ref[c, 1].astype(F32) for c in range(6)]
    for c, value in enumerate(link_times(links, after)):
        high, low = split_two(value)
        edge_ref[6 + c] = high
        edge_ref[12 + c] = low


def phases(group, depth_z, block_z, block_x, scale):
    row = iota((CROWS, LANES), 0)
    angle = ((group * block_z + row // block_x) * PMOM % depth_z).astype(F32)
    angle = angle * (2.0 * math.pi / depth_z)
    inside = row < block_z * block_x
    cos_z = jnp.where(inside, jnp.cos(angle) * scale, 0.0)[:, :1]
    sin_z = jnp.where(inside, jnp.sin(angle) * scale, 0.0)[:, :1]
    return cos_z, sin_z


def chain_kernel(
    depth_z,
    scale,
    block_z,
    block_x,
    table_ref,
    request_ref,
    links_ref,
    links_next_ref,
    forward_ref,
    forward_next_ref,
    chain_ref,
    corner_ref,
    picked_ref,
    link_rows,
    field_rows,
):
    place = lax.axis_index("zs")
    rows_y = links_ref.shape[3]
    zh = block_z + 1
    slot_lanes = zh * XH
    count = block_z * block_x
    no_plane = jnp.zeros((block_x, rows_y), F32)

    def fill_links(i, carry):
        for z in range(block_z):
            link_rows[i, block_x * z : block_x * (z + 1)] = links_ref[i, z].astype(F32)
            at = count + block_x * z
            last = z == block_z - 1
            plane = no_plane if last else links_next_ref[i, z].astype(F32)
            link_rows[i, at : at + block_x] = plane
        return carry

    def fill_field(i, carry):
        for z in range(block_z):
            field_rows[i, block_x * z : block_x * (z + 1)] = forward_ref[i, z].astype(F32)
            at = count + block_x * z
            field_rows[i, at : at + block_x] = forward_next_ref[i, z].astype(F32)
        return carry

    lax.fori_loop(0, 18, fill_links, 0)
    lax.fori_loop(0, 6, fill_field, 0)

    cos_z, sin_z = phases(place // G, depth_z, block_z, block_x, scale)
    total_rows = link_rows.shape[1]

    def step(length, carry):
        for at in range(0, rows_y, LANES):
            lanes = slice(at, at + LANES)
            vec = [
                pltpu.roll(field_rows[c, :, lanes], total_rows - block_x, 0) for c in range(6)
            ]
            for a in range(3):
                real = None
                imag = None
                for b in range(3):
                    link_real = link_rows[a * 3 + b, :, lanes]
                    link_imag = link_rows[9 + a * 3 + b, :, lanes]
                    term_real = link_real * vec[b] - link_imag * vec[3 + b]
                    term_imag = link_real * vec[3 + b] + link_imag * vec[b]
                    real = term_real if real is None else real + term_real
                    imag = term_imag if imag is None else imag + term_imag
                field_rows[a, :, lanes] = real
                field_rows[3 + a, :, lanes] = imag
                top_real, top_imag = real[:CROWS], imag[:CROWS]
                chain_ref[length, a * CROWS : (a + 1) * CROWS, lanes] = (
                    top_real * cos_z - top_imag * sin_z
                )
                chain_ref[length, (3 + a) * CROWS : (4 + a) * CROWS, lanes] = (
                    top_real * sin_z + top_imag * cos_z
                )
        return carry

    lax.fori_loop(0, LMAX, step, 0)

    shape = (6 * CROWS, LANES)
    row = iota(shape, 0)
    lane = iota(shape, 1)
    comp = row // CROWS
    z_step = lane % slot_lanes % zh - row % CROWS // block_x
    x_step = lane % slot_lanes // zh - row % block_x
    here = (lane // slot_lanes == (comp + place % G) % 6) & (row % CROWS < count)
    here = here & (x_step >= 0) & (x_step < 2) & (z_step >= 0) & (z_step < 2)
    table = jnp.broadcast_to(table_ref[0:1], shape)
    for y_step in range(2):
        corner = jnp.where(here, 4 * x_step + 2 * y_step + z_step, 0)
        weights = jnp.where(here, jnp.take_along_axis(table, corner, axis=1), 0.0)
        high, low = split_two(weights)
        corner_ref[0, y_step * 6 * CROWS : (y_step + 1) * 6 * CROWS] = high
        corner_ref[1, y_step * 6 * CROWS : (y_step + 1) * 6 * CROWS] = low

    request = request_ref[...]
    mine = request // LANES == place
    codes = (request % LANES).astype(F32)
    member = jnp.where(mine, 1.0, 0.0)
    below = jnp.where(iota((LANES, LANES), 0) < iota((LANES, LANES), 1), 1.0, 0.0)
    earlier = jnp.dot(member.astype(BF16), below.astype(BF16), preferred_element_type=F32)
    running = jnp.zeros((1, 1), F32)
    picked = jnp.zeros((8, LANES), F32)
    slots = iota((LANES, LANES), 0).astype(F32)
    head = iota((8, LANES), 0) == 0
    for i in range(member.shape[0]):
        key = jnp.where(member[i : i + 1] > 0.5, earlier[i : i + 1] + running, -1.0)
        hits = jnp.where(slots == key, 1.0, 0.0).astype(BF16)
        left = jnp.where(head, codes[i : i + 1], 1.0).astype(BF16)
        picked = picked + lax.dot_general(left, hits, NT_DIMS, preferred_element_type=F32)
        running = running + jnp.sum(member[i : i + 1], axis=1, keepdims=True)
    lane_of = picked[0:1].astype(jnp.int32) + iota((8, LANES), 0) % 2 * NT
    picked_ref[...] = jnp.where(picked[1:2] > 0.5, lane_of, -1)


def tail_kernel(
    depth_z, scale, block_z, block_x, links_ref, links_next_ref, edge_ref, corner_ref, extra_ref
):
    cos_z, sin_z = phases(lax.axis_index("zs") // G, depth_z, block_z, block_x, scale)
    extra_ref[...] = jnp.zeros_like(extra_ref)
    planes = edge_ref[...].astype(F32)
    near = [planes[c] for c in range(6)]
    far = [planes[6 + c] + planes[12 + c] for c in range(6)]
    vecs = [near, far]
    for z in range(2 * block_z - 1, block_z - 3, -1):
        ref = links_ref if z < block_z else links_next_ref
        links = [ref[i, z % block_z].astype(F32) for i in range(18)]
        vecs = [link_times(links, vec) for vec in vecs]
        if z < block_z:
            at = z * block_x
            cos_at, sin_at = cos_z[at : at + block_x], sin_z[at : at + block_x]
            for k, vec in enumerate(vecs):
                kept = k + block_z - 1 - z
                for a in range(3):
                    real, imag = vec[a], vec[3 + a]
                    first = a * CROWS + at
                    extra_ref[kept, first : first + block_x] = real * cos_at - imag * sin_at
                    first = (3 + a) * CROWS + at
                    extra_ref[kept, first : first + block_x] = real * sin_at + imag * cos_at
            vecs = vecs[:-1]


def meet_kernel(
    block_z,
    block_x,
    got_ref,
    corner_ref,
    chain_ref,
    extra_ref,
    seq_ref,
    table_ref,
    seq_rows,
    seq_done,
):
    rows_y = got_ref.shape[0] * NT
    got = got_ref[...].reshape(rows_y, LANES)
    high, low = split_two(got)
    dot = functools.partial(
        lax.dot_general, dimension_numbers=NT_DIMS, preferred_element_type=F32
    )
    both = dot(corner_ref[0], high) + dot(corner_ref[0], low) + dot(corner_ref[1], high)
    size = 6 * CROWS
    seq = both[:size] + pltpu.roll(both[size:], rows_y - NT, 1)
    for comp in range(6):
        for z in range(block_z):
            at = comp * CROWS + z * block_x
            seq_rows[comp, z] = seq[at : at + block_x]
    copy = pltpu.make_async_copy(seq_rows, seq_ref, seq_done)
    copy.start()
    turned = jnp.concatenate([-seq[3 * CROWS :], seq[: 3 * CROWS]], axis=0)
    sums = []
    for length in range(LMAX):
        chain = chain_ref[length]
        if length >= block_z:
            chain = chain + extra_ref[length - block_z]
        for field in (seq, turned):
            prod = field * chain
            part = prod[:8]
            for at in range(8, size, 8):
                part = part + prod[at : at + 8]
            narrow = part[:, :LANES]
            for at in range(LANES, rows_y, LANES):
                narrow = narrow + part[:, at : at + LANES]
            sums.append(jnp.sum(narrow, axis=0, keepdims=True))
    table = jnp.concatenate(sums, axis=0)
    for shift in (64, 32, 16, 8):
        table = table + pltpu.roll(table, shift, 1)
    mine = iota((2 * LMAX, LANES), 1) // NT == iota((2 * LMAX, LANES), 0)
    flat = jnp.sum(jnp.where(mine, table, 0.0), axis=0, keepdims=True)
    table_ref[...] = flat
    copy.wait()


def sum_kernel(mine_ref, other_ref, out_ref):
    out_ref[...] = mine_ref[...] + other_ref[...]


def final_kernel(mine_ref, other_ref, picked_ref, out_ref):
    total = mine_ref[...] + other_ref[...]
    picked = picked_ref[...]
    value = jnp.take_along_axis(
        jnp.broadcast_to(total, picked.shape), jnp.maximum(picked, 0), axis=1
    )
    value = jnp.where(picked >= 0, value, 0.0)
    out_ref[...] = value[:2, : out_ref.shape[1]]


VMEM = pl.BlockSpec(memory_space=pltpu.VMEM)
SMEM = pl.BlockSpec(memory_space=pltpu.SMEM)


def cost(flops, moved):
    return pl.CostEstimate(flops=flops, bytes_accessed=moved, transcendentals=0)


PARAMS = pltpu.CompilerParams(vmem_limit_bytes=16 * 1024 * 1024)
WIDE_PARAMS = pltpu.CompilerParams(vmem_limit_bytes=60 * 1024 * 1024)


def shards(
    quark_up,
    quark_down,
    forward,
    gauge_links,
    corner_weight,
    corner_offset,
    lengths,
    separations,
    owner_map,
):
    devices = lax.axis_size("zs")
    block_z, block_x, rows_y = forward.shape[3:]
    cells = quark_up.shape[3]
    depth_z = cells // (block_x * G)
    scale = 1.0 / math.sqrt(cells * (rows_y // NT))
    links = gauge_links.reshape(18, block_z, block_x, rows_y)
    field = forward.reshape(6, block_z, block_x, rows_y)

    links_next = passed_along(links, "zs", -G)
    field_next = passed_along(field, "zs", -G)
    requests = (lengths.shape[0] // LANES, LANES)
    payload, request, table = pl.pallas_call(
        functools.partial(pack_kernel, block_z, block_x),
        out_shape=(
            jax.ShapeDtypeStruct((devices, NT, LANES), F32),
            jax.ShapeDtypeStruct(requests, jnp.int32),
            jax.ShapeDtypeStruct((8, LANES), F32),
        ),
        grid=(1,),
        in_specs=[SMEM] * 2
        + [pl.BlockSpec(quark_up.shape, lambda i: (0, 0, 0, 0))] * 2
        + [pl.BlockSpec(requests, lambda i: (0, 0))] * 3,
        out_specs=(
            pl.BlockSpec((devices, NT, LANES), lambda i: (0, 0, 0)),
            pl.BlockSpec(requests, lambda i: (0, 0)),
            pl.BlockSpec((8, LANES), lambda i: (0, 0)),
        ),
        compiler_params=WIDE_PARAMS,
        cost_estimate=cost(2_000_000_000, 400_000),
        name="pack",
    )(
        corner_weight,
        corner_offset.T,
        quark_up,
        quark_down,
        lengths.reshape(requests),
        separations.reshape(requests),
        owner_map.reshape(requests),
    )
    got = lax.all_to_all(payload, "zs", split_axis=0, concat_axis=0, tiled=True)

    past = LMAX - block_z
    edge = pl.pallas_call(
        edge_kernel,
        out_shape=jax.ShapeDtypeStruct((18, block_x, rows_y), BF16),
        in_specs=[VMEM] * 2 + [pl.BlockSpec(memory_space=pl.ANY)],
        out_specs=VMEM,
        compiler_params=PARAMS,
        cost_estimate=cost(50_000_000, 60_000),
        name="edge",
    )(links, field, links_next)
    edge_next = passed_along(edge, "zs", -2 * G)
    chain, corner, picked = pl.pallas_call(
        functools.partial(chain_kernel, depth_z, scale, block_z, block_x),
        out_shape=(
            jax.ShapeDtypeStruct((LMAX, 6 * CROWS, rows_y), F32),
            jax.ShapeDtypeStruct((2, 12 * CROWS, LANES), BF16),
            jax.ShapeDtypeStruct((8, LANES), jnp.int32),
        ),
        in_specs=[VMEM] * 6,
        out_specs=(VMEM,) * 3,
        scratch_shapes=[
            pltpu.VMEM((18, 2 * block_z * block_x, rows_y), F32),
            pltpu.VMEM((6, 2 * block_z * block_x, rows_y), F32),
        ],
        compiler_params=PARAMS,
        cost_estimate=cost(3_000_000_000, 200_000),
        name="chain",
    )(table, request, links, links_next, field, field_next)

    extra = pl.pallas_call(
        functools.partial(tail_kernel, depth_z, scale, block_z, block_x),
        out_shape=jax.ShapeDtypeStruct((past, 6 * CROWS, rows_y), F32),
        in_specs=[VMEM] * 3 + [pl.BlockSpec(memory_space=pl.ANY)],
        out_specs=VMEM,
        compiler_params=PARAMS,
        cost_estimate=cost(400_000_000, 200_000),
        name="tail",
    )(links, links_next, edge_next, corner)

    seq, partial = pl.pallas_call(
        functools.partial(meet_kernel, block_z, block_x),
        out_shape=(
            jax.ShapeDtypeStruct((6, block_z, block_x, rows_y), F32),
            jax.ShapeDtypeStruct((1, LANES), F32),
        ),
        in_specs=[VMEM] * 4,
        out_specs=(pl.BlockSpec(memory_space=pl.ANY), VMEM),
        scratch_shapes=[
            pltpu.VMEM((6, block_z, block_x, rows_y), F32),
            pltpu.SemaphoreType.DMA,
        ],
        compiler_params=PARAMS,
        cost_estimate=cost(2_000_000_000, 1_000_000),
        name="meet",
    )(got, corner, chain, extra)
    bit = 1
    while bit < devices:
        other = lax.ppermute(partial, "zs", [(i, i ^ bit) for i in range(devices)])
        bit *= 2
        if bit < devices:
            partial = pl.pallas_call(
                sum_kernel,
                out_shape=jax.ShapeDtypeStruct((1, LANES), F32),
                in_specs=[VMEM] * 2,
                out_specs=VMEM,
                compiler_params=PARAMS,
                name="sum",
            )(partial, other)
    owned = pl.pallas_call(
        final_kernel,
        out_shape=jax.ShapeDtypeStruct((2, MOST), F32),
        in_specs=[VMEM] * 3,
        out_specs=VMEM,
        compiler_params=PARAMS,
        name="final",
    )(partial, other, picked)
    return (seq.reshape(2, 3, 1, block_z, block_x, rows_y), owned.T)


def solution(mesh):
    in_specs = (
        P(None, None, "zs", "grp"),
        P(None, None, "zs", "grp"),
        P(None, None, "zs", None, None, "grp"),
        P(None, None, None, "zs", None, None, "grp"),
        P(),
        P(),
        P("grp"),
        P("grp"),
        P("grp", None),
    )
    out_specs = (P(None, None, "zs", None, None, "grp"), P("zs", "grp"))
    return jax.shard_map(shards, mesh=mesh, in_specs=in_specs, out_specs=out_specs, check_vma=False)
```

```python
import functools
import math

import jax
import jax.numpy as jnp
from jax import lax
from jax.experimental import pallas as pl
from jax.experimental.pallas import tpu as pltpu
from jax.sharding import PartitionSpec as P

NT = 8
LMAX = 8
PMOM = 3
G = 8
MOST = 96
LANES = 128
XH = 3
CROWS = 16

F32 = jnp.float32
BF16 = jnp.bfloat16
NT_DIMS = (((1,), (1,)), ((), ()))


def passed_along(block, axis, distance):
    devices = range(lax.axis_size(axis))
    route = [((i - distance) % len(devices), i) for i in devices]
    return lax.ppermute(block, axis, route)


def split_two(value):
    high = value.astype(BF16)
    return high, (value - high.astype(F32)).astype(BF16)


def iota(shape, axis):
    return lax.broadcasted_iota(jnp.int32, shape, axis)


def pack_kernel(
    block_z,
    block_x,
    weight_ref,
    offset_ref,
    up_ref,
    down_ref,
    lengths_ref,
    separations_ref,
    owners_ref,
    out_ref,
    request_ref,
    table_ref,
):
    codes = lengths_ref[...] * (2 * NT) + separations_ref[...]
    request_ref[...] = owners_ref[...] * LANES + codes
    lane = iota((8, LANES), 1)
    table = jnp.zeros((8, LANES), F32)
    for k in range(8):
        corner = offset_ref[0, k] * 4 + offset_ref[1, k] * 2 + offset_ref[2, k]
        table = jnp.where(lane == corner, weight_ref[k], table)
    table_ref[...] = table
    zh = block_z + 1
    slot_lanes = zh * XH
    width_x = block_x * G
    cells = up_ref.shape[3]
    z_blocks = cells // (block_z * width_x)
    up = up_ref[...].astype(F32)
    down = down_ref[...].astype(F32)

    def cross(a, b, c):
        d, e = (c + 1) % 3, (c + 2) % 3
        return up[a, d] * down[b, e] - up[a, e] * down[b, d]

    planes = [cross(0, 0, c) - cross(1, 1, c) for c in range(3)]
    planes += [cross(0, 1, c) + cross(1, 0, c) for c in range(3)]
    lane = iota((1, 2 * LANES), 1)
    half = lane // LANES
    within = lane % LANES
    slot = within // slot_lanes
    cell = within % slot_lanes
    source_row = iota((LANES, 2 * LANES), 0)
    results = []
    for comp in range(6):
        turned = (slot + 12 - comp - 4 * half) % 6
        source = (cell % zh) * width_x + (block_x * (turned + 4 * half) + cell // zh) % width_x
        source = jnp.where((turned < 4) & (slot < 6), source, -1)
        pick = jnp.where(source_row == source, 1.0, 0.0).astype(BF16)
        wide = jnp.concatenate([planes[comp], planes[comp][:, :LANES]], axis=1)
        rows = []
        for zb in range(z_blocks):
            begin = zb * block_z * width_x
            part = wide[:, begin : begin + LANES]
            high = part.astype(BF16).astype(F32)
            rows += [high, part - high]
        left = jnp.concatenate(rows, axis=0).astype(BF16)
        got = jnp.dot(left, pick, preferred_element_type=F32)
        got = got.reshape(z_blocks, 2, NT, 2 * LANES)
        results.append(got[:, 0] + got[:, 1])
    one_slot = iota((NT, LANES), 1) // slot_lanes
    for zb in range(z_blocks):
        for g in range(G):
            at = (g // 4) * LANES
            value = jnp.zeros((NT, LANES), F32)
            for comp in range(6):
                value = jnp.where(
                    one_slot == (comp + g) % 6, results[comp][zb, :, at : at + LANES], value
                )
            out_ref[zb * G + g] = value


def link_times(links, vec):
    real, imag = [], []
    for a in range(3):
        row = [(links[3 * a + b], links[9 + 3 * a + b]) for b in range(3)]
        real.append(sum(row[b][0] * vec[b] - row[b][1] * vec[3 + b] for b in range(3)))
        imag.append(sum(row[b][0] * vec[3 + b] + row[b][1] * vec[b] for b in range(3)))
    return real + imag


def edge_kernel(links_ref, forward_ref, ready_ref, edge_ref):
    edge_ref[0:6] = forward_ref[:, 0]
    links = [links_ref[i, 0].astype(F32) for i in range(18)]
    after = [forward_ref[c, 1].astype(F32) for c in range(6)]
    for c, value in enumerate(link_times(links, after)):
        high, low = split_two(value)
        edge_ref[6 + c] = high
        edge_ref[12 + c] = low


def phases(group, depth_z, block_z, block_x, scale):
    row = iota((CROWS, LANES), 0)
    angle = ((group * block_z + row // block_x) * PMOM % depth_z).astype(F32)
    angle = angle * (2.0 * math.pi / depth_z)
    inside = row < block_z * block_x
    cos_z = jnp.where(inside, jnp.cos(angle) * scale, 0.0)[:, :1]
    sin_z = jnp.where(inside, jnp.sin(angle) * scale, 0.0)[:, :1]
    return cos_z, sin_z


def chain_kernel(
    depth_z,
    scale,
    block_z,
    block_x,
    table_ref,
    request_ref,
    links_ref,
    links_next_ref,
    forward_ref,
    forward_next_ref,
    chain_ref,
    corner_ref,
    picked_ref,
    link_rows,
    field_rows,
):
    place = lax.axis_index("zs")
    rows_y = links_ref.shape[3]
    zh = block_z + 1
    slot_lanes = zh * XH
    count = block_z * block_x
    no_plane = jnp.zeros((block_x, rows_y), F32)

    def fill_links(i, carry):
        for z in range(block_z):
            link_rows[i, block_x * z : block_x * (z + 1)] = links_ref[i, z].astype(F32)
            at = count + block_x * z
            last = z == block_z - 1
            plane = no_plane if last else links_next_ref[i, z].astype(F32)
            link_rows[i, at : at + block_x] = plane
        return carry

    def fill_field(i, carry):
        for z in range(block_z):
            field_rows[i, block_x * z : block_x * (z + 1)] = forward_ref[i, z].astype(F32)
            at = count + block_x * z
            field_rows[i, at : at + block_x] = forward_next_ref[i, z].astype(F32)
        return carry

    lax.fori_loop(0, 18, fill_links, 0)
    lax.fori_loop(0, 6, fill_field, 0)

    cos_z, sin_z = phases(place // G, depth_z, block_z, block_x, scale)
    total_rows = link_rows.shape[1]

    def step(length, carry):
        for at in range(0, rows_y, LANES):
            lanes = slice(at, at + LANES)
            vec = [
                pltpu.roll(field_rows[c, :, lanes], total_rows - block_x, 0) for c in range(6)
            ]
            for a in range(3):
                real = None
                imag = None
                for b in range(3):
                    link_real = link_rows[a * 3 + b, :, lanes]
                    link_imag = link_rows[9 + a * 3 + b, :, lanes]
                    term_real = link_real * vec[b] - link_imag * vec[3 + b]
                    term_imag = link_real * vec[3 + b] + link_imag * vec[b]
                    real = term_real if real is None else real + term_real
                    imag = term_imag if imag is None else imag + term_imag
                field_rows[a, :, lanes] = real
                field_rows[3 + a, :, lanes] = imag
                top_real, top_imag = real[:CROWS], imag[:CROWS]
                chain_ref[length, a * CROWS : (a + 1) * CROWS, lanes] = (
                    top_real * cos_z - top_imag * sin_z
                )
                chain_ref[length, (3 + a) * CROWS : (4 + a) * CROWS, lanes] = (
                    top_real * sin_z + top_imag * cos_z
                )
        return carry

    lax.fori_loop(0, LMAX, step, 0)

    shape = (6 * CROWS, LANES)
    row = iota(shape, 0)
    lane = iota(shape, 1)
    comp = row // CROWS
    z_step = lane % slot_lanes % zh - row % CROWS // block_x
    x_step = lane % slot_lanes // zh - row % block_x
    here = (lane // slot_lanes == (comp + place % G) % 6) & (row % CROWS < count)
    here = here & (x_step >= 0) & (x_step < 2) & (z_step >= 0) & (z_step < 2)
    table = jnp.broadcast_to(table_ref[0:1], shape)
    for y_step in range(2):
        corner = jnp.where(here, 4 * x_step + 2 * y_step + z_step, 0)
        weights = jnp.where(here, jnp.take_along_axis(table, corner, axis=1), 0.0)
        high, low = split_two(weights)
        corner_ref[0, y_step * 6 * CROWS : (y_step + 1) * 6 * CROWS] = high
        corner_ref[1, y_step * 6 * CROWS : (y_step + 1) * 6 * CROWS] = low

    request = request_ref[...]
    mine = request // LANES == place
    codes = (request % LANES).astype(F32)
    member = jnp.where(mine, 1.0, 0.0)
    below = jnp.where(iota((LANES, LANES), 0) < iota((LANES, LANES), 1), 1.0, 0.0)
    earlier = jnp.dot(member.astype(BF16), below.astype(BF16), preferred_element_type=F32)
    running = jnp.zeros((1, 1), F32)
    picked = jnp.zeros((8, LANES), F32)
    slots = iota((LANES, LANES), 0).astype(F32)
    head = iota((8, LANES), 0) == 0
    for i in range(member.shape[0]):
        key = jnp.where(member[i : i + 1] > 0.5, earlier[i : i + 1] + running, -1.0)
        hits = jnp.where(slots == key, 1.0, 0.0).astype(BF16)
        left = jnp.where(head, codes[i : i + 1], 1.0).astype(BF16)
        picked = picked + lax.dot_general(left, hits, NT_DIMS, preferred_element_type=F32)
        running = running + jnp.sum(member[i : i + 1], axis=1, keepdims=True)
    lane_of = picked[0:1].astype(jnp.int32) + iota((8, LANES), 0) % 2 * NT
    picked_ref[...] = jnp.where(picked[1:2] > 0.5, lane_of, -1)


def tail_kernel(
    depth_z, scale, block_z, block_x, links_ref, links_next_ref, edge_ref, corner_ref, extra_ref
):
    cos_z, sin_z = phases(lax.axis_index("zs") // G, depth_z, block_z, block_x, scale)
    extra_ref[...] = jnp.zeros_like(extra_ref)
    planes = edge_ref[...].astype(F32)
    near = [planes[c] for c in range(6)]
    far = [planes[6 + c] + planes[12 + c] for c in range(6)]
    vecs = [near, far]
    for z in range(2 * block_z - 1, block_z - 3, -1):
        ref = links_ref if z < block_z else links_next_ref
        links = [ref[i, z % block_z].astype(F32) for i in range(18)]
        vecs = [link_times(links, vec) for vec in vecs]
        if z < block_z:
            at = z * block_x
            cos_at, sin_at = cos_z[at : at + block_x], sin_z[at : at + block_x]
            for k, vec in enumerate(vecs):
                kept = k + block_z - 1 - z
                for a in range(3):
                    real, imag = vec[a], vec[3 + a]
                    first = a * CROWS + at
                    extra_ref[kept, first : first + block_x] = real * cos_at - imag * sin_at
                    first = (3 + a) * CROWS + at
                    extra_ref[kept, first : first + block_x] = real * sin_at + imag * cos_at
            vecs = vecs[:-1]


def meet_kernel(block_z, block_x, got_ref, corner_ref, chain_ref, extra_ref, seq_ref, table_ref):
    rows_y = got_ref.shape[0] * NT
    got = got_ref[...].reshape(rows_y, LANES)
    high, low = split_two(got)
    dot = functools.partial(
        lax.dot_general, dimension_numbers=NT_DIMS, preferred_element_type=F32
    )
    both = dot(corner_ref[0], high) + dot(corner_ref[0], low) + dot(corner_ref[1], high)
    size = 6 * CROWS
    seq = both[:size] + pltpu.roll(both[size:], rows_y - NT, 1)
    seq_ref[...] = seq
    turned = jnp.concatenate([-seq[3 * CROWS :], seq[: 3 * CROWS]], axis=0)
    sums = []
    for length in range(LMAX):
        chain = chain_ref[length]
        if length >= block_z:
            chain = chain + extra_ref[length - block_z]
        for field in (seq, turned):
            prod = field * chain
            part = prod[:8]
            for at in range(8, size, 8):
                part = part + prod[at : at + 8]
            narrow = part[:, :LANES]
            for at in range(LANES, rows_y, LANES):
                narrow = narrow + part[:, at : at + LANES]
            sums.append(jnp.sum(narrow, axis=0, keepdims=True))
    table = jnp.concatenate(sums, axis=0)
    for shift in (64, 32, 16, 8):
        table = table + pltpu.roll(table, shift, 1)
    mine = iota((2 * LMAX, LANES), 1) // NT == iota((2 * LMAX, LANES), 0)
    flat = jnp.sum(jnp.where(mine, table, 0.0), axis=0, keepdims=True)
    table_ref[...] = jnp.broadcast_to(flat, table_ref.shape)


def store_kernel(rows_ref, seq_ref):
    block_z, block_x = seq_ref.shape[1:3]
    for comp in range(6):
        for z in range(block_z):
            at = comp * CROWS + z * block_x
            seq_ref[comp, z] = rows_ref[at : at + block_x]


def final_kernel(tables_ref, picked_ref, out_ref):
    total = jnp.sum(tables_ref[...], axis=0, keepdims=True)
    picked = picked_ref[...]
    value = jnp.take_along_axis(
        jnp.broadcast_to(total, picked.shape), jnp.maximum(picked, 0), axis=1
    )
    value = jnp.where(picked >= 0, value, 0.0)
    out_ref[...] = value[:2, : out_ref.shape[1]]


VMEM = pl.BlockSpec(memory_space=pltpu.VMEM)
SMEM = pl.BlockSpec(memory_space=pltpu.SMEM)


def cost(flops, moved):
    return pl.CostEstimate(flops=flops, bytes_accessed=moved, transcendentals=0)


PARAMS = pltpu.CompilerParams(vmem_limit_bytes=16 * 1024 * 1024)
WIDE_PARAMS = pltpu.CompilerParams(vmem_limit_bytes=60 * 1024 * 1024)


def shards(
    quark_up,
    quark_down,
    forward,
    gauge_links,
    corner_weight,
    corner_offset,
    lengths,
    separations,
    owner_map,
):
    devices = lax.axis_size("zs")
    block_z, block_x, rows_y = forward.shape[3:]
    cells = quark_up.shape[3]
    depth_z = cells // (block_x * G)
    scale = 1.0 / math.sqrt(cells * (rows_y // NT))
    links = gauge_links.reshape(18, block_z, block_x, rows_y)
    field = forward.reshape(6, block_z, block_x, rows_y)

    links_next = passed_along(links, "zs", -G)
    field_next = passed_along(field, "zs", -G)
    requests = (lengths.shape[0] // LANES, LANES)
    payload, request, table = pl.pallas_call(
        functools.partial(pack_kernel, block_z, block_x),
        out_shape=(
            jax.ShapeDtypeStruct((devices, NT, LANES), F32),
            jax.ShapeDtypeStruct(requests, jnp.int32),
            jax.ShapeDtypeStruct((8, LANES), F32),
        ),
        grid=(1,),
        in_specs=[SMEM] * 2
        + [pl.BlockSpec(quark_up.shape, lambda i: (0, 0, 0, 0))] * 2
        + [pl.BlockSpec(requests, lambda i: (0, 0))] * 3,
        out_specs=(
            pl.BlockSpec((devices, NT, LANES), lambda i: (0, 0, 0)),
            pl.BlockSpec(requests, lambda i: (0, 0)),
            pl.BlockSpec((8, LANES), lambda i: (0, 0)),
        ),
        compiler_params=WIDE_PARAMS,
        cost_estimate=cost(2_000_000_000, 400_000),
        name="pack",
    )(
        corner_weight,
        corner_offset.T,
        quark_up,
        quark_down,
        lengths.reshape(requests),
        separations.reshape(requests),
        owner_map.reshape(requests),
    )
    got = lax.all_to_all(payload, "zs", split_axis=0, concat_axis=0, tiled=True)

    past = LMAX - block_z
    edge = pl.pallas_call(
        edge_kernel,
        out_shape=jax.ShapeDtypeStruct((18, block_x, rows_y), BF16),
        in_specs=[VMEM] * 2 + [pl.BlockSpec(memory_space=pl.ANY)],
        out_specs=VMEM,
        compiler_params=PARAMS,
        cost_estimate=cost(50_000_000, 60_000),
        name="edge",
    )(links, field, links_next)
    edge_next = passed_along(edge, "zs", -2 * G)
    chain, corner, picked = pl.pallas_call(
        functools.partial(chain_kernel, depth_z, scale, block_z, block_x),
        out_shape=(
            jax.ShapeDtypeStruct((LMAX, 6 * CROWS, rows_y), F32),
            jax.ShapeDtypeStruct((2, 12 * CROWS, LANES), BF16),
            jax.ShapeDtypeStruct((8, LANES), jnp.int32),
        ),
        in_specs=[VMEM] * 6,
        out_specs=(VMEM,) * 3,
        scratch_shapes=[
            pltpu.VMEM((18, 2 * block_z * block_x, rows_y), F32),
            pltpu.VMEM((6, 2 * block_z * block_x, rows_y), F32),
        ],
        compiler_params=PARAMS,
        cost_estimate=cost(3_000_000_000, 200_000),
        name="chain",
    )(table, request, links, links_next, field, field_next)

    extra = pl.pallas_call(
        functools.partial(tail_kernel, depth_z, scale, block_z, block_x),
        out_shape=jax.ShapeDtypeStruct((past, 6 * CROWS, rows_y), F32),
        in_specs=[VMEM] * 3 + [pl.BlockSpec(memory_space=pl.ANY)],
        out_specs=VMEM,
        compiler_params=PARAMS,
        cost_estimate=cost(400_000_000, 200_000),
        name="tail",
    )(links, links_next, edge_next, corner)

    seq_rows, partial = pl.pallas_call(
        functools.partial(meet_kernel, block_z, block_x),
        out_shape=(
            jax.ShapeDtypeStruct((6 * CROWS, rows_y), F32),
            jax.ShapeDtypeStruct((devices, LANES), F32),
        ),
        in_specs=[VMEM] * 4,
        out_specs=(VMEM, VMEM),
        compiler_params=PARAMS,
        cost_estimate=cost(2_000_000_000, 1_000_000),
        name="meet",
    )(got, corner, chain, extra)
    tables = lax.all_to_all(
        partial.reshape(devices, 1, LANES), "zs", split_axis=0, concat_axis=0, tiled=True
    ).reshape(devices, LANES)
    seq = pl.pallas_call(
        store_kernel,
        out_shape=jax.ShapeDtypeStruct((6, block_z, block_x, rows_y), F32),
        in_specs=[VMEM],
        out_specs=VMEM,
        compiler_params=PARAMS,
        cost_estimate=cost(2_000_000_000, 200_000),
        name="store",
    )(seq_rows)
    owned = pl.pallas_call(
        final_kernel,
        out_shape=jax.ShapeDtypeStruct((2, MOST), F32),
        in_specs=[VMEM] * 2,
        out_specs=VMEM,
        compiler_params=PARAMS,
        name="final",
    )(tables, picked)
    return (seq.reshape(2, 3, 1, block_z, block_x, rows_y), owned.T)


def solution(mesh):
    in_specs = (
        P(None, None, "zs", "grp"),
        P(None, None, "zs", "grp"),
        P(None, None, "zs", None, None, "grp"),
        P(None, None, None, "zs", None, None, "grp"),
        P(),
        P(),
        P("grp"),
        P("grp"),
        P("grp", None),
    )
    out_specs = (P(None, None, "zs", None, None, "grp"), P("zs", "grp"))
    return jax.shard_map(shards, mesh=mesh, in_specs=in_specs, out_specs=out_specs, check_vma=False)
```

```python
import functools
import math

import jax
import jax.numpy as jnp
from jax import lax
from jax.experimental import pallas as pl
from jax.experimental.pallas import tpu as pltpu
from jax.sharding import PartitionSpec as P

NT = 8
LMAX = 8
PMOM = 3
G = 8
MOST = 96
LANES = 128
XH = 3
CROWS = 16

F32 = jnp.float32
BF16 = jnp.bfloat16
NT_DIMS = (((1,), (1,)), ((), ()))


def passed_along(block, axis, distance):
    devices = range(lax.axis_size(axis))
    route = [((i - distance) % len(devices), i) for i in devices]
    return lax.ppermute(block, axis, route)


def split_two(value):
    high = value.astype(BF16)
    return high, (value - high.astype(F32)).astype(BF16)


def iota(shape, axis):
    return lax.broadcasted_iota(jnp.int32, shape, axis)


def pack_kernel(last_group, block_z, block_x, up_ref, down_ref, *refs):
    *_, out_ref, up_rows, down_rows, out_rows, done = refs
    groups = lax.axis_size("zs") // G
    group = lax.axis_index("zs") // G

    @pl.when((group == groups - 1) == last_group)
    def _():
        copies = [
            pltpu.make_async_copy(up_ref, up_rows, done.at[0]),
            pltpu.make_async_copy(down_ref, down_rows, done.at[1]),
        ]
        for copy in copies:
            copy.start()
        for copy in copies:
            copy.wait()
        pack_rows(block_z, block_x, up_rows, down_rows, out_rows)
        copy = pltpu.make_async_copy(out_rows, out_ref, done.at[2])
        copy.start()
        copy.wait()


def pack_rows(block_z, block_x, up_ref, down_ref, out_ref):
    zh = block_z + 1
    slot_lanes = zh * XH
    width_x = block_x * G
    cells = up_ref.shape[3]
    z_blocks = cells // (block_z * width_x)
    up = up_ref[...].astype(F32)
    down = down_ref[...].astype(F32)

    def cross(a, b, c):
        d, e = (c + 1) % 3, (c + 2) % 3
        return up[a, d] * down[b, e] - up[a, e] * down[b, d]

    planes = [cross(0, 0, c) - cross(1, 1, c) for c in range(3)]
    planes += [cross(0, 1, c) + cross(1, 0, c) for c in range(3)]
    lane = iota((1, 2 * LANES), 1)
    half = lane // LANES
    within = lane % LANES
    slot = within // slot_lanes
    cell = within % slot_lanes
    source_row = iota((LANES, 2 * LANES), 0)
    results = []
    for comp in range(6):
        turned = (slot + 12 - comp - 4 * half) % 6
        source = (cell % zh) * width_x + (block_x * (turned + 4 * half) + cell // zh) % width_x
        source = jnp.where((turned < 4) & (slot < 6), source, -1)
        pick = jnp.where(source_row == source, 1.0, 0.0).astype(BF16)
        wide = jnp.concatenate([planes[comp], planes[comp][:, :LANES]], axis=1)
        rows = []
        for zb in range(z_blocks):
            begin = zb * block_z * width_x
            part = wide[:, begin : begin + LANES]
            high = part.astype(BF16).astype(F32)
            rows += [high, part - high]
        left = jnp.concatenate(rows, axis=0).astype(BF16)
        got = jnp.dot(left, pick, preferred_element_type=F32)
        got = got.reshape(z_blocks, 2, NT, 2 * LANES)
        results.append(got[:, 0] + got[:, 1])
    one_slot = iota((NT, LANES), 1) // slot_lanes
    for zb in range(z_blocks):
        for g in range(G):
            at = (g // 4) * LANES
            value = jnp.zeros((NT, LANES), F32)
            for comp in range(6):
                value = jnp.where(
                    one_slot == (comp + g) % 6, results[comp][zb, :, at : at + LANES], value
                )
            out_ref[zb * G + g] = value


def link_times(links, vec):
    real, imag = [], []
    for a in range(3):
        row = [(links[3 * a + b], links[9 + 3 * a + b]) for b in range(3)]
        real.append(sum(row[b][0] * vec[b] - row[b][1] * vec[3 + b] for b in range(3)))
        imag.append(sum(row[b][0] * vec[3 + b] + row[b][1] * vec[b] for b in range(3)))
    return real + imag


def edge_kernel(links_ref, forward_ref, ready_ref, edge_ref):
    edge_ref[0:6] = forward_ref[:, 0]
    links = [links_ref[i, 0].astype(F32) for i in range(18)]
    after = [forward_ref[c, 1].astype(F32) for c in range(6)]
    for c, value in enumerate(link_times(links, after)):
        high, low = split_two(value)
        edge_ref[6 + c] = high
        edge_ref[12 + c] = low


def phases(group, depth_z, block_z, block_x, scale):
    row = iota((CROWS, LANES), 0)
    angle = ((group * block_z + row // block_x) * PMOM % depth_z).astype(F32)
    angle = angle * (2.0 * math.pi / depth_z)
    inside = row < block_z * block_x
    cos_z = jnp.where(inside, jnp.cos(angle) * scale, 0.0)[:, :1]
    sin_z = jnp.where(inside, jnp.sin(angle) * scale, 0.0)[:, :1]
    return cos_z, sin_z


def chain_kernel(
    depth_z,
    scale,
    block_z,
    block_x,
    weight_ref,
    offset_ref,
    lengths_ref,
    separations_ref,
    owners_ref,
    links_ref,
    links_next_ref,
    forward_ref,
    forward_next_ref,
    chain_ref,
    corner_ref,
    picked_ref,
    link_rows,
    field_rows,
):
    place = lax.axis_index("zs")
    rows_y = links_ref.shape[3]
    zh = block_z + 1
    slot_lanes = zh * XH
    count = block_z * block_x
    no_plane = jnp.zeros((block_x, rows_y), F32)

    def fill_links(i, carry):
        for z in range(block_z):
            link_rows[i, block_x * z : block_x * (z + 1)] = links_ref[i, z].astype(F32)
            at = count + block_x * z
            last = z == block_z - 1
            plane = no_plane if last else links_next_ref[i, z].astype(F32)
            link_rows[i, at : at + block_x] = plane
        return carry

    def fill_field(i, carry):
        for z in range(block_z):
            field_rows[i, block_x * z : block_x * (z + 1)] = forward_ref[i, z].astype(F32)
            at = count + block_x * z
            field_rows[i, at : at + block_x] = forward_next_ref[i, z].astype(F32)
        return carry

    lax.fori_loop(0, 18, fill_links, 0)
    lax.fori_loop(0, 6, fill_field, 0)

    cos_z, sin_z = phases(place // G, depth_z, block_z, block_x, scale)
    total_rows = link_rows.shape[1]

    def step(length, carry):
        for at in range(0, rows_y, LANES):
            lanes = slice(at, at + LANES)
            vec = [
                pltpu.roll(field_rows[c, :, lanes], total_rows - block_x, 0) for c in range(6)
            ]
            for a in range(3):
                real = None
                imag = None
                for b in range(3):
                    link_real = link_rows[a * 3 + b, :, lanes]
                    link_imag = link_rows[9 + a * 3 + b, :, lanes]
                    term_real = link_real * vec[b] - link_imag * vec[3 + b]
                    term_imag = link_real * vec[3 + b] + link_imag * vec[b]
                    real = term_real if real is None else real + term_real
                    imag = term_imag if imag is None else imag + term_imag
                field_rows[a, :, lanes] = real
                field_rows[3 + a, :, lanes] = imag
                top_real, top_imag = real[:CROWS], imag[:CROWS]
                chain_ref[length, a * CROWS : (a + 1) * CROWS, lanes] = (
                    top_real * cos_z - top_imag * sin_z
                )
                chain_ref[length, (3 + a) * CROWS : (4 + a) * CROWS, lanes] = (
                    top_real * sin_z + top_imag * cos_z
                )
        return carry

    lax.fori_loop(0, LMAX, step, 0)

    shape = (6 * CROWS, LANES)
    row = iota(shape, 0)
    lane = iota(shape, 1)
    comp = row // CROWS
    z_step = lane % slot_lanes % zh - row % CROWS // block_x
    x_step = lane % slot_lanes // zh - row % block_x
    here = (lane // slot_lanes == (comp + place % G) % 6) & (row % CROWS < count)
    here = here & (x_step >= 0) & (x_step < 2) & (z_step >= 0) & (z_step < 2)
    table = jnp.zeros((8, LANES), F32)
    for k in range(8):
        corner = offset_ref[0, k] * 4 + offset_ref[1, k] * 2 + offset_ref[2, k]
        table = jnp.where(iota((8, LANES), 1) == corner, weight_ref[k], table)
    table = jnp.broadcast_to(table[0:1], shape)
    for y_step in range(2):
        corner = jnp.where(here, 4 * x_step + 2 * y_step + z_step, 0)
        weights = jnp.where(here, jnp.take_along_axis(table, corner, axis=1), 0.0)
        high, low = split_two(weights)
        corner_ref[0, y_step * 6 * CROWS : (y_step + 1) * 6 * CROWS] = high
        corner_ref[1, y_step * 6 * CROWS : (y_step + 1) * 6 * CROWS] = low

    mine = owners_ref[...] == place
    codes = (lengths_ref[...] * (2 * NT) + separations_ref[...]).astype(F32)
    member = jnp.where(mine, 1.0, 0.0)
    below = jnp.where(iota((LANES, LANES), 0) < iota((LANES, LANES), 1), 1.0, 0.0)
    earlier = jnp.dot(member.astype(BF16), below.astype(BF16), preferred_element_type=F32)
    running = jnp.zeros((1, 1), F32)
    picked = jnp.zeros((8, LANES), F32)
    slots = iota((LANES, LANES), 0).astype(F32)
    head = iota((8, LANES), 0) == 0
    for i in range(member.shape[0]):
        key = jnp.where(member[i : i + 1] > 0.5, earlier[i : i + 1] + running, -1.0)
        hits = jnp.where(slots == key, 1.0, 0.0).astype(BF16)
        left = jnp.where(head, codes[i : i + 1], 1.0).astype(BF16)
        picked = picked + lax.dot_general(left, hits, NT_DIMS, preferred_element_type=F32)
        running = running + jnp.sum(member[i : i + 1], axis=1, keepdims=True)
    lane_of = picked[0:1].astype(jnp.int32) + iota((8, LANES), 0) % 2 * NT
    picked_ref[...] = jnp.where(picked[1:2] > 0.5, lane_of, -1)


def tail_kernel(
    depth_z, scale, block_z, block_x, links_ref, links_next_ref, edge_ref, corner_ref, extra_ref
):
    cos_z, sin_z = phases(lax.axis_index("zs") // G, depth_z, block_z, block_x, scale)
    extra_ref[...] = jnp.zeros_like(extra_ref)
    planes = edge_ref[...].astype(F32)
    near = [planes[c] for c in range(6)]
    far = [planes[6 + c] + planes[12 + c] for c in range(6)]
    vecs = [near, far]
    for z in range(2 * block_z - 1, block_z - 3, -1):
        ref = links_ref if z < block_z else links_next_ref
        links = [ref[i, z % block_z].astype(F32) for i in range(18)]
        vecs = [link_times(links, vec) for vec in vecs]
        if z < block_z:
            at = z * block_x
            cos_at, sin_at = cos_z[at : at + block_x], sin_z[at : at + block_x]
            for k, vec in enumerate(vecs):
                kept = k + block_z - 1 - z
                for a in range(3):
                    real, imag = vec[a], vec[3 + a]
                    first = a * CROWS + at
                    extra_ref[kept, first : first + block_x] = real * cos_at - imag * sin_at
                    first = (3 + a) * CROWS + at
                    extra_ref[kept, first : first + block_x] = real * sin_at + imag * cos_at
            vecs = vecs[:-1]


def meet_kernel(block_z, block_x, got_ref, corner_ref, chain_ref, extra_ref, seq_ref, table_ref):
    rows_y = got_ref.shape[0] * NT
    got = got_ref[...].reshape(rows_y, LANES)
    high, low = split_two(got)
    dot = functools.partial(
        lax.dot_general, dimension_numbers=NT_DIMS, preferred_element_type=F32
    )
    both = dot(corner_ref[0], high) + dot(corner_ref[0], low) + dot(corner_ref[1], high)
    size = 6 * CROWS
    seq = both[:size] + pltpu.roll(both[size:], rows_y - NT, 1)
    for comp in range(6):
        for z in range(block_z):
            at = comp * CROWS + z * block_x
            seq_ref[comp, z] = seq[at : at + block_x]
    turned = jnp.concatenate([-seq[3 * CROWS :], seq[: 3 * CROWS]], axis=0)
    sums = []
    for length in range(LMAX):
        chain = chain_ref[length]
        if length >= block_z:
            chain = chain + extra_ref[length - block_z]
        for field in (seq, turned):
            prod = field * chain
            part = prod[:8]
            for at in range(8, size, 8):
                part = part + prod[at : at + 8]
            narrow = part[:, :LANES]
            for at in range(LANES, rows_y, LANES):
                narrow = narrow + part[:, at : at + LANES]
            sums.append(jnp.sum(narrow, axis=0, keepdims=True))
    table = jnp.concatenate(sums, axis=0)
    for shift in (64, 32, 16, 8):
        table = table + pltpu.roll(table, shift, 1)
    mine = iota((2 * LMAX, LANES), 1) // NT == iota((2 * LMAX, LANES), 0)
    flat = jnp.sum(jnp.where(mine, table, 0.0), axis=0, keepdims=True)
    table_ref[...] = jnp.broadcast_to(flat, table_ref.shape)


def final_kernel(tables_ref, picked_ref, out_ref):
    total = jnp.sum(tables_ref[...], axis=0, keepdims=True)
    picked = picked_ref[...]
    value = jnp.take_along_axis(
        jnp.broadcast_to(total, picked.shape), jnp.maximum(picked, 0), axis=1
    )
    value = jnp.where(picked >= 0, value, 0.0)
    out_ref[...] = value[:2, : out_ref.shape[1]]


VMEM = pl.BlockSpec(memory_space=pltpu.VMEM)
SMEM = pl.BlockSpec(memory_space=pltpu.SMEM)


def cost(flops, moved):
    return pl.CostEstimate(flops=flops, bytes_accessed=moved, transcendentals=0)


PARAMS = pltpu.CompilerParams(vmem_limit_bytes=16 * 1024 * 1024)
WIDE_PARAMS = pltpu.CompilerParams(vmem_limit_bytes=60 * 1024 * 1024)
WHOLE_PARAMS = pltpu.CompilerParams(vmem_limit_bytes=67_100_000)


def shards(
    quark_up,
    quark_down,
    forward,
    gauge_links,
    corner_weight,
    corner_offset,
    lengths,
    separations,
    owner_map,
):
    devices = lax.axis_size("zs")
    block_z, block_x, rows_y = forward.shape[3:]
    cells = quark_up.shape[3]
    depth_z = cells // (block_x * G)
    scale = 1.0 / math.sqrt(cells * (rows_y // NT))
    links = gauge_links.reshape(18, block_z, block_x, rows_y)
    field = forward.reshape(6, block_z, block_x, rows_y)

    def packed(last_group, *payload):
        anywhere = pl.BlockSpec(memory_space=pl.ANY)
        return pl.pallas_call(
            functools.partial(pack_kernel, last_group, block_z, block_x),
            out_shape=jax.ShapeDtypeStruct((devices, NT, LANES), F32),
            in_specs=[anywhere] * (2 + len(payload)),
            out_specs=anywhere,
            input_output_aliases={2: 0} if payload else {},
            scratch_shapes=[
                pltpu.VMEM(quark_up.shape, BF16),
                pltpu.VMEM(quark_up.shape, BF16),
                pltpu.VMEM((devices, NT, LANES), F32),
                pltpu.SemaphoreType.DMA((3,)),
            ],
            compiler_params=WIDE_PARAMS if last_group else WHOLE_PARAMS,
            cost_estimate=cost(2_000_000_000, 400_000) if last_group else cost(1_000, 1_000),
            name="pack",
        )(quark_up, quark_down, *payload)

    payload = packed(False)
    payload, links_out, field_out = lax.optimization_barrier((payload, links, field))
    links_next = passed_along(links_out, "zs", -G)
    field_next = passed_along(field_out, "zs", -G)
    payload = packed(True, payload)
    got = lax.all_to_all(payload, "zs", split_axis=0, concat_axis=0, tiled=True)

    past = LMAX - block_z
    requests = (lengths.shape[0] // LANES, LANES)
    edge = pl.pallas_call(
        edge_kernel,
        out_shape=jax.ShapeDtypeStruct((18, block_x, rows_y), BF16),
        in_specs=[VMEM] * 2 + [pl.BlockSpec(memory_space=pl.ANY)],
        out_specs=VMEM,
        compiler_params=PARAMS,
        cost_estimate=cost(50_000_000, 60_000),
        name="edge",
    )(links, field, links_next)
    edge_next = passed_along(edge, "zs", -2 * G)
    chain, corner, picked = pl.pallas_call(
        functools.partial(chain_kernel, depth_z, scale, block_z, block_x),
        out_shape=(
            jax.ShapeDtypeStruct((LMAX, 6 * CROWS, rows_y), F32),
            jax.ShapeDtypeStruct((2, 12 * CROWS, LANES), BF16),
            jax.ShapeDtypeStruct((8, LANES), jnp.int32),
        ),
        in_specs=[SMEM] * 2 + [VMEM] * 7,
        out_specs=(VMEM,) * 3,
        scratch_shapes=[
            pltpu.VMEM((18, 2 * block_z * block_x, rows_y), F32),
            pltpu.VMEM((6, 2 * block_z * block_x, rows_y), F32),
        ],
        compiler_params=PARAMS,
        cost_estimate=cost(3_000_000_000, 200_000),
        name="chain",
    )(
        corner_weight,
        corner_offset.T,
        lengths.reshape(requests),
        separations.reshape(requests),
        owner_map.reshape(requests),
        links,
        links_next,
        field,
        field_next,
    )

    extra = pl.pallas_call(
        functools.partial(tail_kernel, depth_z, scale, block_z, block_x),
        out_shape=jax.ShapeDtypeStruct((past, 6 * CROWS, rows_y), F32),
        in_specs=[VMEM] * 3 + [pl.BlockSpec(memory_space=pl.ANY)],
        out_specs=VMEM,
        compiler_params=PARAMS,
        cost_estimate=cost(400_000_000, 200_000),
        name="tail",
    )(links, links_next, edge_next, corner)

    seq, partial = pl.pallas_call(
        functools.partial(meet_kernel, block_z, block_x),
        out_shape=(
            jax.ShapeDtypeStruct((6, block_z, block_x, rows_y), F32),
            jax.ShapeDtypeStruct((devices, LANES), F32),
        ),
        in_specs=[VMEM] * 4,
        out_specs=(VMEM, VMEM),
        compiler_params=PARAMS,
        cost_estimate=cost(2_000_000_000, 1_000_000),
        name="meet",
    )(got, corner, chain, extra)
    tables = lax.all_to_all(
        partial.reshape(devices, 1, LANES), "zs", split_axis=0, concat_axis=0, tiled=True
    ).reshape(devices, LANES)
    owned = pl.pallas_call(
        final_kernel,
        out_shape=jax.ShapeDtypeStruct((2, MOST), F32),
        in_specs=[VMEM] * 2,
        out_specs=VMEM,
        compiler_params=PARAMS,
        name="final",
    )(tables, picked)
    return (seq.reshape(2, 3, 1, block_z, block_x, rows_y), owned.T)


def solution(mesh):
    in_specs = (
        P(None, None, "zs", "grp"),
        P(None, None, "zs", "grp"),
        P(None, None, "zs", None, None, "grp"),
        P(None, None, None, "zs", None, None, "grp"),
        P(),
        P(),
        P("grp"),
        P("grp"),
        P("grp", None),
    )
    out_specs = (P(None, None, "zs", None, None, "grp"), P("zs", "grp"))
    return jax.shard_map(shards, mesh=mesh, in_specs=in_specs, out_specs=out_specs, check_vma=False)
```

```python
import functools
import math

import jax
import jax.numpy as jnp
from jax import lax
from jax.experimental import pallas as pl
from jax.experimental.pallas import tpu as pltpu
from jax.sharding import PartitionSpec as P

NT = 8
LMAX = 8
PMOM = 3
G = 8
MOST = 96
LANES = 128
XH = 3
CROWS = 16

F32 = jnp.float32
BF16 = jnp.bfloat16
NT_DIMS = (((1,), (1,)), ((), ()))


def passed_along(block, axis, distance):
    devices = range(lax.axis_size(axis))
    route = [((i - distance) % len(devices), i) for i in devices]
    return lax.ppermute(block, axis, route)


def split_two(value):
    high = value.astype(BF16)
    return high, (value - high.astype(F32)).astype(BF16)


def iota(shape, axis):
    return lax.broadcasted_iota(jnp.int32, shape, axis)


def pack_kernel(
    block_z,
    block_x,
    weight_ref,
    offset_ref,
    up_ref,
    down_ref,
    lengths_ref,
    separations_ref,
    owners_ref,
    out_ref,
    request_ref,
    table_ref,
):
    codes = lengths_ref[...] * (2 * NT) + separations_ref[...]
    request_ref[...] = owners_ref[...] * LANES + codes
    lane = iota((8, LANES), 1)
    table = jnp.zeros((8, LANES), F32)
    for k in range(8):
        corner = offset_ref[0, k] * 4 + offset_ref[1, k] * 2 + offset_ref[2, k]
        table = jnp.where(lane == corner, weight_ref[k], table)
    table_ref[...] = table
    zh = block_z + 1
    slot_lanes = zh * XH
    width_x = block_x * G
    cells = up_ref.shape[3]
    z_blocks = cells // (block_z * width_x)
    up = up_ref[...].astype(F32)
    down = down_ref[...].astype(F32)

    def cross(a, b, c):
        d, e = (c + 1) % 3, (c + 2) % 3
        return up[a, d] * down[b, e] - up[a, e] * down[b, d]

    planes = [cross(0, 0, c) - cross(1, 1, c) for c in range(3)]
    planes += [cross(0, 1, c) + cross(1, 0, c) for c in range(3)]
    lane = iota((1, 2 * LANES), 1)
    half = lane // LANES
    within = lane % LANES
    slot = within // slot_lanes
    cell = within % slot_lanes
    source_row = iota((LANES, 2 * LANES), 0)
    results = []
    for comp in range(6):
        turned = (slot + 12 - comp - 4 * half) % 6
        source = (cell % zh) * width_x + (block_x * (turned + 4 * half) + cell // zh) % width_x
        source = jnp.where((turned < 4) & (slot < 6), source, -1)
        pick = jnp.where(source_row == source, 1.0, 0.0).astype(BF16)
        wide = jnp.concatenate([planes[comp], planes[comp][:, :LANES]], axis=1)
        rows = []
        for zb in range(z_blocks):
            begin = zb * block_z * width_x
            part = wide[:, begin : begin + LANES]
            high = part.astype(BF16).astype(F32)
            rows += [high, part - high]
        left = jnp.concatenate(rows, axis=0).astype(BF16)
        got = jnp.dot(left, pick, preferred_element_type=F32)
        got = got.reshape(z_blocks, 2, NT, 2 * LANES)
        results.append(got[:, 0] + got[:, 1])
    one_slot = iota((NT, LANES), 1) // slot_lanes
    for zb in range(z_blocks):
        for g in range(G):
            at = (g // 4) * LANES
            value = jnp.zeros((NT, LANES), F32)
            for comp in range(6):
                value = jnp.where(
                    one_slot == (comp + g) % 6, results[comp][zb, :, at : at + LANES], value
                )
            out_ref[zb * G + g] = value


def link_times(links, vec):
    real, imag = [], []
    for a in range(3):
        row = [(links[3 * a + b], links[9 + 3 * a + b]) for b in range(3)]
        real.append(sum(row[b][0] * vec[b] - row[b][1] * vec[3 + b] for b in range(3)))
        imag.append(sum(row[b][0] * vec[3 + b] + row[b][1] * vec[b] for b in range(3)))
    return real + imag


def edge_kernel(links_ref, forward_ref, ready_ref, edge_ref):
    edge_ref[0:6] = forward_ref[:, 0]
    links = [links_ref[i, 0].astype(F32) for i in range(18)]
    after = [forward_ref[c, 1].astype(F32) for c in range(6)]
    for c, value in enumerate(link_times(links, after)):
        high, low = split_two(value)
        edge_ref[6 + c] = high
        edge_ref[12 + c] = low


def phases(group, depth_z, block_z, block_x, scale):
    row = iota((CROWS, LANES), 0)
    angle = ((group * block_z + row // block_x) * PMOM % depth_z).astype(F32)
    angle = angle * (2.0 * math.pi / depth_z)
    inside = row < block_z * block_x
    cos_z = jnp.where(inside, jnp.cos(angle) * scale, 0.0)[:, :1]
    sin_z = jnp.where(inside, jnp.sin(angle) * scale, 0.0)[:, :1]
    return cos_z, sin_z


def chain_kernel(
    depth_z,
    scale,
    block_z,
    block_x,
    table_ref,
    request_ref,
    links_ref,
    links_next_ref,
    forward_ref,
    forward_next_ref,
    chain_ref,
    corner_ref,
    picked_ref,
    link_rows,
    field_rows,
):
    place = lax.axis_index("zs")
    rows_y = links_ref.shape[3]
    zh = block_z + 1
    slot_lanes = zh * XH
    count = block_z * block_x
    no_plane = jnp.zeros((block_x, rows_y), F32)

    def fill_links(i, carry):
        for z in range(block_z):
            link_rows[i, block_x * z : block_x * (z + 1)] = links_ref[i, z].astype(F32)
            at = count + block_x * z
            last = z == block_z - 1
            plane = no_plane if last else links_next_ref[i, z].astype(F32)
            link_rows[i, at : at + block_x] = plane
        return carry

    def fill_field(i, carry):
        for z in range(block_z):
            field_rows[i, block_x * z : block_x * (z + 1)] = forward_ref[i, z].astype(F32)
            at = count + block_x * z
            field_rows[i, at : at + block_x] = forward_next_ref[i, z].astype(F32)
        return carry

    lax.fori_loop(0, 18, fill_links, 0)
    lax.fori_loop(0, 6, fill_field, 0)

    cos_z, sin_z = phases(place // G, depth_z, block_z, block_x, scale)
    total_rows = link_rows.shape[1]

    def step(length, carry):
        for at in range(0, rows_y, LANES):
            lanes = slice(at, at + LANES)
            vec = [
                pltpu.roll(field_rows[c, :, lanes], total_rows - block_x, 0) for c in range(6)
            ]
            for a in range(3):
                real = None
                imag = None
                for b in range(3):
                    link_real = link_rows[a * 3 + b, :, lanes]
                    link_imag = link_rows[9 + a * 3 + b, :, lanes]
                    term_real = link_real * vec[b] - link_imag * vec[3 + b]
                    term_imag = link_real * vec[3 + b] + link_imag * vec[b]
                    real = term_real if real is None else real + term_real
                    imag = term_imag if imag is None else imag + term_imag
                field_rows[a, :, lanes] = real
                field_rows[3 + a, :, lanes] = imag
                top_real, top_imag = real[:CROWS], imag[:CROWS]
                chain_ref[length, a * CROWS : (a + 1) * CROWS, lanes] = (
                    top_real * cos_z - top_imag * sin_z
                )
                chain_ref[length, (3 + a) * CROWS : (4 + a) * CROWS, lanes] = (
                    top_real * sin_z + top_imag * cos_z
                )
        return carry

    lax.fori_loop(0, LMAX, step, 0)

    shape = (6 * CROWS, LANES)
    row = iota(shape, 0)
    lane = iota(shape, 1)
    comp = row // CROWS
    z_step = lane % slot_lanes % zh - row % CROWS // block_x
    x_step = lane % slot_lanes // zh - row % block_x
    here = (lane // slot_lanes == (comp + place % G) % 6) & (row % CROWS < count)
    here = here & (x_step >= 0) & (x_step < 2) & (z_step >= 0) & (z_step < 2)
    table = jnp.broadcast_to(table_ref[0:1], shape)
    for y_step in range(2):
        corner = jnp.where(here, 4 * x_step + 2 * y_step + z_step, 0)
        weights = jnp.where(here, jnp.take_along_axis(table, corner, axis=1), 0.0)
        high, low = split_two(weights)
        corner_ref[0, y_step * 6 * CROWS : (y_step + 1) * 6 * CROWS] = high
        corner_ref[1, y_step * 6 * CROWS : (y_step + 1) * 6 * CROWS] = low

    request = request_ref[...]
    mine = request // LANES == place
    codes = (request % LANES).astype(F32)
    member = jnp.where(mine, 1.0, 0.0)
    below = jnp.where(iota((LANES, LANES), 0) < iota((LANES, LANES), 1), 1.0, 0.0)
    earlier = jnp.dot(member.astype(BF16), below.astype(BF16), preferred_element_type=F32)
    running = jnp.zeros((1, 1), F32)
    picked = jnp.zeros((8, LANES), F32)
    slots = iota((LANES, LANES), 0).astype(F32)
    head = iota((8, LANES), 0) == 0
    for i in range(member.shape[0]):
        key = jnp.where(member[i : i + 1] > 0.5, earlier[i : i + 1] + running, -1.0)
        hits = jnp.where(slots == key, 1.0, 0.0).astype(BF16)
        left = jnp.where(head, codes[i : i + 1], 1.0).astype(BF16)
        picked = picked + lax.dot_general(left, hits, NT_DIMS, preferred_element_type=F32)
        running = running + jnp.sum(member[i : i + 1], axis=1, keepdims=True)
    lane_of = picked[0:1].astype(jnp.int32) + iota((8, LANES), 0) % 2 * NT
    picked_ref[...] = jnp.where(picked[1:2] > 0.5, lane_of, -1)


def tail_kernel(
    depth_z, scale, block_z, block_x, links_ref, links_next_ref, edge_ref, corner_ref, extra_ref
):
    cos_z, sin_z = phases(lax.axis_index("zs") // G, depth_z, block_z, block_x, scale)
    extra_ref[...] = jnp.zeros_like(extra_ref)
    planes = edge_ref[...].astype(F32)
    near = [planes[c] for c in range(6)]
    far = [planes[6 + c] + planes[12 + c] for c in range(6)]
    vecs = [near, far]
    for z in range(2 * block_z - 1, block_z - 3, -1):
        ref = links_ref if z < block_z else links_next_ref
        links = [ref[i, z % block_z].astype(F32) for i in range(18)]
        vecs = [link_times(links, vec) for vec in vecs]
        if z < block_z:
            at = z * block_x
            cos_at, sin_at = cos_z[at : at + block_x], sin_z[at : at + block_x]
            for k, vec in enumerate(vecs):
                kept = k + block_z - 1 - z
                for a in range(3):
                    real, imag = vec[a], vec[3 + a]
                    first = a * CROWS + at
                    extra_ref[kept, first : first + block_x] = real * cos_at - imag * sin_at
                    first = (3 + a) * CROWS + at
                    extra_ref[kept, first : first + block_x] = real * sin_at + imag * cos_at
            vecs = vecs[:-1]


def meet_kernel(block_z, block_x, got_ref, corner_ref, chain_ref, extra_ref, seq_ref, table_ref):
    rows_y = got_ref.shape[0] * NT
    got = got_ref[...].reshape(rows_y, LANES)
    high, low = split_two(got)
    dot = functools.partial(
        lax.dot_general, dimension_numbers=NT_DIMS, preferred_element_type=F32
    )
    both = dot(corner_ref[0], high) + dot(corner_ref[0], low) + dot(corner_ref[1], high)
    size = 6 * CROWS
    seq = both[:size] + pltpu.roll(both[size:], rows_y - NT, 1)
    for comp in range(6):
        for z in range(block_z):
            at = comp * CROWS + z * block_x
            seq_ref[comp, z] = seq[at : at + block_x]
    turned = jnp.concatenate([-seq[3 * CROWS :], seq[: 3 * CROWS]], axis=0)
    for length in range(LMAX):
        chain = chain_ref[length]
        if length >= block_z:
            chain = chain + extra_ref[length - block_z]
        for field in (seq, turned):
            prod = field * chain
            part = prod[:8]
            for at in range(8, size, 8):
                part = part + prod[at : at + 8]
            narrow = part[:, :LANES]
            for at in range(LANES, rows_y, LANES):
                narrow = narrow + part[:, at : at + LANES]
            row = (2 * length + (field is turned)) * 8
            table_ref[row : row + 8] = narrow


def final_kernel(total_ref, picked_ref, out_ref):
    table = jnp.sum(total_ref[...].reshape(2 * LMAX, 8, LANES), axis=1)
    for shift in (64, 32, 16, 8):
        table = table + pltpu.roll(table, shift, 1)
    mine = iota((2 * LMAX, LANES), 1) // NT == iota((2 * LMAX, LANES), 0)
    total = jnp.sum(jnp.where(mine, table, 0.0), axis=0, keepdims=True)
    picked = picked_ref[...]
    value = jnp.take_along_axis(
        jnp.broadcast_to(total, picked.shape), jnp.maximum(picked, 0), axis=1
    )
    value = jnp.where(picked >= 0, value, 0.0)
    out_ref[...] = value[:2, : out_ref.shape[1]]


VMEM = pl.BlockSpec(memory_space=pltpu.VMEM)
SMEM = pl.BlockSpec(memory_space=pltpu.SMEM)


def cost(flops, moved):
    return pl.CostEstimate(flops=flops, bytes_accessed=moved, transcendentals=0)


PARAMS = pltpu.CompilerParams(vmem_limit_bytes=16 * 1024 * 1024)
WIDE_PARAMS = pltpu.CompilerParams(vmem_limit_bytes=60 * 1024 * 1024)


def shards(
    quark_up,
    quark_down,
    forward,
    gauge_links,
    corner_weight,
    corner_offset,
    lengths,
    separations,
    owner_map,
):
    devices = lax.axis_size("zs")
    block_z, block_x, rows_y = forward.shape[3:]
    cells = quark_up.shape[3]
    depth_z = cells // (block_x * G)
    scale = 1.0 / math.sqrt(cells * (rows_y // NT))
    links = gauge_links.reshape(18, block_z, block_x, rows_y)
    field = forward.reshape(6, block_z, block_x, rows_y)

    links_next = passed_along(links, "zs", -G)
    field_next = passed_along(field, "zs", -G)
    requests = (lengths.shape[0] // LANES, LANES)
    payload, request, table = pl.pallas_call(
        functools.partial(pack_kernel, block_z, block_x),
        out_shape=(
            jax.ShapeDtypeStruct((devices, NT, LANES), F32),
            jax.ShapeDtypeStruct(requests, jnp.int32),
            jax.ShapeDtypeStruct((8, LANES), F32),
        ),
        grid=(1,),
        in_specs=[SMEM] * 2
        + [pl.BlockSpec(quark_up.shape, lambda i: (0, 0, 0, 0))] * 2
        + [pl.BlockSpec(requests, lambda i: (0, 0))] * 3,
        out_specs=(
            pl.BlockSpec((devices, NT, LANES), lambda i: (0, 0, 0)),
            pl.BlockSpec(requests, lambda i: (0, 0)),
            pl.BlockSpec((8, LANES), lambda i: (0, 0)),
        ),
        compiler_params=WIDE_PARAMS,
        cost_estimate=cost(2_000_000_000, 400_000),
        name="pack",
    )(
        corner_weight,
        corner_offset.T,
        quark_up,
        quark_down,
        lengths.reshape(requests),
        separations.reshape(requests),
        owner_map.reshape(requests),
    )
    got = lax.all_to_all(payload, "zs", split_axis=0, concat_axis=0, tiled=True)

    past = LMAX - block_z
    edge = pl.pallas_call(
        edge_kernel,
        out_shape=jax.ShapeDtypeStruct((18, block_x, rows_y), BF16),
        in_specs=[VMEM] * 2 + [pl.BlockSpec(memory_space=pl.ANY)],
        out_specs=VMEM,
        compiler_params=PARAMS,
        cost_estimate=cost(50_000_000, 60_000),
        name="edge",
    )(links, field, links_next)
    edge_next = passed_along(edge, "zs", -2 * G)
    chain, corner, picked = pl.pallas_call(
        functools.partial(chain_kernel, depth_z, scale, block_z, block_x),
        out_shape=(
            jax.ShapeDtypeStruct((LMAX, 6 * CROWS, rows_y), F32),
            jax.ShapeDtypeStruct((2, 12 * CROWS, LANES), BF16),
            jax.ShapeDtypeStruct((8, LANES), jnp.int32),
        ),
        in_specs=[VMEM] * 6,
        out_specs=(VMEM,) * 3,
        scratch_shapes=[
            pltpu.VMEM((18, 2 * block_z * block_x, rows_y), F32),
            pltpu.VMEM((6, 2 * block_z * block_x, rows_y), F32),
        ],
        compiler_params=PARAMS,
        cost_estimate=cost(3_000_000_000, 200_000),
        name="chain",
    )(table, request, links, links_next, field, field_next)

    extra = pl.pallas_call(
        functools.partial(tail_kernel, depth_z, scale, block_z, block_x),
        out_shape=jax.ShapeDtypeStruct((past, 6 * CROWS, rows_y), F32),
        in_specs=[VMEM] * 3 + [pl.BlockSpec(memory_space=pl.ANY)],
        out_specs=VMEM,
        compiler_params=PARAMS,
        cost_estimate=cost(400_000_000, 200_000),
        name="tail",
    )(links, links_next, edge_next, corner)

    seq, partial = pl.pallas_call(
        functools.partial(meet_kernel, block_z, block_x),
        out_shape=(
            jax.ShapeDtypeStruct((6, block_z, block_x, rows_y), F32),
            jax.ShapeDtypeStruct((16 * LMAX, LANES), F32),
        ),
        in_specs=[VMEM] * 4,
        out_specs=(VMEM, VMEM),
        compiler_params=PARAMS,
        cost_estimate=cost(2_000_000_000, 1_000_000),
        name="meet",
    )(got, corner, chain, extra)
    total = lax.psum(partial, "zs")
    owned = pl.pallas_call(
        final_kernel,
        out_shape=jax.ShapeDtypeStruct((2, MOST), F32),
        in_specs=[VMEM] * 2,
        out_specs=VMEM,
        compiler_params=PARAMS,
        name="final",
    )(total, picked)
    return (seq.reshape(2, 3, 1, block_z, block_x, rows_y), owned.T)


def solution(mesh):
    in_specs = (
        P(None, None, "zs", "grp"),
        P(None, None, "zs", "grp"),
        P(None, None, "zs", None, None, "grp"),
        P(None, None, None, "zs", None, None, "grp"),
        P(),
        P(),
        P("grp"),
        P("grp"),
        P("grp", None),
    )
    out_specs = (P(None, None, "zs", None, None, "grp"), P("zs", "grp"))
    return jax.shard_map(shards, mesh=mesh, in_specs=in_specs, out_specs=out_specs, check_vma=False)
```

```python
import functools
import math

import jax
import jax.numpy as jnp
from jax import lax
from jax.experimental import pallas as pl
from jax.experimental.pallas import tpu as pltpu
from jax.sharding import PartitionSpec as P

NT = 8
LMAX = 8
PMOM = 3
G = 8
MOST = 96
LANES = 128
XH = 3
CROWS = 16

F32 = jnp.float32
BF16 = jnp.bfloat16
NT_DIMS = (((1,), (1,)), ((), ()))


def passed_along(block, axis, distance):
    devices = range(lax.axis_size(axis))
    route = [((i - distance) % len(devices), i) for i in devices]
    return lax.ppermute(block, axis, route)


def split_two(value):
    high = value.astype(BF16)
    return high, (value - high.astype(F32)).astype(BF16)


def iota(shape, axis):
    return lax.broadcasted_iota(jnp.int32, shape, axis)


def pack_kernel(upper_half, block_z, block_x, up_ref, down_ref, *refs):
    *_, out_ref, up_rows, down_rows, out_rows, done = refs
    groups = lax.axis_size("zs") // G
    group = lax.axis_index("zs") // G

    @pl.when((group >= groups // 2) == upper_half)
    def _():
        copies = [
            pltpu.make_async_copy(up_ref, up_rows, done.at[0]),
            pltpu.make_async_copy(down_ref, down_rows, done.at[1]),
        ]
        for copy in copies:
            copy.start()
        for copy in copies:
            copy.wait()
        sends = [
            pltpu.make_async_copy(
                out_rows.at[zb * G : (zb + 1) * G], out_ref.at[zb * G : (zb + 1) * G], done.at[2 + zb]
            )
            for zb in range(groups)
        ]
        pack_rows(block_z, block_x, up_rows, down_rows, out_rows, sends)
        for copy in sends:
            copy.wait()


def pack_rows(block_z, block_x, up_ref, down_ref, out_ref, sends):
    zh = block_z + 1
    slot_lanes = zh * XH
    width_x = block_x * G
    cells = up_ref.shape[3]
    z_blocks = cells // (block_z * width_x)
    up = up_ref[...].astype(F32)
    down = down_ref[...].astype(F32)

    def cross(a, b, c):
        d, e = (c + 1) % 3, (c + 2) % 3
        return up[a, d] * down[b, e] - up[a, e] * down[b, d]

    planes = [cross(0, 0, c) - cross(1, 1, c) for c in range(3)]
    planes += [cross(0, 1, c) + cross(1, 0, c) for c in range(3)]
    lane = iota((1, 2 * LANES), 1)
    half = lane // LANES
    within = lane % LANES
    slot = within // slot_lanes
    cell = within % slot_lanes
    source_row = iota((LANES, 2 * LANES), 0)
    results = []
    for comp in range(6):
        turned = (slot + 12 - comp - 4 * half) % 6
        source = (cell % zh) * width_x + (block_x * (turned + 4 * half) + cell // zh) % width_x
        source = jnp.where((turned < 4) & (slot < 6), source, -1)
        pick = jnp.where(source_row == source, 1.0, 0.0).astype(BF16)
        wide = jnp.concatenate([planes[comp], planes[comp][:, :LANES]], axis=1)
        rows = []
        for zb in range(z_blocks):
            begin = zb * block_z * width_x
            part = wide[:, begin : begin + LANES]
            high = part.astype(BF16).astype(F32)
            rows += [high, part - high]
        left = jnp.concatenate(rows, axis=0).astype(BF16)
        got = jnp.dot(left, pick, preferred_element_type=F32)
        got = got.reshape(z_blocks, 2, NT, 2 * LANES)
        results.append(got[:, 0] + got[:, 1])
    one_slot = iota((NT, LANES), 1) // slot_lanes
    for zb in range(z_blocks):
        for g in range(G):
            at = (g // 4) * LANES
            value = jnp.zeros((NT, LANES), F32)
            for comp in range(6):
                value = jnp.where(
                    one_slot == (comp + g) % 6, results[comp][zb, :, at : at + LANES], value
                )
            out_ref[zb * G + g] = value
        sends[zb].start()


def link_times(links, vec):
    real, imag = [], []
    for a in range(3):
        row = [(links[3 * a + b], links[9 + 3 * a + b]) for b in range(3)]
        real.append(sum(row[b][0] * vec[b] - row[b][1] * vec[3 + b] for b in range(3)))
        imag.append(sum(row[b][0] * vec[3 + b] + row[b][1] * vec[b] for b in range(3)))
    return real + imag


def edge_kernel(links_ref, forward_ref, ready_ref, edge_ref):
    edge_ref[0:6] = forward_ref[:, 0]
    links = [links_ref[i, 0].astype(F32) for i in range(18)]
    after = [forward_ref[c, 1].astype(F32) for c in range(6)]
    for c, value in enumerate(link_times(links, after)):
        high, low = split_two(value)
        edge_ref[6 + c] = high
        edge_ref[12 + c] = low


def phases(group, depth_z, block_z, block_x, scale):
    row = iota((CROWS, LANES), 0)
    angle = ((group * block_z + row // block_x) * PMOM % depth_z).astype(F32)
    angle = angle * (2.0 * math.pi / depth_z)
    inside = row < block_z * block_x
    cos_z = jnp.where(inside, jnp.cos(angle) * scale, 0.0)[:, :1]
    sin_z = jnp.where(inside, jnp.sin(angle) * scale, 0.0)[:, :1]
    return cos_z, sin_z


def chain_kernel(
    depth_z,
    scale,
    block_z,
    block_x,
    weight_ref,
    offset_ref,
    lengths_ref,
    separations_ref,
    owners_ref,
    links_ref,
    links_next_ref,
    forward_ref,
    forward_next_ref,
    chain_ref,
    corner_ref,
    picked_ref,
    link_rows,
    field_rows,
):
    place = lax.axis_index("zs")
    rows_y = links_ref.shape[3]
    zh = block_z + 1
    slot_lanes = zh * XH
    count = block_z * block_x
    no_plane = jnp.zeros((block_x, rows_y), F32)

    def fill_links(i, carry):
        for z in range(block_z):
            link_rows[i, block_x * z : block_x * (z + 1)] = links_ref[i, z].astype(F32)
            at = count + block_x * z
            last = z == block_z - 1
            plane = no_plane if last else links_next_ref[i, z].astype(F32)
            link_rows[i, at : at + block_x] = plane
        return carry

    def fill_field(i, carry):
        for z in range(block_z):
            field_rows[i, block_x * z : block_x * (z + 1)] = forward_ref[i, z].astype(F32)
            at = count + block_x * z
            field_rows[i, at : at + block_x] = forward_next_ref[i, z].astype(F32)
        return carry

    lax.fori_loop(0, 18, fill_links, 0)
    lax.fori_loop(0, 6, fill_field, 0)

    cos_z, sin_z = phases(place // G, depth_z, block_z, block_x, scale)
    total_rows = link_rows.shape[1]

    def step(length, carry):
        for at in range(0, rows_y, LANES):
            lanes = slice(at, at + LANES)
            vec = [
                pltpu.roll(field_rows[c, :, lanes], total_rows - block_x, 0) for c in range(6)
            ]
            for a in range(3):
                real = None
                imag = None
                for b in range(3):
                    link_real = link_rows[a * 3 + b, :, lanes]
                    link_imag = link_rows[9 + a * 3 + b, :, lanes]
                    term_real = link_real * vec[b] - link_imag * vec[3 + b]
                    term_imag = link_real * vec[3 + b] + link_imag * vec[b]
                    real = term_real if real is None else real + term_real
                    imag = term_imag if imag is None else imag + term_imag
                field_rows[a, :, lanes] = real
                field_rows[3 + a, :, lanes] = imag
                top_real, top_imag = real[:CROWS], imag[:CROWS]
                chain_ref[length, a * CROWS : (a + 1) * CROWS, lanes] = (
                    top_real * cos_z - top_imag * sin_z
                )
                chain_ref[length, (3 + a) * CROWS : (4 + a) * CROWS, lanes] = (
                    top_real * sin_z + top_imag * cos_z
                )
        return carry

    lax.fori_loop(0, LMAX, step, 0)

    shape = (6 * CROWS, LANES)
    row = iota(shape, 0)
    lane = iota(shape, 1)
    comp = row // CROWS
    z_step = lane % slot_lanes % zh - row % CROWS // block_x
    x_step = lane % slot_lanes // zh - row % block_x
    here = (lane // slot_lanes == (comp + place % G) % 6) & (row % CROWS < count)
    here = here & (x_step >= 0) & (x_step < 2) & (z_step >= 0) & (z_step < 2)
    table = jnp.zeros((8, LANES), F32)
    for k in range(8):
        corner = offset_ref[0, k] * 4 + offset_ref[1, k] * 2 + offset_ref[2, k]
        table = jnp.where(iota((8, LANES), 1) == corner, weight_ref[k], table)
    table = jnp.broadcast_to(table[0:1], shape)
    for y_step in range(2):
        corner = jnp.where(here, 4 * x_step + 2 * y_step + z_step, 0)
        weights = jnp.where(here, jnp.take_along_axis(table, corner, axis=1), 0.0)
        high, low = split_two(weights)
        rows = slice(y_step * 6 * CROWS, (y_step + 1) * 6 * CROWS)
        corner_ref[rows] = jnp.concatenate([high, high, low], axis=1)

    mine = owners_ref[...] == place
    codes = (lengths_ref[...] * (2 * NT) + separations_ref[...]).astype(F32)
    member = jnp.where(mine, 1.0, 0.0)
    below = jnp.where(iota((LANES, LANES), 0) < iota((LANES, LANES), 1), 1.0, 0.0)
    earlier = jnp.dot(member.astype(BF16), below.astype(BF16), preferred_element_type=F32)
    running = jnp.zeros((1, 1), F32)
    picked = jnp.zeros((8, LANES), F32)
    slots = iota((LANES, LANES), 0).astype(F32)
    head = iota((8, LANES), 0) == 0
    for i in range(member.shape[0]):
        key = jnp.where(member[i : i + 1] > 0.5, earlier[i : i + 1] + running, -1.0)
        hits = jnp.where(slots == key, 1.0, 0.0).astype(BF16)
        left = jnp.where(head, codes[i : i + 1], 1.0).astype(BF16)
        picked = picked + lax.dot_general(left, hits, NT_DIMS, preferred_element_type=F32)
        running = running + jnp.sum(member[i : i + 1], axis=1, keepdims=True)
    lane_of = picked[0:1].astype(jnp.int32) + iota((8, LANES), 0) % 2 * NT
    picked_ref[...] = jnp.where(picked[1:2] > 0.5, lane_of, -1)


def tail_kernel(
    depth_z, scale, block_z, block_x, links_ref, links_next_ref, edge_ref, corner_ref, extra_ref
):
    cos_z, sin_z = phases(lax.axis_index("zs") // G, depth_z, block_z, block_x, scale)
    extra_ref[...] = jnp.zeros_like(extra_ref)
    planes = edge_ref[...].astype(F32)
    near = [planes[c] for c in range(6)]
    far = [planes[6 + c] + planes[12 + c] for c in range(6)]
    vecs = [near, far]
    for z in range(2 * block_z - 1, block_z - 3, -1):
        ref = links_ref if z < block_z else links_next_ref
        links = [ref[i, z % block_z].astype(F32) for i in range(18)]
        vecs = [link_times(links, vec) for vec in vecs]
        if z < block_z:
            at = z * block_x
            cos_at, sin_at = cos_z[at : at + block_x], sin_z[at : at + block_x]
            for k, vec in enumerate(vecs):
                kept = k + block_z - 1 - z
                for a in range(3):
                    real, imag = vec[a], vec[3 + a]
                    first = a * CROWS + at
                    extra_ref[kept, first : first + block_x] = real * cos_at - imag * sin_at
                    first = (3 + a) * CROWS + at
                    extra_ref[kept, first : first + block_x] = real * sin_at + imag * cos_at
            vecs = vecs[:-1]


def meet_kernel(block_z, block_x, got_ref, corner_ref, chain_ref, extra_ref, seq_ref, table_ref):
    rows_y = got_ref.shape[0] * NT
    got = got_ref[...].reshape(rows_y, LANES)
    high, low = split_two(got)
    terms = jnp.concatenate([high, low, high], axis=1)
    both = lax.dot_general(corner_ref[...], terms, NT_DIMS, preferred_element_type=F32)
    size = 6 * CROWS
    seq = both[:size] + pltpu.roll(both[size:], rows_y - NT, 1)
    for comp in range(6):
        for z in range(block_z):
            at = comp * CROWS + z * block_x
            seq_ref[comp, z] = seq[at : at + block_x]
    turned = jnp.concatenate([-seq[3 * CROWS :], seq[: 3 * CROWS]], axis=0)
    sums = []
    for length in range(LMAX):
        chain = chain_ref[length]
        if length >= block_z:
            chain = chain + extra_ref[length - block_z]
        for field in (seq, turned):
            prod = field * chain
            part = prod[:8]
            for at in range(8, size, 8):
                part = part + prod[at : at + 8]
            narrow = part[:, :LANES]
            for at in range(LANES, rows_y, LANES):
                narrow = narrow + part[:, at : at + LANES]
            sums.append(narrow)
    rows = 2 * LMAX * 8
    high, low = split_two(jnp.concatenate(sums, axis=0))
    same_t = jnp.where(iota((LANES, LANES), 0) % NT == iota((LANES, LANES), 1) % NT, 1.0, 0.0)
    table = jnp.dot(
        jnp.concatenate([high, low], axis=0), same_t.astype(BF16), preferred_element_type=F32
    )
    table = table[:rows] + table[rows:]
    mine = iota((rows, LANES), 1) // NT == iota((rows, LANES), 0) // 8
    flat = jnp.sum(jnp.where(mine, table, 0.0), axis=0, keepdims=True)
    table_ref[...] = jnp.broadcast_to(flat, table_ref.shape)


def final_kernel(tables_ref, picked_ref, out_ref):
    total = jnp.sum(tables_ref[...], axis=0, keepdims=True)
    picked = picked_ref[...]
    value = jnp.take_along_axis(
        jnp.broadcast_to(total, picked.shape), jnp.maximum(picked, 0), axis=1
    )
    value = jnp.where(picked >= 0, value, 0.0)
    out_ref[...] = value[:2, : out_ref.shape[1]]


VMEM = pl.BlockSpec(memory_space=pltpu.VMEM)
SMEM = pl.BlockSpec(memory_space=pltpu.SMEM)


def cost(flops, moved):
    return pl.CostEstimate(flops=flops, bytes_accessed=moved, transcendentals=0)


PARAMS = pltpu.CompilerParams(vmem_limit_bytes=16 * 1024 * 1024)
WIDE_PARAMS = pltpu.CompilerParams(vmem_limit_bytes=60 * 1024 * 1024)
WHOLE_PARAMS = pltpu.CompilerParams(vmem_limit_bytes=67_100_000)


def shards(
    quark_up,
    quark_down,
    forward,
    gauge_links,
    corner_weight,
    corner_offset,
    lengths,
    separations,
    owner_map,
):
    devices = lax.axis_size("zs")
    block_z, block_x, rows_y = forward.shape[3:]
    cells = quark_up.shape[3]
    depth_z = cells // (block_x * G)
    scale = 1.0 / math.sqrt(cells * (rows_y // NT))
    links = gauge_links.reshape(18, block_z, block_x, rows_y)
    field = forward.reshape(6, block_z, block_x, rows_y)

    def packed(upper_half, *payload):
        anywhere = pl.BlockSpec(memory_space=pl.ANY)
        return pl.pallas_call(
            functools.partial(pack_kernel, upper_half, block_z, block_x),
            out_shape=jax.ShapeDtypeStruct((devices, NT, LANES), F32),
            in_specs=[anywhere] * (2 + len(payload)),
            out_specs=anywhere,
            input_output_aliases={2: 0} if payload else {},
            scratch_shapes=[
                pltpu.VMEM(quark_up.shape, BF16),
                pltpu.VMEM(quark_up.shape, BF16),
                pltpu.VMEM((devices, NT, LANES), F32),
                pltpu.SemaphoreType.DMA((2 + devices // G,)),
            ],
            compiler_params=WIDE_PARAMS if upper_half else WHOLE_PARAMS,
            cost_estimate=cost(2_000_000_000, 400_000) if upper_half else cost(1_000, 1_000),
            name="pack",
        )(quark_up, quark_down, *payload)

    payload = packed(False)
    payload, links_out, field_out = lax.optimization_barrier((payload, links, field))
    links_next = passed_along(links_out, "zs", -G)
    field_next = passed_along(field_out, "zs", -G)
    payload = packed(True, payload)
    got = lax.all_to_all(payload, "zs", split_axis=0, concat_axis=0, tiled=True)

    past = LMAX - block_z
    requests = (lengths.shape[0] // LANES, LANES)
    edge = pl.pallas_call(
        edge_kernel,
        out_shape=jax.ShapeDtypeStruct((18, block_x, rows_y), BF16),
        in_specs=[VMEM] * 2 + [pl.BlockSpec(memory_space=pl.ANY)],
        out_specs=VMEM,
        compiler_params=PARAMS,
        cost_estimate=cost(50_000_000, 60_000),
        name="edge",
    )(links, field, links_next)
    edge_next = passed_along(edge, "zs", -2 * G)
    chain, corner, picked = pl.pallas_call(
        functools.partial(chain_kernel, depth_z, scale, block_z, block_x),
        out_shape=(
            jax.ShapeDtypeStruct((LMAX, 6 * CROWS, rows_y), F32),
            jax.ShapeDtypeStruct((12 * CROWS, 3 * LANES), BF16),
            jax.ShapeDtypeStruct((8, LANES), jnp.int32),
        ),
        in_specs=[SMEM] * 2 + [VMEM] * 7,
        out_specs=(VMEM,) * 3,
        scratch_shapes=[
            pltpu.VMEM((18, 2 * block_z * block_x, rows_y), F32),
            pltpu.VMEM((6, 2 * block_z * block_x, rows_y), F32),
        ],
        compiler_params=PARAMS,
        cost_estimate=cost(3_000_000_000, 200_000),
        name="chain",
    )(
        corner_weight,
        corner_offset.T,
        lengths.reshape(requests),
        separations.reshape(requests),
        owner_map.reshape(requests),
        links,
        links_next,
        field,
        field_next,
    )

    extra = pl.pallas_call(
        functools.partial(tail_kernel, depth_z, scale, block_z, block_x),
        out_shape=jax.ShapeDtypeStruct((past, 6 * CROWS, rows_y), F32),
        in_specs=[VMEM] * 3 + [pl.BlockSpec(memory_space=pl.ANY)],
        out_specs=VMEM,
        compiler_params=PARAMS,
        cost_estimate=cost(400_000_000, 200_000),
        name="tail",
    )(links, links_next, edge_next, corner)

    seq, partial = pl.pallas_call(
        functools.partial(meet_kernel, block_z, block_x),
        out_shape=(
            jax.ShapeDtypeStruct((6, block_z, block_x, rows_y), F32),
            jax.ShapeDtypeStruct((devices, LANES), F32),
        ),
        in_specs=[VMEM] * 4,
        out_specs=(VMEM, VMEM),
        compiler_params=PARAMS,
        cost_estimate=cost(2_000_000_000, 1_000_000),
        name="meet",
    )(got, corner, chain, extra)
    tables = lax.all_to_all(
        partial.reshape(devices, 1, LANES), "zs", split_axis=0, concat_axis=0, tiled=True
    ).reshape(devices, LANES)
    owned = pl.pallas_call(
        final_kernel,
        out_shape=jax.ShapeDtypeStruct((2, MOST), F32),
        in_specs=[VMEM] * 2,
        out_specs=VMEM,
        compiler_params=PARAMS,
        name="final",
    )(tables, picked)
    return (seq.reshape(2, 3, 1, block_z, block_x, rows_y), owned.T)


def solution(mesh):
    in_specs = (
        P(None, None, "zs", "grp"),
        P(None, None, "zs", "grp"),
        P(None, None, "zs", None, None, "grp"),
        P(None, None, None, "zs", None, None, "grp"),
        P(),
        P(),
        P("grp"),
        P("grp"),
        P("grp", None),
    )
    out_specs = (P(None, None, "zs", None, None, "grp"), P("zs", "grp"))
    return jax.shard_map(shards, mesh=mesh, in_specs=in_specs, out_specs=out_specs, check_vma=False)
```

```python
import functools
import math

import jax
import jax.numpy as jnp
from jax import lax
from jax.experimental import pallas as pl
from jax.experimental.pallas import tpu as pltpu
from jax.sharding import PartitionSpec as P

NT = 8
LMAX = 8
PMOM = 3
G = 8
MOST = 96
LANES = 128
XH = 3
CROWS = 16
GROUP = 32

F32 = jnp.float32
BF16 = jnp.bfloat16
NT_DIMS = (((1,), (1,)), ((), ()))


def passed_along(block, axis, distance):
    devices = range(lax.axis_size(axis))
    route = [((i - distance) % len(devices), i) for i in devices]
    return lax.ppermute(block, axis, route)


def split_two(value):
    high = value.astype(BF16)
    return high, (value - high.astype(F32)).astype(BF16)


def iota(shape, axis):
    return lax.broadcasted_iota(jnp.int32, shape, axis)


def pack_kernel(
    block_z,
    block_x,
    weight_ref,
    offset_ref,
    up_ref,
    down_ref,
    lengths_ref,
    separations_ref,
    owners_ref,
    out_ref,
    request_ref,
    table_ref,
):
    codes = lengths_ref[...] * (2 * NT) + separations_ref[...]
    request_ref[...] = owners_ref[...] * LANES + codes
    lane = iota((8, LANES), 1)
    table = jnp.zeros((8, LANES), F32)
    for k in range(8):
        corner = offset_ref[0, k] * 4 + offset_ref[1, k] * 2 + offset_ref[2, k]
        table = jnp.where(lane == corner, weight_ref[k], table)
    table_ref[...] = table
    zh = block_z + 1
    slot_lanes = zh * XH
    width_x = block_x * G
    cells = up_ref.shape[3]
    z_blocks = cells // (block_z * width_x)
    up = up_ref[...].astype(F32)
    down = down_ref[...].astype(F32)

    def cross(a, b, c):
        d, e = (c + 1) % 3, (c + 2) % 3
        return up[a, d] * down[b, e] - up[a, e] * down[b, d]

    planes = [cross(0, 0, c) - cross(1, 1, c) for c in range(3)]
    planes += [cross(0, 1, c) + cross(1, 0, c) for c in range(3)]
    lane = iota((1, 2 * LANES), 1)
    cell = lane % GROUP
    source = (cell % zh) * width_x + (block_x * (lane // GROUP) + cell // zh) % width_x
    source = jnp.where(cell < slot_lanes, source, -1)
    pick = jnp.where(iota((LANES, 2 * LANES), 0) == source, 1.0, 0.0).astype(BF16)
    rows = []
    for plane in planes:
        wide = jnp.concatenate([plane, plane[:, :LANES]], axis=1)
        for zb in range(z_blocks):
            begin = zb * block_z * width_x
            part = wide[:, begin : begin + LANES]
            high = part.astype(BF16).astype(F32)
            rows += [high, part - high]
    left = jnp.concatenate(rows, axis=0).astype(BF16)
    got = jnp.dot(left, pick, preferred_element_type=F32)
    got = got.reshape(6 * z_blocks, 2, NT, 2 * LANES)
    got = (got[:, 0] + got[:, 1]).reshape(6, z_blocks * NT, 2 * LANES)
    slot = iota((z_blocks * NT, LANES), 1) // slot_lanes
    per_half = LANES // GROUP
    for g in range(G):
        at = (g // per_half) * LANES
        value = jnp.zeros((z_blocks * NT, LANES), F32)
        for comp in range(6):
            shift = (comp * slot_lanes - (g % per_half) * GROUP) % LANES
            part = got[comp, :, at : at + LANES]
            part = pltpu.roll(part, shift, 1) if shift else part
            value = jnp.where(slot == comp, part, value)
        for zb in range(z_blocks):
            out_ref[zb * G + g] = value[zb * NT : (zb + 1) * NT]


def link_times(links, vec):
    real, imag = [], []
    for a in range(3):
        row = [(links[3 * a + b], links[9 + 3 * a + b]) for b in range(3)]
        real.append(sum(row[b][0] * vec[b] - row[b][1] * vec[3 + b] for b in range(3)))
        imag.append(sum(row[b][0] * vec[3 + b] + row[b][1] * vec[b] for b in range(3)))
    return real + imag


def edge_kernel(links_ref, forward_ref, ready_ref, edge_ref):
    edge_ref[0:6] = forward_ref[:, 0]
    links = [links_ref[i, 0].astype(F32) for i in range(18)]
    after = [forward_ref[c, 1].astype(F32) for c in range(6)]
    for c, value in enumerate(link_times(links, after)):
        high, low = split_two(value)
        edge_ref[6 + c] = high
        edge_ref[12 + c] = low


def phases(group, depth_z, block_z, block_x, scale):
    row = iota((CROWS, LANES), 0)
    angle = ((group * block_z + row // block_x) * PMOM % depth_z).astype(F32)
    angle = angle * (2.0 * math.pi / depth_z)
    inside = row < block_z * block_x
    cos_z = jnp.where(inside, jnp.cos(angle) * scale, 0.0)[:, :1]
    sin_z = jnp.where(inside, jnp.sin(angle) * scale, 0.0)[:, :1]
    return cos_z, sin_z


def chain_kernel(
    depth_z,
    scale,
    block_z,
    block_x,
    table_ref,
    request_ref,
    links_ref,
    links_next_ref,
    forward_ref,
    forward_next_ref,
    chain_ref,
    corner_ref,
    picked_ref,
    link_rows,
    field_rows,
):
    place = lax.axis_index("zs")
    rows_y = links_ref.shape[3]
    zh = block_z + 1
    slot_lanes = zh * XH
    count = block_z * block_x
    no_plane = jnp.zeros((block_x, rows_y), F32)

    def fill_links(i, carry):
        for z in range(block_z):
            link_rows[i, block_x * z : block_x * (z + 1)] = links_ref[i, z].astype(F32)
            at = count + block_x * z
            last = z == block_z - 1
            plane = no_plane if last else links_next_ref[i, z].astype(F32)
            link_rows[i, at : at + block_x] = plane
        return carry

    def fill_field(i, carry):
        for z in range(block_z):
            field_rows[i, block_x * z : block_x * (z + 1)] = forward_ref[i, z].astype(F32)
            at = count + block_x * z
            field_rows[i, at : at + block_x] = forward_next_ref[i, z].astype(F32)
        return carry

    lax.fori_loop(0, 18, fill_links, 0)
    lax.fori_loop(0, 6, fill_field, 0)

    cos_z, sin_z = phases(place // G, depth_z, block_z, block_x, scale)
    total_rows = link_rows.shape[1]

    def step(length, carry):
        for at in range(0, rows_y, LANES):
            lanes = slice(at, at + LANES)
            vec = [
                pltpu.roll(field_rows[c, :, lanes], total_rows - block_x, 0) for c in range(6)
            ]
            for a in range(3):
                real = None
                imag = None
                for b in range(3):
                    link_real = link_rows[a * 3 + b, :, lanes]
                    link_imag = link_rows[9 + a * 3 + b, :, lanes]
                    term_real = link_real * vec[b] - link_imag * vec[3 + b]
                    term_imag = link_real * vec[3 + b] + link_imag * vec[b]
                    real = term_real if real is None else real + term_real
                    imag = term_imag if imag is None else imag + term_imag
                field_rows[a, :, lanes] = real
                field_rows[3 + a, :, lanes] = imag
                top_real, top_imag = real[:CROWS], imag[:CROWS]
                chain_ref[length, a * CROWS : (a + 1) * CROWS, lanes] = (
                    top_real * cos_z - top_imag * sin_z
                )
                chain_ref[length, (3 + a) * CROWS : (4 + a) * CROWS, lanes] = (
                    top_real * sin_z + top_imag * cos_z
                )
        return carry

    lax.fori_loop(0, LMAX, step, 0)

    shape = (6 * CROWS, LANES)
    row = iota(shape, 0)
    lane = iota(shape, 1)
    comp = row // CROWS
    z_step = lane % slot_lanes % zh - row % CROWS // block_x
    x_step = lane % slot_lanes // zh - row % block_x
    here = (lane // slot_lanes == comp) & (row % CROWS < count)
    here = here & (x_step >= 0) & (x_step < 2) & (z_step >= 0) & (z_step < 2)
    table = jnp.broadcast_to(table_ref[0:1], shape)
    for y_step in range(2):
        corner = jnp.where(here, 4 * x_step + 2 * y_step + z_step, 0)
        weights = jnp.where(here, jnp.take_along_axis(table, corner, axis=1), 0.0)
        high, low = split_two(weights)
        corner_ref[0, y_step * 6 * CROWS : (y_step + 1) * 6 * CROWS] = high
        corner_ref[1, y_step * 6 * CROWS : (y_step + 1) * 6 * CROWS] = low

    request = request_ref[...]
    mine = request // LANES == place
    codes = (request % LANES).astype(F32)
    member = jnp.where(mine, 1.0, 0.0)
    below = jnp.where(iota((LANES, LANES), 0) < iota((LANES, LANES), 1), 1.0, 0.0)
    earlier = jnp.dot(member.astype(BF16), below.astype(BF16), preferred_element_type=F32)
    running = jnp.zeros((1, 1), F32)
    picked = jnp.zeros((8, LANES), F32)
    slots = iota((LANES, LANES), 0).astype(F32)
    head = iota((8, LANES), 0) == 0
    for i in range(member.shape[0]):
        key = jnp.where(member[i : i + 1] > 0.5, earlier[i : i + 1] + running, -1.0)
        hits = jnp.where(slots == key, 1.0, 0.0).astype(BF16)
        left = jnp.where(head, codes[i : i + 1], 1.0).astype(BF16)
        picked = picked + lax.dot_general(left, hits, NT_DIMS, preferred_element_type=F32)
        running = running + jnp.sum(member[i : i + 1], axis=1, keepdims=True)
    lane_of = picked[0:1].astype(jnp.int32) + iota((8, LANES), 0) % 2 * NT
    picked_ref[...] = jnp.where(picked[1:2] > 0.5, lane_of, -1)


def tail_kernel(
    depth_z, scale, block_z, block_x, links_ref, links_next_ref, edge_ref, corner_ref, extra_ref
):
    cos_z, sin_z = phases(lax.axis_index("zs") // G, depth_z, block_z, block_x, scale)
    extra_ref[...] = jnp.zeros_like(extra_ref)
    planes = edge_ref[...].astype(F32)
    near = [planes[c] for c in range(6)]
    far = [planes[6 + c] + planes[12 + c] for c in range(6)]
    vecs = [near, far]
    for z in range(2 * block_z - 1, block_z - 3, -1):
        ref = links_ref if z < block_z else links_next_ref
        links = [ref[i, z % block_z].astype(F32) for i in range(18)]
        vecs = [link_times(links, vec) for vec in vecs]
        if z < block_z:
            at = z * block_x
            cos_at, sin_at = cos_z[at : at + block_x], sin_z[at : at + block_x]
            for k, vec in enumerate(vecs):
                kept = k + block_z - 1 - z
                for a in range(3):
                    real, imag = vec[a], vec[3 + a]
                    first = a * CROWS + at
                    extra_ref[kept, first : first + block_x] = real * cos_at - imag * sin_at
                    first = (3 + a) * CROWS + at
                    extra_ref[kept, first : first + block_x] = real * sin_at + imag * cos_at
            vecs = vecs[:-1]


def meet_kernel(block_z, block_x, got_ref, corner_ref, chain_ref, extra_ref, seq_ref, table_ref):
    rows_y = got_ref.shape[0] * NT
    got = got_ref[...].reshape(rows_y, LANES)
    high, low = split_two(got)
    dot = functools.partial(
        lax.dot_general, dimension_numbers=NT_DIMS, preferred_element_type=F32
    )
    both = dot(corner_ref[0], high) + dot(corner_ref[0], low) + dot(corner_ref[1], high)
    size = 6 * CROWS
    seq = both[:size] + pltpu.roll(both[size:], rows_y - NT, 1)
    for comp in range(6):
        for z in range(block_z):
            at = comp * CROWS + z * block_x
            seq_ref[comp, z] = seq[at : at + block_x]
    turned = jnp.concatenate([-seq[3 * CROWS :], seq[: 3 * CROWS]], axis=0)
    sums = []
    for length in range(LMAX):
        chain = chain_ref[length]
        if length >= block_z:
            chain = chain + extra_ref[length - block_z]
        for field in (seq, turned):
            prod = field * chain
            part = prod[:8]
            for at in range(8, size, 8):
                part = part + prod[at : at + 8]
            narrow = part[:, :LANES]
            for at in range(LANES, rows_y, LANES):
                narrow = narrow + part[:, at : at + LANES]
            sums.append(jnp.sum(narrow, axis=0, keepdims=True))
    table = jnp.concatenate(sums, axis=0)
    for shift in (64, 32, 16, 8):
        table = table + pltpu.roll(table, shift, 1)
    mine = iota((2 * LMAX, LANES), 1) // NT == iota((2 * LMAX, LANES), 0)
    flat = jnp.sum(jnp.where(mine, table, 0.0), axis=0, keepdims=True)
    table_ref[...] = jnp.broadcast_to(flat, table_ref.shape)


def final_kernel(tables_ref, picked_ref, out_ref):
    total = jnp.sum(tables_ref[...], axis=0, keepdims=True)
    picked = picked_ref[...]
    value = jnp.take_along_axis(
        jnp.broadcast_to(total, picked.shape), jnp.maximum(picked, 0), axis=1
    )
    value = jnp.where(picked >= 0, value, 0.0)
    out_ref[...] = value[:2, : out_ref.shape[1]]


VMEM = pl.BlockSpec(memory_space=pltpu.VMEM)
SMEM = pl.BlockSpec(memory_space=pltpu.SMEM)


def cost(flops, moved):
    return pl.CostEstimate(flops=flops, bytes_accessed=moved, transcendentals=0)


PARAMS = pltpu.CompilerParams(vmem_limit_bytes=16 * 1024 * 1024)
WIDE_PARAMS = pltpu.CompilerParams(vmem_limit_bytes=60 * 1024 * 1024)


def shards(
    quark_up,
    quark_down,
    forward,
    gauge_links,
    corner_weight,
    corner_offset,
    lengths,
    separations,
    owner_map,
):
    devices = lax.axis_size("zs")
    block_z, block_x, rows_y = forward.shape[3:]
    cells = quark_up.shape[3]
    depth_z = cells // (block_x * G)
    scale = 1.0 / math.sqrt(cells * (rows_y // NT))
    links = gauge_links.reshape(18, block_z, block_x, rows_y)
    field = forward.reshape(6, block_z, block_x, rows_y)

    links_next = passed_along(links, "zs", -G)
    field_next = passed_along(field, "zs", -G)
    requests = (lengths.shape[0] // LANES, LANES)
    payload, request, table = pl.pallas_call(
        functools.partial(pack_kernel, block_z, block_x),
        out_shape=(
            jax.ShapeDtypeStruct((devices, NT, LANES), F32),
            jax.ShapeDtypeStruct(requests, jnp.int32),
            jax.ShapeDtypeStruct((8, LANES), F32),
        ),
        grid=(1,),
        in_specs=[SMEM] * 2
        + [pl.BlockSpec(quark_up.shape, lambda i: (0, 0, 0, 0))] * 2
        + [pl.BlockSpec(requests, lambda i: (0, 0))] * 3,
        out_specs=(
            pl.BlockSpec((devices, NT, LANES), lambda i: (0, 0, 0)),
            pl.BlockSpec(requests, lambda i: (0, 0)),
            pl.BlockSpec((8, LANES), lambda i: (0, 0)),
        ),
        compiler_params=WIDE_PARAMS,
        cost_estimate=cost(2_000_000_000, 400_000),
        name="pack",
    )(
        corner_weight,
        corner_offset.T,
        quark_up,
        quark_down,
        lengths.reshape(requests),
        separations.reshape(requests),
        owner_map.reshape(requests),
    )
    got = lax.all_to_all(payload, "zs", split_axis=0, concat_axis=0, tiled=True)

    past = LMAX - block_z
    edge = pl.pallas_call(
        edge_kernel,
        out_shape=jax.ShapeDtypeStruct((18, block_x, rows_y), BF16),
        in_specs=[VMEM] * 2 + [pl.BlockSpec(memory_space=pl.ANY)],
        out_specs=VMEM,
        compiler_params=PARAMS,
        cost_estimate=cost(50_000_000, 60_000),
        name="edge",
    )(links, field, links_next)
    edge_next = passed_along(edge, "zs", -2 * G)
    chain, corner, picked = pl.pallas_call(
        functools.partial(chain_kernel, depth_z, scale, block_z, block_x),
        out_shape=(
            jax.ShapeDtypeStruct((LMAX, 6 * CROWS, rows_y), F32),
            jax.ShapeDtypeStruct((2, 12 * CROWS, LANES), BF16),
            jax.ShapeDtypeStruct((8, LANES), jnp.int32),
        ),
        in_specs=[VMEM] * 6,
        out_specs=(VMEM,) * 3,
        scratch_shapes=[
            pltpu.VMEM((18, 2 * block_z * block_x, rows_y), F32),
            pltpu.VMEM((6, 2 * block_z * block_x, rows_y), F32),
        ],
        compiler_params=PARAMS,
        cost_estimate=cost(3_000_000_000, 200_000),
        name="chain",
    )(table, request, links, links_next, field, field_next)

    extra = pl.pallas_call(
        functools.partial(tail_kernel, depth_z, scale, block_z, block_x),
        out_shape=jax.ShapeDtypeStruct((past, 6 * CROWS, rows_y), F32),
        in_specs=[VMEM] * 3 + [pl.BlockSpec(memory_space=pl.ANY)],
        out_specs=VMEM,
        compiler_params=PARAMS,
        cost_estimate=cost(400_000_000, 200_000),
        name="tail",
    )(links, links_next, edge_next, corner)

    seq, partial = pl.pallas_call(
        functools.partial(meet_kernel, block_z, block_x),
        out_shape=(
            jax.ShapeDtypeStruct((6, block_z, block_x, rows_y), F32),
            jax.ShapeDtypeStruct((devices, LANES), F32),
        ),
        in_specs=[VMEM] * 4,
        out_specs=(VMEM, VMEM),
        compiler_params=PARAMS,
        cost_estimate=cost(2_000_000_000, 1_000_000),
        name="meet",
    )(got, corner, chain, extra)
    tables = lax.all_to_all(
        partial.reshape(devices, 1, LANES), "zs", split_axis=0, concat_axis=0, tiled=True
    ).reshape(devices, LANES)
    owned = pl.pallas_call(
        final_kernel,
        out_shape=jax.ShapeDtypeStruct((2, MOST), F32),
        in_specs=[VMEM] * 2,
        out_specs=VMEM,
        compiler_params=PARAMS,
        name="final",
    )(tables, picked)
    return (seq.reshape(2, 3, 1, block_z, block_x, rows_y), owned.T)


def solution(mesh):
    in_specs = (
        P(None, None, "zs", "grp"),
        P(None, None, "zs", "grp"),
        P(None, None, "zs", None, None, "grp"),
        P(None, None, None, "zs", None, None, "grp"),
        P(),
        P(),
        P("grp"),
        P("grp"),
        P("grp", None),
    )
    out_specs = (P(None, None, "zs", None, None, "grp"), P("zs", "grp"))
    return jax.shard_map(shards, mesh=mesh, in_specs=in_specs, out_specs=out_specs, check_vma=False)
```

```python
import functools
import math

import jax
import jax.numpy as jnp
import numpy as np
from jax import lax
from jax.experimental import pallas as pl
from jax.experimental.pallas import tpu as pltpu
from jax.sharding import PartitionSpec as P

NT = 8
LMAX = 8
PMOM = 3
G = 8
MOST = 96
LANES = 128
XH = 3
CROWS = 16

F32 = jnp.float32
BF16 = jnp.bfloat16
NT_DIMS = (((1,), (1,)), ((), ()))


def passed_along(block, axis, distance):
    devices = range(lax.axis_size(axis))
    route = [((i - distance) % len(devices), i) for i in devices]
    return lax.ppermute(block, axis, route)


def split_two(value):
    high = value.astype(BF16)
    return high, (value - high.astype(F32)).astype(BF16)


def iota(shape, axis):
    return lax.broadcasted_iota(jnp.int32, shape, axis)


def pick_matrices(block_z, block_x):
    zh = block_z + 1
    lane = np.arange(2 * LANES)
    half, slot, cell = lane // LANES, lane % LANES // (zh * XH), lane % LANES % (zh * XH)
    width_x = block_x * G
    picks = []
    for comp in range(6):
        turned = (slot + 12 - comp - 4 * half) % 6
        source = cell % zh * width_x + (block_x * (turned + 4 * half) + cell // zh) % width_x
        source = np.where((turned < 4) & (slot < 6), source, -1)
        picks.append(np.arange(LANES)[:, None] == source[None, :])
    return jnp.asarray(np.stack(picks), BF16)


def pack_kernel(
    block_z,
    block_x,
    weight_ref,
    offset_ref,
    up_ref,
    down_ref,
    lengths_ref,
    separations_ref,
    owners_ref,
    pick_ref,
    out_ref,
    request_ref,
    table_ref,
):
    codes = lengths_ref[...] * (2 * NT) + separations_ref[...]
    request_ref[...] = owners_ref[...] * LANES + codes
    lane = iota((8, LANES), 1)
    table = jnp.zeros((8, LANES), F32)
    for k in range(8):
        corner = offset_ref[0, k] * 4 + offset_ref[1, k] * 2 + offset_ref[2, k]
        table = jnp.where(lane == corner, weight_ref[k], table)
    table_ref[...] = table
    zh = block_z + 1
    slot_lanes = zh * XH
    width_x = block_x * G
    cells = up_ref.shape[3]
    z_blocks = cells // (block_z * width_x)
    up = up_ref[...].astype(F32)
    down = down_ref[...].astype(F32)

    def cross(a, b, c):
        d, e = (c + 1) % 3, (c + 2) % 3
        return up[a, d] * down[b, e] - up[a, e] * down[b, d]

    planes = [cross(0, 0, c) - cross(1, 1, c) for c in range(3)]
    planes += [cross(0, 1, c) + cross(1, 0, c) for c in range(3)]
    results = []
    for comp in range(6):
        wide = jnp.concatenate([planes[comp], planes[comp][:, :LANES]], axis=1)
        rows = []
        for zb in range(z_blocks):
            begin = zb * block_z * width_x
            part = wide[:, begin : begin + LANES]
            high = part.astype(BF16).astype(F32)
            rows += [high, part - high]
        left = jnp.concatenate(rows, axis=0).astype(BF16)
        got = jnp.dot(left, pick_ref[comp], preferred_element_type=F32)
        got = got.reshape(z_blocks, 2, NT, 2 * LANES)
        results.append(got[:, 0] + got[:, 1])
    one_slot = iota((NT, LANES), 1) // slot_lanes
    for zb in range(z_blocks):
        for g in range(G):
            at = (g // 4) * LANES
            value = jnp.zeros((NT, LANES), F32)
            for comp in range(6):
                value = jnp.where(
                    one_slot == (comp + g) % 6, results[comp][zb, :, at : at + LANES], value
                )
            out_ref[zb * G + g] = value


def link_times(links, vec):
    real, imag = [], []
    for a in range(3):
        row = [(links[3 * a + b], links[9 + 3 * a + b]) for b in range(3)]
        real.append(sum(row[b][0] * vec[b] - row[b][1] * vec[3 + b] for b in range(3)))
        imag.append(sum(row[b][0] * vec[3 + b] + row[b][1] * vec[b] for b in range(3)))
    return real + imag


def edge_kernel(links_ref, forward_ref, ready_ref, edge_ref):
    edge_ref[0:6] = forward_ref[:, 0]
    links = [links_ref[i, 0].astype(F32) for i in range(18)]
    after = [forward_ref[c, 1].astype(F32) for c in range(6)]
    for c, value in enumerate(link_times(links, after)):
        high, low = split_two(value)
        edge_ref[6 + c] = high
        edge_ref[12 + c] = low


def phases(group, depth_z, block_z, block_x, scale):
    row = iota((CROWS, LANES), 0)
    angle = ((group * block_z + row // block_x) * PMOM % depth_z).astype(F32)
    angle = angle * (2.0 * math.pi / depth_z)
    inside = row < block_z * block_x
    cos_z = jnp.where(inside, jnp.cos(angle) * scale, 0.0)[:, :1]
    sin_z = jnp.where(inside, jnp.sin(angle) * scale, 0.0)[:, :1]
    return cos_z, sin_z


def chain_kernel(
    depth_z,
    scale,
    block_z,
    block_x,
    table_ref,
    request_ref,
    links_ref,
    links_next_ref,
    forward_ref,
    forward_next_ref,
    chain_ref,
    corner_ref,
    picked_ref,
    link_rows,
    field_rows,
):
    place = lax.axis_index("zs")
    rows_y = links_ref.shape[3]
    zh = block_z + 1
    slot_lanes = zh * XH
    count = block_z * block_x
    no_plane = jnp.zeros((block_x, rows_y), F32)

    def fill_links(i, carry):
        for z in range(block_z):
            link_rows[i, block_x * z : block_x * (z + 1)] = links_ref[i, z].astype(F32)
            at = count + block_x * z
            last = z == block_z - 1
            plane = no_plane if last else links_next_ref[i, z].astype(F32)
            link_rows[i, at : at + block_x] = plane
        return carry

    def fill_field(i, carry):
        for z in range(block_z):
            field_rows[i, block_x * z : block_x * (z + 1)] = forward_ref[i, z].astype(F32)
            at = count + block_x * z
            field_rows[i, at : at + block_x] = forward_next_ref[i, z].astype(F32)
        return carry

    lax.fori_loop(0, 18, fill_links, 0)
    lax.fori_loop(0, 6, fill_field, 0)

    cos_z, sin_z = phases(place // G, depth_z, block_z, block_x, scale)
    total_rows = link_rows.shape[1]

    def step(length, carry):
        for at in range(0, rows_y, LANES):
            lanes = slice(at, at + LANES)
            vec = [
                pltpu.roll(field_rows[c, :, lanes], total_rows - block_x, 0) for c in range(6)
            ]
            for a in range(3):
                real = None
                imag = None
                for b in range(3):
                    link_real = link_rows[a * 3 + b, :, lanes]
                    link_imag = link_rows[9 + a * 3 + b, :, lanes]
                    term_real = link_real * vec[b] - link_imag * vec[3 + b]
                    term_imag = link_real * vec[3 + b] + link_imag * vec[b]
                    real = term_real if real is None else real + term_real
                    imag = term_imag if imag is None else imag + term_imag
                field_rows[a, :, lanes] = real
                field_rows[3 + a, :, lanes] = imag
                top_real, top_imag = real[:CROWS], imag[:CROWS]
                chain_ref[length, a * CROWS : (a + 1) * CROWS, lanes] = (
                    top_real * cos_z - top_imag * sin_z
                )
                chain_ref[length, (3 + a) * CROWS : (4 + a) * CROWS, lanes] = (
                    top_real * sin_z + top_imag * cos_z
                )
        return carry

    lax.fori_loop(0, LMAX, step, 0)

    shape = (6 * CROWS, LANES)
    row = iota(shape, 0)
    lane = iota(shape, 1)
    comp = row // CROWS
    z_step = lane % slot_lanes % zh - row % CROWS // block_x
    x_step = lane % slot_lanes // zh - row % block_x
    here = (lane // slot_lanes == (comp + place % G) % 6) & (row % CROWS < count)
    here = here & (x_step >= 0) & (x_step < 2) & (z_step >= 0) & (z_step < 2)
    table = jnp.broadcast_to(table_ref[0:1], shape)
    for y_step in range(2):
        corner = jnp.where(here, 4 * x_step + 2 * y_step + z_step, 0)
        weights = jnp.where(here, jnp.take_along_axis(table, corner, axis=1), 0.0)
        high, low = split_two(weights)
        corner_ref[0, y_step * 6 * CROWS : (y_step + 1) * 6 * CROWS] = high
        corner_ref[1, y_step * 6 * CROWS : (y_step + 1) * 6 * CROWS] = low

    request = request_ref[...]
    mine = request // LANES == place
    codes = (request % LANES).astype(F32)
    member = jnp.where(mine, 1.0, 0.0)
    below = jnp.where(iota((LANES, LANES), 0) < iota((LANES, LANES), 1), 1.0, 0.0)
    earlier = jnp.dot(member.astype(BF16), below.astype(BF16), preferred_element_type=F32)
    running = jnp.zeros((1, 1), F32)
    picked = jnp.zeros((8, LANES), F32)
    slots = iota((LANES, LANES), 0).astype(F32)
    head = iota((8, LANES), 0) == 0
    for i in range(member.shape[0]):
        key = jnp.where(member[i : i + 1] > 0.5, earlier[i : i + 1] + running, -1.0)
        hits = jnp.where(slots == key, 1.0, 0.0).astype(BF16)
        left = jnp.where(head, codes[i : i + 1], 1.0).astype(BF16)
        picked = picked + lax.dot_general(left, hits, NT_DIMS, preferred_element_type=F32)
        running = running + jnp.sum(member[i : i + 1], axis=1, keepdims=True)
    lane_of = picked[0:1].astype(jnp.int32) + iota((8, LANES), 0) % 2 * NT
    picked_ref[...] = jnp.where(picked[1:2] > 0.5, lane_of, -1)


def tail_kernel(
    depth_z, scale, block_z, block_x, links_ref, links_next_ref, edge_ref, corner_ref, extra_ref
):
    cos_z, sin_z = phases(lax.axis_index("zs") // G, depth_z, block_z, block_x, scale)
    extra_ref[...] = jnp.zeros_like(extra_ref)
    planes = edge_ref[...].astype(F32)
    near = [planes[c] for c in range(6)]
    far = [planes[6 + c] + planes[12 + c] for c in range(6)]
    vecs = [near, far]
    for z in range(2 * block_z - 1, block_z - 3, -1):
        ref = links_ref if z < block_z else links_next_ref
        links = [ref[i, z % block_z].astype(F32) for i in range(18)]
        vecs = [link_times(links, vec) for vec in vecs]
        if z < block_z:
            at = z * block_x
            cos_at, sin_at = cos_z[at : at + block_x], sin_z[at : at + block_x]
            for k, vec in enumerate(vecs):
                kept = k + block_z - 1 - z
                for a in range(3):
                    real, imag = vec[a], vec[3 + a]
                    first = a * CROWS + at
                    extra_ref[kept, first : first + block_x] = real * cos_at - imag * sin_at
                    first = (3 + a) * CROWS + at
                    extra_ref[kept, first : first + block_x] = real * sin_at + imag * cos_at
            vecs = vecs[:-1]


def meet_kernel(block_z, block_x, got_ref, corner_ref, chain_ref, extra_ref, seq_ref, table_ref):
    rows_y = got_ref.shape[0] * NT
    got = got_ref[...].reshape(rows_y, LANES)
    high, low = split_two(got)
    dot = functools.partial(
        lax.dot_general, dimension_numbers=NT_DIMS, preferred_element_type=F32
    )
    both = dot(corner_ref[0], high) + dot(corner_ref[0], low) + dot(corner_ref[1], high)
    size = 6 * CROWS
    seq = both[:size] + pltpu.roll(both[size:], rows_y - NT, 1)
    for comp in range(6):
        for z in range(block_z):
            at = comp * CROWS + z * block_x
            seq_ref[comp, z] = seq[at : at + block_x]
    turned = jnp.concatenate([-seq[3 * CROWS :], seq[: 3 * CROWS]], axis=0)
    sums = []
    for length in range(LMAX):
        chain = chain_ref[length]
        if length >= block_z:
            chain = chain + extra_ref[length - block_z]
        for field in (seq, turned):
            prod = field * chain
            part = prod[:8]
            for at in range(8, size, 8):
                part = part + prod[at : at + 8]
            narrow = part[:, :LANES]
            for at in range(LANES, rows_y, LANES):
                narrow = narrow + part[:, at : at + LANES]
            sums.append(jnp.sum(narrow, axis=0, keepdims=True))
    table = jnp.concatenate(sums, axis=0)
    for shift in (64, 32, 16, 8):
        table = table + pltpu.roll(table, shift, 1)
    mine = iota((2 * LMAX, LANES), 1) // NT == iota((2 * LMAX, LANES), 0)
    flat = jnp.sum(jnp.where(mine, table, 0.0), axis=0, keepdims=True)
    table_ref[...] = jnp.broadcast_to(flat, table_ref.shape)


def final_kernel(tables_ref, picked_ref, out_ref):
    total = jnp.sum(tables_ref[...], axis=0, keepdims=True)
    picked = picked_ref[...]
    value = jnp.take_along_axis(
        jnp.broadcast_to(total, picked.shape), jnp.maximum(picked, 0), axis=1
    )
    value = jnp.where(picked >= 0, value, 0.0)
    out_ref[...] = value[:2, : out_ref.shape[1]]


VMEM = pl.BlockSpec(memory_space=pltpu.VMEM)
SMEM = pl.BlockSpec(memory_space=pltpu.SMEM)


def cost(flops, moved):
    return pl.CostEstimate(flops=flops, bytes_accessed=moved, transcendentals=0)


PARAMS = pltpu.CompilerParams(vmem_limit_bytes=16 * 1024 * 1024)
WIDE_PARAMS = pltpu.CompilerParams(vmem_limit_bytes=60 * 1024 * 1024)


def shards(
    quark_up,
    quark_down,
    forward,
    gauge_links,
    corner_weight,
    corner_offset,
    lengths,
    separations,
    owner_map,
):
    devices = lax.axis_size("zs")
    block_z, block_x, rows_y = forward.shape[3:]
    cells = quark_up.shape[3]
    depth_z = cells // (block_x * G)
    scale = 1.0 / math.sqrt(cells * (rows_y // NT))
    links = gauge_links.reshape(18, block_z, block_x, rows_y)
    field = forward.reshape(6, block_z, block_x, rows_y)

    links_next = passed_along(links, "zs", -G)
    field_next = passed_along(field, "zs", -G)
    requests = (lengths.shape[0] // LANES, LANES)
    payload, request, table = pl.pallas_call(
        functools.partial(pack_kernel, block_z, block_x),
        out_shape=(
            jax.ShapeDtypeStruct((devices, NT, LANES), F32),
            jax.ShapeDtypeStruct(requests, jnp.int32),
            jax.ShapeDtypeStruct((8, LANES), F32),
        ),
        grid=(1,),
        in_specs=[SMEM] * 2
        + [pl.BlockSpec(quark_up.shape, lambda i: (0, 0, 0, 0))] * 2
        + [pl.BlockSpec(requests, lambda i: (0, 0))] * 3
        + [pl.BlockSpec((6, LANES, 2 * LANES), lambda i: (0, 0, 0))],
        out_specs=(
            pl.BlockSpec((devices, NT, LANES), lambda i: (0, 0, 0)),
            pl.BlockSpec(requests, lambda i: (0, 0)),
            pl.BlockSpec((8, LANES), lambda i: (0, 0)),
        ),
        compiler_params=WIDE_PARAMS,
        cost_estimate=cost(2_000_000_000, 400_000),
        name="pack",
    )(
        corner_weight,
        corner_offset.T,
        quark_up,
        quark_down,
        lengths.reshape(requests),
        separations.reshape(requests),
        owner_map.reshape(requests),
        pick_matrices(block_z, block_x),
    )
    got = lax.all_to_all(payload, "zs", split_axis=0, concat_axis=0, tiled=True)

    past = LMAX - block_z
    edge = pl.pallas_call(
        edge_kernel,
        out_shape=jax.ShapeDtypeStruct((18, block_x, rows_y), BF16),
        in_specs=[VMEM] * 2 + [pl.BlockSpec(memory_space=pl.ANY)],
        out_specs=VMEM,
        compiler_params=PARAMS,
        cost_estimate=cost(50_000_000, 60_000),
        name="edge",
    )(links, field, links_next)
    edge_next = passed_along(edge, "zs", -2 * G)
    chain, corner, picked = pl.pallas_call(
        functools.partial(chain_kernel, depth_z, scale, block_z, block_x),
        out_shape=(
            jax.ShapeDtypeStruct((LMAX, 6 * CROWS, rows_y), F32),
            jax.ShapeDtypeStruct((2, 12 * CROWS, LANES), BF16),
            jax.ShapeDtypeStruct((8, LANES), jnp.int32),
        ),
        in_specs=[VMEM] * 6,
        out_specs=(VMEM,) * 3,
        scratch_shapes=[
            pltpu.VMEM((18, 2 * block_z * block_x, rows_y), F32),
            pltpu.VMEM((6, 2 * block_z * block_x, rows_y), F32),
        ],
        compiler_params=PARAMS,
        cost_estimate=cost(3_000_000_000, 200_000),
        name="chain",
    )(table, request, links, links_next, field, field_next)

    extra = pl.pallas_call(
        functools.partial(tail_kernel, depth_z, scale, block_z, block_x),
        out_shape=jax.ShapeDtypeStruct((past, 6 * CROWS, rows_y), F32),
        in_specs=[VMEM] * 3 + [pl.BlockSpec(memory_space=pl.ANY)],
        out_specs=VMEM,
        compiler_params=PARAMS,
        cost_estimate=cost(400_000_000, 200_000),
        name="tail",
    )(links, links_next, edge_next, corner)

    seq, partial = pl.pallas_call(
        functools.partial(meet_kernel, block_z, block_x),
        out_shape=(
            jax.ShapeDtypeStruct((6, block_z, block_x, rows_y), F32),
            jax.ShapeDtypeStruct((devices, LANES), F32),
        ),
        in_specs=[VMEM] * 4,
        out_specs=(VMEM, VMEM),
        compiler_params=PARAMS,
        cost_estimate=cost(2_000_000_000, 1_000_000),
        name="meet",
    )(got, corner, chain, extra)
    tables = lax.all_to_all(
        partial.reshape(devices, 1, LANES), "zs", split_axis=0, concat_axis=0, tiled=True
    ).reshape(devices, LANES)
    owned = pl.pallas_call(
        final_kernel,
        out_shape=jax.ShapeDtypeStruct((2, MOST), F32),
        in_specs=[VMEM] * 2,
        out_specs=VMEM,
        compiler_params=PARAMS,
        name="final",
    )(tables, picked)
    return (seq.reshape(2, 3, 1, block_z, block_x, rows_y), owned.T)


def solution(mesh):
    in_specs = (
        P(None, None, "zs", "grp"),
        P(None, None, "zs", "grp"),
        P(None, None, "zs", None, None, "grp"),
        P(None, None, None, "zs", None, None, "grp"),
        P(),
        P(),
        P("grp"),
        P("grp"),
        P("grp", None),
    )
    out_specs = (P(None, None, "zs", None, None, "grp"), P("zs", "grp"))
    return jax.shard_map(shards, mesh=mesh, in_specs=in_specs, out_specs=out_specs, check_vma=False)
```

```python
import functools
import math

import jax
import jax.numpy as jnp
from jax import lax
from jax.experimental import pallas as pl
from jax.experimental.pallas import tpu as pltpu
from jax.sharding import PartitionSpec as P

NT = 8
LMAX = 8
PMOM = 3
G = 8
MOST = 96
LANES = 128
XH = 3
CROWS = 16

F32 = jnp.float32
BF16 = jnp.bfloat16
NT_DIMS = (((1,), (1,)), ((), ()))


def passed_along(block, axis, distance):
    devices = range(lax.axis_size(axis))
    route = [((i - distance) % len(devices), i) for i in devices]
    return lax.ppermute(block, axis, route)


def split_two(value):
    high = value.astype(BF16)
    return high, (value - high.astype(F32)).astype(BF16)


def iota(shape, axis):
    return lax.broadcasted_iota(jnp.int32, shape, axis)


def pack_kernel(
    block_z,
    block_x,
    weight_ref,
    offset_ref,
    up_ref,
    down_ref,
    lengths_ref,
    separations_ref,
    owners_ref,
    out_ref,
    request_ref,
    table_ref,
):
    codes = lengths_ref[...] * (2 * NT) + separations_ref[...]
    request_ref[...] = owners_ref[...] * LANES + codes
    lane = iota((8, LANES), 1)
    table = jnp.zeros((8, LANES), F32)
    for k in range(8):
        corner = offset_ref[0, k] * 4 + offset_ref[1, k] * 2 + offset_ref[2, k]
        table = jnp.where(lane == corner, weight_ref[k], table)
    table_ref[...] = table
    zh = block_z + 1
    slot_lanes = zh * XH
    width_x = block_x * G
    cells = up_ref.shape[3]
    z_blocks = cells // (block_z * width_x)
    up = up_ref[...].astype(F32)
    down = down_ref[...].astype(F32)

    def cross(a, b, c):
        d, e = (c + 1) % 3, (c + 2) % 3
        return up[a, d] * down[b, e] - up[a, e] * down[b, d]

    planes = [cross(0, 0, c) - cross(1, 1, c) for c in range(3)]
    planes += [cross(0, 1, c) + cross(1, 0, c) for c in range(3)]
    lane = iota((1, 2 * LANES), 1)
    half = lane // LANES
    within = lane % LANES
    slot = within // slot_lanes
    cell = within % slot_lanes
    source_row = iota((LANES, 2 * LANES), 0)
    results = []
    for comp in range(6):
        turned = (slot + 12 - comp - 4 * half) % 6
        source = (cell % zh) * width_x + (block_x * (turned + 4 * half) + cell // zh) % width_x
        source = jnp.where((turned < 4) & (slot < 6), source, -1)
        pick = jnp.where(source_row == source, 1.0, 0.0).astype(BF16)
        wide = jnp.concatenate([planes[comp], planes[comp][:, :LANES]], axis=1)
        rows = []
        for zb in range(z_blocks):
            begin = zb * block_z * width_x
            part = wide[:, begin : begin + LANES]
            high = part.astype(BF16).astype(F32)
            rows += [high, part - high]
        left = jnp.concatenate(rows, axis=0).astype(BF16)
        got = jnp.dot(left, pick, preferred_element_type=F32)
        got = got.reshape(z_blocks, 2, NT, 2 * LANES)
        results.append(got[:, 0] + got[:, 1])
    one_slot = iota((NT, LANES), 1) // slot_lanes
    for zb in range(z_blocks):
        for g in range(G):
            at = (g // 4) * LANES
            value = jnp.zeros((NT, LANES), F32)
            for comp in range(6):
                value = jnp.where(
                    one_slot == (comp + g) % 6, results[comp][zb, :, at : at + LANES], value
                )
            out_ref[zb * G + g] = value


def link_times(links, vec):
    real, imag = [], []
    for a in range(3):
        row = [(links[3 * a + b], links[9 + 3 * a + b]) for b in range(3)]
        real.append(sum(row[b][0] * vec[b] - row[b][1] * vec[3 + b] for b in range(3)))
        imag.append(sum(row[b][0] * vec[3 + b] + row[b][1] * vec[b] for b in range(3)))
    return real + imag


def edge_kernel(links_ref, forward_ref, ready_ref, edge_ref):
    edge_ref[0:6] = forward_ref[:, 0]
    links = [links_ref[i, 0].astype(F32) for i in range(18)]
    after = [forward_ref[c, 1].astype(F32) for c in range(6)]
    for c, value in enumerate(link_times(links, after)):
        high, low = split_two(value)
        edge_ref[6 + c] = high
        edge_ref[12 + c] = low


def phases(group, depth_z, block_z, block_x, scale):
    row = iota((CROWS, LANES), 0)
    angle = ((group * block_z + row // block_x) * PMOM % depth_z).astype(F32)
    angle = angle * (2.0 * math.pi / depth_z)
    inside = row < block_z * block_x
    cos_z = jnp.where(inside, jnp.cos(angle) * scale, 0.0)[:, :1]
    sin_z = jnp.where(inside, jnp.sin(angle) * scale, 0.0)[:, :1]
    return cos_z, sin_z


def chain_kernel(
    depth_z,
    scale,
    block_z,
    block_x,
    table_ref,
    request_ref,
    links_ref,
    links_next_ref,
    forward_ref,
    forward_next_ref,
    chain_ref,
    corner_ref,
    picked_ref,
    link_rows,
    field_rows,
):
    place = lax.axis_index("zs")
    rows_y = links_ref.shape[3]
    zh = block_z + 1
    slot_lanes = zh * XH
    count = block_z * block_x
    no_plane = jnp.zeros((block_x, rows_y), F32)

    def fill_links(i, carry):
        for z in range(block_z):
            link_rows[i, block_x * z : block_x * (z + 1)] = links_ref[i, z].astype(F32)
            at = count + block_x * z
            last = z == block_z - 1
            plane = no_plane if last else links_next_ref[i, z].astype(F32)
            link_rows[i, at : at + block_x] = plane
        return carry

    def fill_field(i, carry):
        for z in range(block_z):
            field_rows[i, block_x * z : block_x * (z + 1)] = forward_ref[i, z].astype(F32)
            at = count + block_x * z
            field_rows[i, at : at + block_x] = forward_next_ref[i, z].astype(F32)
        return carry

    lax.fori_loop(0, 18, fill_links, 0)
    lax.fori_loop(0, 6, fill_field, 0)

    cos_z, sin_z = phases(place // G, depth_z, block_z, block_x, scale)
    total_rows = link_rows.shape[1]

    def step(length, carry):
        for at in range(0, rows_y, LANES):
            lanes = slice(at, at + LANES)
            vec = [
                pltpu.roll(field_rows[c, :, lanes], total_rows - block_x, 0) for c in range(6)
            ]
            for a in range(3):
                real = None
                imag = None
                for b in range(3):
                    link_real = link_rows[a * 3 + b, :, lanes]
                    link_imag = link_rows[9 + a * 3 + b, :, lanes]
                    term_real = link_real * vec[b] - link_imag * vec[3 + b]
                    term_imag = link_real * vec[3 + b] + link_imag * vec[b]
                    real = term_real if real is None else real + term_real
                    imag = term_imag if imag is None else imag + term_imag
                field_rows[a, :, lanes] = real
                field_rows[3 + a, :, lanes] = imag
                top_real, top_imag = real[:CROWS], imag[:CROWS]
                chain_ref[length, a * CROWS : (a + 1) * CROWS, lanes] = (
                    top_real * cos_z - top_imag * sin_z
                )
                chain_ref[length, (3 + a) * CROWS : (4 + a) * CROWS, lanes] = (
                    top_real * sin_z + top_imag * cos_z
                )
        return carry

    lax.fori_loop(0, LMAX, step, 0)

    shape = (6 * CROWS, LANES)
    row = iota(shape, 0)
    lane = iota(shape, 1)
    comp = row // CROWS
    z_step = lane % slot_lanes % zh - row % CROWS // block_x
    x_step = lane % slot_lanes // zh - row % block_x
    here = (lane // slot_lanes == (comp + place % G) % 6) & (row % CROWS < count)
    here = here & (x_step >= 0) & (x_step < 2) & (z_step >= 0) & (z_step < 2)
    table = jnp.broadcast_to(table_ref[0:1], shape)
    for y_step in range(2):
        corner = jnp.where(here, 4 * x_step + 2 * y_step + z_step, 0)
        weights = jnp.where(here, jnp.take_along_axis(table, corner, axis=1), 0.0)
        high, low = split_two(weights)
        corner_ref[0, y_step * 6 * CROWS : (y_step + 1) * 6 * CROWS] = high
        corner_ref[1, y_step * 6 * CROWS : (y_step + 1) * 6 * CROWS] = low

    request = request_ref[...]
    mine = request // LANES == place
    codes = (request % LANES).astype(F32)
    member = jnp.where(mine, 1.0, 0.0)
    below = jnp.where(iota((LANES, LANES), 0) < iota((LANES, LANES), 1), 1.0, 0.0)
    earlier = jnp.dot(member.astype(BF16), below.astype(BF16), preferred_element_type=F32)
    running = jnp.zeros((1, 1), F32)
    picked = jnp.zeros((8, LANES), F32)
    slots = iota((LANES, LANES), 0).astype(F32)
    head = iota((8, LANES), 0) == 0
    for i in range(member.shape[0]):
        key = jnp.where(member[i : i + 1] > 0.5, earlier[i : i + 1] + running, -1.0)
        hits = jnp.where(slots == key, 1.0, 0.0).astype(BF16)
        left = jnp.where(head, codes[i : i + 1], 1.0).astype(BF16)
        picked = picked + lax.dot_general(left, hits, NT_DIMS, preferred_element_type=F32)
        running = running + jnp.sum(member[i : i + 1], axis=1, keepdims=True)
    lane_of = picked[0:1].astype(jnp.int32) + iota((8, LANES), 0) % 2 * NT
    picked_ref[...] = jnp.where(picked[1:2] > 0.5, lane_of, -1)


def tail_kernel(
    depth_z, scale, block_z, block_x, links_ref, links_next_ref, edge_ref, corner_ref, extra_ref
):
    cos_z, sin_z = phases(lax.axis_index("zs") // G, depth_z, block_z, block_x, scale)
    extra_ref[...] = jnp.zeros_like(extra_ref)
    planes = edge_ref[...].astype(F32)
    near = [planes[c] for c in range(6)]
    far = [planes[6 + c] + planes[12 + c] for c in range(6)]
    vecs = [near, far]
    for z in range(2 * block_z - 1, block_z - 3, -1):
        ref = links_ref if z < block_z else links_next_ref
        links = [ref[i, z % block_z].astype(F32) for i in range(18)]
        vecs = [link_times(links, vec) for vec in vecs]
        if z < block_z:
            at = z * block_x
            cos_at, sin_at = cos_z[at : at + block_x], sin_z[at : at + block_x]
            for k, vec in enumerate(vecs):
                kept = k + block_z - 1 - z
                for a in range(3):
                    real, imag = vec[a], vec[3 + a]
                    first = a * CROWS + at
                    extra_ref[kept, first : first + block_x] = real * cos_at - imag * sin_at
                    first = (3 + a) * CROWS + at
                    extra_ref[kept, first : first + block_x] = real * sin_at + imag * cos_at
            vecs = vecs[:-1]


def meet_kernel(block_z, block_x, got_ref, corner_ref, chain_ref, extra_ref, seq_ref, table_ref):
    rows_y = got_ref.shape[0] * NT
    got = got_ref[...].reshape(rows_y, LANES)
    high, low = split_two(got)
    dot = functools.partial(
        lax.dot_general, dimension_numbers=NT_DIMS, preferred_element_type=F32
    )
    both = dot(corner_ref[0], high) + dot(corner_ref[0], low) + dot(corner_ref[1], high)
    size = 6 * CROWS
    seq = both[:size] + pltpu.roll(both[size:], rows_y - NT, 1)
    for comp in range(6):
        for z in range(block_z):
            at = comp * CROWS + z * block_x
            seq_ref[comp, z] = seq[at : at + block_x]
    turned = jnp.concatenate([-seq[3 * CROWS :], seq[: 3 * CROWS]], axis=0)
    sums = []
    for length in range(LMAX):
        chain = chain_ref[length]
        if length >= block_z:
            chain = chain + extra_ref[length - block_z]
        for field in (seq, turned):
            prod = field * chain
            part = prod[:8]
            for at in range(8, size, 8):
                part = part + prod[at : at + 8]
            narrow = part[:, :LANES]
            for at in range(LANES, rows_y, LANES):
                narrow = narrow + part[:, at : at + LANES]
            sums.append(jnp.sum(narrow, axis=0, keepdims=True))
    table = jnp.concatenate(sums, axis=0)
    for shift in (64, 32, 16, 8):
        table = table + pltpu.roll(table, shift, 1)
    mine = iota((2 * LMAX, LANES), 1) // NT == iota((2 * LMAX, LANES), 0)
    flat = jnp.sum(jnp.where(mine, table, 0.0), axis=0, keepdims=True)
    table_ref[...] = jnp.broadcast_to(flat, table_ref.shape)


def final_kernel(tables_ref, picked_ref, out_ref):
    total = jnp.sum(tables_ref[...], axis=0, keepdims=True)
    picked = picked_ref[...]
    value = jnp.take_along_axis(
        jnp.broadcast_to(total, picked.shape), jnp.maximum(picked, 0), axis=1
    )
    value = jnp.where(picked >= 0, value, 0.0)
    out_ref[...] = value[:2, : out_ref.shape[1]]


VMEM = pl.BlockSpec(memory_space=pltpu.VMEM)
SMEM = pl.BlockSpec(memory_space=pltpu.SMEM)


def cost(flops, moved):
    return pl.CostEstimate(flops=flops, bytes_accessed=moved, transcendentals=0)


PARAMS = pltpu.CompilerParams(vmem_limit_bytes=16 * 1024 * 1024)
WIDE_PARAMS = pltpu.CompilerParams(vmem_limit_bytes=60 * 1024 * 1024)


def shards(
    quark_up,
    quark_down,
    forward,
    gauge_links,
    corner_weight,
    corner_offset,
    lengths,
    separations,
    owner_map,
):
    devices = lax.axis_size("zs")
    block_z, block_x, rows_y = forward.shape[3:]
    cells = quark_up.shape[3]
    depth_z = cells // (block_x * G)
    scale = 1.0 / math.sqrt(cells * (rows_y // NT))
    links = gauge_links.reshape(18, block_z, block_x, rows_y)
    field = forward.reshape(6, block_z, block_x, rows_y)

    links_next = passed_along(links, "zs", -G)
    field_next = passed_along(field, "zs", -G)
    requests = (lengths.shape[0] // LANES, LANES)
    payload, request, table = pl.pallas_call(
        functools.partial(pack_kernel, block_z, block_x),
        out_shape=(
            jax.ShapeDtypeStruct((devices, NT, LANES), F32),
            jax.ShapeDtypeStruct(requests, jnp.int32),
            jax.ShapeDtypeStruct((8, LANES), F32),
        ),
        grid=(1,),
        in_specs=[SMEM] * 2
        + [pl.BlockSpec(quark_up.shape, lambda i: (0, 0, 0, 0))] * 2
        + [pl.BlockSpec(requests, lambda i: (0, 0))] * 3,
        out_specs=(
            pl.BlockSpec((devices, NT, LANES), lambda i: (0, 0, 0)),
            pl.BlockSpec(requests, lambda i: (0, 0)),
            pl.BlockSpec((8, LANES), lambda i: (0, 0)),
        ),
        compiler_params=WIDE_PARAMS,
        cost_estimate=cost(2_000_000_000, 400_000),
        name="pack",
    )(
        corner_weight,
        corner_offset.T,
        quark_up,
        quark_down,
        lengths.reshape(requests),
        separations.reshape(requests),
        owner_map.reshape(requests),
    )
    got = lax.all_to_all(payload, "zs", split_axis=0, concat_axis=0, tiled=True)

    past = LMAX - block_z
    chain, corner, picked = pl.pallas_call(
        functools.partial(chain_kernel, depth_z, scale, block_z, block_x),
        out_shape=(
            jax.ShapeDtypeStruct((LMAX, 6 * CROWS, rows_y), F32),
            jax.ShapeDtypeStruct((2, 12 * CROWS, LANES), BF16),
            jax.ShapeDtypeStruct((8, LANES), jnp.int32),
        ),
        in_specs=[VMEM] * 6,
        out_specs=(VMEM,) * 3,
        scratch_shapes=[
            pltpu.VMEM((18, 2 * block_z * block_x, rows_y), F32),
            pltpu.VMEM((6, 2 * block_z * block_x, rows_y), F32),
        ],
        compiler_params=PARAMS,
        cost_estimate=cost(3_000_000_000, 200_000),
        name="chain",
    )(table, request, links, links_next, field, field_next)

    edge = pl.pallas_call(
        edge_kernel,
        out_shape=jax.ShapeDtypeStruct((18, block_x, rows_y), BF16),
        in_specs=[VMEM] * 2 + [pl.BlockSpec(memory_space=pl.ANY)],
        out_specs=VMEM,
        compiler_params=PARAMS,
        cost_estimate=cost(50_000_000, 60_000),
        name="edge",
    )(links, field, corner)
    edge_next = passed_along(edge, "zs", -2 * G)
    extra = pl.pallas_call(
        functools.partial(tail_kernel, depth_z, scale, block_z, block_x),
        out_shape=jax.ShapeDtypeStruct((past, 6 * CROWS, rows_y), F32),
        in_specs=[VMEM] * 3 + [pl.BlockSpec(memory_space=pl.ANY)],
        out_specs=VMEM,
        compiler_params=PARAMS,
        cost_estimate=cost(400_000_000, 200_000),
        name="tail",
    )(links, links_next, edge_next, corner)

    seq, partial = pl.pallas_call(
        functools.partial(meet_kernel, block_z, block_x),
        out_shape=(
            jax.ShapeDtypeStruct((6, block_z, block_x, rows_y), F32),
            jax.ShapeDtypeStruct((devices, LANES), F32),
        ),
        in_specs=[VMEM] * 4,
        out_specs=(VMEM, VMEM),
        compiler_params=PARAMS,
        cost_estimate=cost(2_000_000_000, 1_000_000),
        name="meet",
    )(got, corner, chain, extra)
    tables = lax.all_to_all(
        partial.reshape(devices, 1, LANES), "zs", split_axis=0, concat_axis=0, tiled=True
    ).reshape(devices, LANES)
    owned = pl.pallas_call(
        final_kernel,
        out_shape=jax.ShapeDtypeStruct((2, MOST), F32),
        in_specs=[VMEM] * 2,
        out_specs=VMEM,
        compiler_params=PARAMS,
        name="final",
    )(tables, picked)
    return (seq.reshape(2, 3, 1, block_z, block_x, rows_y), owned.T)


def solution(mesh):
    in_specs = (
        P(None, None, "zs", "grp"),
        P(None, None, "zs", "grp"),
        P(None, None, "zs", None, None, "grp"),
        P(None, None, None, "zs", None, None, "grp"),
        P(),
        P(),
        P("grp"),
        P("grp"),
        P("grp", None),
    )
    out_specs = (P(None, None, "zs", None, None, "grp"), P("zs", "grp"))
    return jax.shard_map(shards, mesh=mesh, in_specs=in_specs, out_specs=out_specs, check_vma=False)
```

```python
import functools
import math

import jax
import jax.numpy as jnp
from jax import lax
from jax.experimental import pallas as pl
from jax.experimental.pallas import tpu as pltpu
from jax.sharding import PartitionSpec as P

NT = 8
LMAX = 8
PMOM = 3
G = 8
MOST = 96
LANES = 128
XH = 3
CROWS = 16

F32 = jnp.float32
BF16 = jnp.bfloat16
NT_DIMS = (((1,), (1,)), ((), ()))


def passed_along(block, axis, distance):
    devices = range(lax.axis_size(axis))
    route = [((i - distance) % len(devices), i) for i in devices]
    return lax.ppermute(block, axis, route)


def split_two(value):
    high = value.astype(BF16)
    return high, (value - high.astype(F32)).astype(BF16)


def iota(shape, axis):
    return lax.broadcasted_iota(jnp.int32, shape, axis)


def pack_kernel(
    block_z,
    block_x,
    weight_ref,
    offset_ref,
    up_ref,
    down_ref,
    lengths_ref,
    separations_ref,
    owners_ref,
    out_ref,
    request_ref,
    table_ref,
):
    codes = lengths_ref[...] * (2 * NT) + separations_ref[...]
    request_ref[...] = owners_ref[...] * LANES + codes
    lane = iota((8, LANES), 1)
    table = jnp.zeros((8, LANES), F32)
    for k in range(8):
        corner = offset_ref[0, k] * 4 + offset_ref[1, k] * 2 + offset_ref[2, k]
        table = jnp.where(lane == corner, weight_ref[k], table)
    table_ref[...] = table
    zh = block_z + 1
    slot_lanes = zh * XH
    width_x = block_x * G
    cells = up_ref.shape[3]
    z_blocks = cells // (block_z * width_x)
    up = up_ref[...].astype(F32)
    down = down_ref[...].astype(F32)

    def cross(a, b, c):
        d, e = (c + 1) % 3, (c + 2) % 3
        return up[a, d] * down[b, e] - up[a, e] * down[b, d]

    planes = [cross(0, 0, c) - cross(1, 1, c) for c in range(3)]
    planes += [cross(0, 1, c) + cross(1, 0, c) for c in range(3)]
    lane = iota((1, 2 * LANES), 1)
    half = lane // LANES
    within = lane % LANES
    slot = within // slot_lanes
    cell = within % slot_lanes
    source_row = iota((LANES, 2 * LANES), 0)
    results = []
    for comp in range(6):
        turned = (slot + 12 - comp - 4 * half) % 6
        source = (cell % zh) * width_x + (block_x * (turned + 4 * half) + cell // zh) % width_x
        source = jnp.where((turned < 4) & (slot < 6), source, -1)
        pick = jnp.where(source_row == source, 1.0, 0.0).astype(BF16)
        wide = jnp.concatenate([planes[comp], planes[comp][:, :LANES]], axis=1)
        rows = []
        for zb in range(z_blocks):
            begin = zb * block_z * width_x
            part = wide[:, begin : begin + LANES]
            high = part.astype(BF16).astype(F32)
            rows += [high, part - high]
        left = jnp.concatenate(rows, axis=0).astype(BF16)
        got = jnp.dot(left, pick, preferred_element_type=F32)
        got = got.reshape(z_blocks, 2, NT, 2 * LANES)
        results.append(got[:, 0] + got[:, 1])
    one_slot = iota((NT, LANES), 1) // slot_lanes
    for zb in range(z_blocks):
        for g in range(G):
            at = (g // 4) * LANES
            value = jnp.zeros((NT, LANES), F32)
            for comp in range(6):
                value = jnp.where(
                    one_slot == (comp + g) % 6, results[comp][zb, :, at : at + LANES], value
                )
            out_ref[zb * G + g] = value


def link_times(links, vec):
    real, imag = [], []
    for a in range(3):
        row = [(links[3 * a + b], links[9 + 3 * a + b]) for b in range(3)]
        real.append(sum(row[b][0] * vec[b] - row[b][1] * vec[3 + b] for b in range(3)))
        imag.append(sum(row[b][0] * vec[3 + b] + row[b][1] * vec[b] for b in range(3)))
    return real + imag


def edge_kernel(links_ref, forward_ref, ready_ref, edge_ref):
    edge_ref[0:6] = forward_ref[:, 0]
    links = [links_ref[i, 0].astype(F32) for i in range(18)]
    after = [forward_ref[c, 1].astype(F32) for c in range(6)]
    for c, value in enumerate(link_times(links, after)):
        high, low = split_two(value)
        edge_ref[6 + c] = high
        edge_ref[12 + c] = low


def phases(group, depth_z, block_z, block_x, scale):
    row = iota((CROWS, LANES), 0)
    angle = ((group * block_z + row // block_x) * PMOM % depth_z).astype(F32)
    angle = angle * (2.0 * math.pi / depth_z)
    inside = row < block_z * block_x
    cos_z = jnp.where(inside, jnp.cos(angle) * scale, 0.0)[:, :1]
    sin_z = jnp.where(inside, jnp.sin(angle) * scale, 0.0)[:, :1]
    return cos_z, sin_z


def chain_kernel(
    depth_z,
    scale,
    block_z,
    block_x,
    table_ref,
    request_ref,
    links_ref,
    links_next_ref,
    forward_ref,
    forward_next_ref,
    chain_ref,
    corner_ref,
    picked_ref,
    link_rows,
    field_rows,
):
    place = lax.axis_index("zs")
    rows_y = links_ref.shape[3]
    zh = block_z + 1
    slot_lanes = zh * XH
    count = block_z * block_x
    no_plane = jnp.zeros((block_x, rows_y), F32)

    def fill_links(i, carry):
        for z in range(block_z):
            link_rows[i, block_x * z : block_x * (z + 1)] = links_ref[i, z].astype(F32)
            at = count + block_x * z
            last = z == block_z - 1
            plane = no_plane if last else links_next_ref[i, z].astype(F32)
            link_rows[i, at : at + block_x] = plane
        return carry

    def fill_field(i, carry):
        for z in range(block_z):
            field_rows[i, block_x * z : block_x * (z + 1)] = forward_ref[i, z].astype(F32)
            at = count + block_x * z
            field_rows[i, at : at + block_x] = forward_next_ref[i, z].astype(F32)
        return carry

    lax.fori_loop(0, 18, fill_links, 0)
    lax.fori_loop(0, 6, fill_field, 0)

    cos_z, sin_z = phases(place // G, depth_z, block_z, block_x, scale)
    total_rows = link_rows.shape[1]

    def step(length, carry):
        for at in range(0, rows_y, LANES):
            lanes = slice(at, at + LANES)
            vec = [
                pltpu.roll(field_rows[c, :, lanes], total_rows - block_x, 0) for c in range(6)
            ]
            for a in range(3):
                real = None
                imag = None
                for b in range(3):
                    link_real = link_rows[a * 3 + b, :, lanes]
                    link_imag = link_rows[9 + a * 3 + b, :, lanes]
                    term_real = link_real * vec[b] - link_imag * vec[3 + b]
                    term_imag = link_real * vec[3 + b] + link_imag * vec[b]
                    real = term_real if real is None else real + term_real
                    imag = term_imag if imag is None else imag + term_imag
                field_rows[a, :, lanes] = real
                field_rows[3 + a, :, lanes] = imag
                top_real, top_imag = real[:CROWS], imag[:CROWS]
                chain_ref[length, a * CROWS : (a + 1) * CROWS, lanes] = (
                    top_real * cos_z - top_imag * sin_z
                )
                chain_ref[length, (3 + a) * CROWS : (4 + a) * CROWS, lanes] = (
                    top_real * sin_z + top_imag * cos_z
                )
        return carry

    lax.fori_loop(0, LMAX, step, 0)

    shape = (6 * CROWS, LANES)
    row = iota(shape, 0)
    lane = iota(shape, 1)
    comp = row // CROWS
    z_step = lane % slot_lanes % zh - row % CROWS // block_x
    x_step = lane % slot_lanes // zh - row % block_x
    here = (lane // slot_lanes == (comp + place % G) % 6) & (row % CROWS < count)
    here = here & (x_step >= 0) & (x_step < 2) & (z_step >= 0) & (z_step < 2)
    table = jnp.broadcast_to(table_ref[0:1], shape)
    for y_step in range(2):
        corner = jnp.where(here, 4 * x_step + 2 * y_step + z_step, 0)
        weights = jnp.where(here, jnp.take_along_axis(table, corner, axis=1), 0.0)
        high, low = split_two(weights)
        rows = slice(y_step * 6 * CROWS, (y_step + 1) * 6 * CROWS)
        corner_ref[rows] = jnp.concatenate([high, high, low], axis=1)

    request = request_ref[...]
    mine = request // LANES == place
    codes = (request % LANES).astype(F32)
    member = jnp.where(mine, 1.0, 0.0)
    below = jnp.where(iota((LANES, LANES), 0) < iota((LANES, LANES), 1), 1.0, 0.0)
    earlier = jnp.dot(member.astype(BF16), below.astype(BF16), preferred_element_type=F32)
    running = jnp.zeros((1, 1), F32)
    picked = jnp.zeros((8, LANES), F32)
    slots = iota((LANES, LANES), 0).astype(F32)
    head = iota((8, LANES), 0) == 0
    for i in range(member.shape[0]):
        key = jnp.where(member[i : i + 1] > 0.5, earlier[i : i + 1] + running, -1.0)
        hits = jnp.where(slots == key, 1.0, 0.0).astype(BF16)
        left = jnp.where(head, codes[i : i + 1], 1.0).astype(BF16)
        picked = picked + lax.dot_general(left, hits, NT_DIMS, preferred_element_type=F32)
        running = running + jnp.sum(member[i : i + 1], axis=1, keepdims=True)
    lane_of = picked[0:1].astype(jnp.int32) + iota((8, LANES), 0) % 2 * NT
    picked_ref[...] = jnp.where(picked[1:2] > 0.5, lane_of, -1)


def tail_kernel(
    depth_z, scale, block_z, block_x, links_ref, links_next_ref, edge_ref, corner_ref, extra_ref
):
    cos_z, sin_z = phases(lax.axis_index("zs") // G, depth_z, block_z, block_x, scale)
    extra_ref[...] = jnp.zeros_like(extra_ref)
    planes = edge_ref[...].astype(F32)
    near = [planes[c] for c in range(6)]
    far = [planes[6 + c] + planes[12 + c] for c in range(6)]
    vecs = [near, far]
    for z in range(2 * block_z - 1, block_z - 3, -1):
        ref = links_ref if z < block_z else links_next_ref
        links = [ref[i, z % block_z].astype(F32) for i in range(18)]
        vecs = [link_times(links, vec) for vec in vecs]
        if z < block_z:
            at = z * block_x
            cos_at, sin_at = cos_z[at : at + block_x], sin_z[at : at + block_x]
            for k, vec in enumerate(vecs):
                kept = k + block_z - 1 - z
                for a in range(3):
                    real, imag = vec[a], vec[3 + a]
                    first = a * CROWS + at
                    extra_ref[kept, first : first + block_x] = real * cos_at - imag * sin_at
                    first = (3 + a) * CROWS + at
                    extra_ref[kept, first : first + block_x] = real * sin_at + imag * cos_at
            vecs = vecs[:-1]


def meet_kernel(block_z, block_x, got_ref, corner_ref, chain_ref, extra_ref, seq_ref, table_ref):
    rows_y = got_ref.shape[0] * NT
    got = got_ref[...].reshape(rows_y, LANES)
    high, low = split_two(got)
    terms = jnp.concatenate([high, low, high], axis=1)
    both = lax.dot_general(corner_ref[...], terms, NT_DIMS, preferred_element_type=F32)
    size = 6 * CROWS
    seq = both[:size] + pltpu.roll(both[size:], rows_y - NT, 1)
    for comp in range(6):
        for z in range(block_z):
            at = comp * CROWS + z * block_x
            seq_ref[comp, z] = seq[at : at + block_x]
    turned = jnp.concatenate([-seq[3 * CROWS :], seq[: 3 * CROWS]], axis=0)
    sums = []
    for length in range(LMAX):
        chain = chain_ref[length]
        if length >= block_z:
            chain = chain + extra_ref[length - block_z]
        for field in (seq, turned):
            prod = field * chain
            part = prod[:8]
            for at in range(8, size, 8):
                part = part + prod[at : at + 8]
            narrow = part[:, :LANES]
            for at in range(LANES, rows_y, LANES):
                narrow = narrow + part[:, at : at + LANES]
            sums.append(narrow)
    rows = 2 * LMAX * 8
    high, low = split_two(jnp.concatenate(sums, axis=0))
    same_t = jnp.where(iota((LANES, LANES), 0) % NT == iota((LANES, LANES), 1) % NT, 1.0, 0.0)
    table = jnp.dot(
        jnp.concatenate([high, low], axis=0), same_t.astype(BF16), preferred_element_type=F32
    )
    table = table[:rows] + table[rows:]
    mine = iota((rows, LANES), 1) // NT == iota((rows, LANES), 0) // 8
    flat = jnp.sum(jnp.where(mine, table, 0.0), axis=0, keepdims=True)
    table_ref[...] = jnp.broadcast_to(flat, table_ref.shape)


def final_kernel(tables_ref, picked_ref, out_ref):
    total = jnp.sum(tables_ref[...], axis=0, keepdims=True)
    picked = picked_ref[...]
    value = jnp.take_along_axis(
        jnp.broadcast_to(total, picked.shape), jnp.maximum(picked, 0), axis=1
    )
    value = jnp.where(picked >= 0, value, 0.0)
    out_ref[...] = value[:2, : out_ref.shape[1]]


VMEM = pl.BlockSpec(memory_space=pltpu.VMEM)
SMEM = pl.BlockSpec(memory_space=pltpu.SMEM)


def cost(flops, moved):
    return pl.CostEstimate(flops=flops, bytes_accessed=moved, transcendentals=0)


PARAMS = pltpu.CompilerParams(vmem_limit_bytes=16 * 1024 * 1024)
WIDE_PARAMS = pltpu.CompilerParams(vmem_limit_bytes=60 * 1024 * 1024)


def shards(
    quark_up,
    quark_down,
    forward,
    gauge_links,
    corner_weight,
    corner_offset,
    lengths,
    separations,
    owner_map,
):
    devices = lax.axis_size("zs")
    block_z, block_x, rows_y = forward.shape[3:]
    cells = quark_up.shape[3]
    depth_z = cells // (block_x * G)
    scale = 1.0 / math.sqrt(cells * (rows_y // NT))
    links = gauge_links.reshape(18, block_z, block_x, rows_y)
    field = forward.reshape(6, block_z, block_x, rows_y)

    links_next = passed_along(links, "zs", -G)
    field_next = passed_along(field, "zs", -G)
    requests = (lengths.shape[0] // LANES, LANES)
    payload, request, table = pl.pallas_call(
        functools.partial(pack_kernel, block_z, block_x),
        out_shape=(
            jax.ShapeDtypeStruct((devices, NT, LANES), F32),
            jax.ShapeDtypeStruct(requests, jnp.int32),
            jax.ShapeDtypeStruct((8, LANES), F32),
        ),
        grid=(1,),
        in_specs=[SMEM] * 2
        + [pl.BlockSpec(quark_up.shape, lambda i: (0, 0, 0, 0))] * 2
        + [pl.BlockSpec(requests, lambda i: (0, 0))] * 3,
        out_specs=(
            pl.BlockSpec((devices, NT, LANES), lambda i: (0, 0, 0)),
            pl.BlockSpec(requests, lambda i: (0, 0)),
            pl.BlockSpec((8, LANES), lambda i: (0, 0)),
        ),
        compiler_params=WIDE_PARAMS,
        cost_estimate=cost(2_000_000_000, 400_000),
        name="pack",
    )(
        corner_weight,
        corner_offset.T,
        quark_up,
        quark_down,
        lengths.reshape(requests),
        separations.reshape(requests),
        owner_map.reshape(requests),
    )
    got = lax.all_to_all(payload, "zs", split_axis=0, concat_axis=0, tiled=True)

    past = LMAX - block_z
    edge = pl.pallas_call(
        edge_kernel,
        out_shape=jax.ShapeDtypeStruct((18, block_x, rows_y), BF16),
        in_specs=[VMEM] * 2 + [pl.BlockSpec(memory_space=pl.ANY)],
        out_specs=VMEM,
        compiler_params=PARAMS,
        cost_estimate=cost(50_000_000, 60_000),
        name="edge",
    )(links, field, links_next)
    edge_next = passed_along(edge, "zs", -2 * G)
    chain, corner, picked = pl.pallas_call(
        functools.partial(chain_kernel, depth_z, scale, block_z, block_x),
        out_shape=(
            jax.ShapeDtypeStruct((LMAX, 6 * CROWS, rows_y), F32),
            jax.ShapeDtypeStruct((12 * CROWS, 3 * LANES), BF16),
            jax.ShapeDtypeStruct((8, LANES), jnp.int32),
        ),
        in_specs=[VMEM] * 6,
        out_specs=(VMEM,) * 3,
        scratch_shapes=[
            pltpu.VMEM((18, 2 * block_z * block_x, rows_y), F32),
            pltpu.VMEM((6, 2 * block_z * block_x, rows_y), F32),
        ],
        compiler_params=PARAMS,
        cost_estimate=cost(3_000_000_000, 200_000),
        name="chain",
    )(table, request, links, links_next, field, field_next)

    extra = pl.pallas_call(
        functools.partial(tail_kernel, depth_z, scale, block_z, block_x),
        out_shape=jax.ShapeDtypeStruct((past, 6 * CROWS, rows_y), F32),
        in_specs=[VMEM] * 3 + [pl.BlockSpec(memory_space=pl.ANY)],
        out_specs=VMEM,
        compiler_params=PARAMS,
        cost_estimate=cost(400_000_000, 200_000),
        name="tail",
    )(links, links_next, edge_next, corner)

    seq, partial = pl.pallas_call(
        functools.partial(meet_kernel, block_z, block_x),
        out_shape=(
            jax.ShapeDtypeStruct((6, block_z, block_x, rows_y), F32),
            jax.ShapeDtypeStruct((devices, LANES), F32),
        ),
        in_specs=[VMEM] * 4,
        out_specs=(VMEM, VMEM),
        compiler_params=PARAMS,
        cost_estimate=cost(2_000_000_000, 1_000_000),
        name="meet",
    )(got, corner, chain, extra)
    tables = lax.all_to_all(
        partial.reshape(devices, 1, LANES), "zs", split_axis=0, concat_axis=0, tiled=True
    ).reshape(devices, LANES)
    owned = pl.pallas_call(
        final_kernel,
        out_shape=jax.ShapeDtypeStruct((2, MOST), F32),
        in_specs=[VMEM] * 2,
        out_specs=VMEM,
        compiler_params=PARAMS,
        name="final",
    )(tables, picked)
    return (seq.reshape(2, 3, 1, block_z, block_x, rows_y), owned.T)


def solution(mesh):
    in_specs = (
        P(None, None, "zs", "grp"),
        P(None, None, "zs", "grp"),
        P(None, None, "zs", None, None, "grp"),
        P(None, None, None, "zs", None, None, "grp"),
        P(),
        P(),
        P("grp"),
        P("grp"),
        P("grp", None),
    )
    out_specs = (P(None, None, "zs", None, None, "grp"), P("zs", "grp"))
    return jax.shard_map(shards, mesh=mesh, in_specs=in_specs, out_specs=out_specs, check_vma=False)
```

```python
import functools
import math

import jax
import jax.numpy as jnp
from jax import lax
from jax.experimental import pallas as pl
from jax.experimental.pallas import tpu as pltpu
from jax.sharding import PartitionSpec as P

NT = 8
LMAX = 8
PMOM = 3
G = 8
MOST = 96
LANES = 128
XH = 3
CROWS = 16

F32 = jnp.float32
BF16 = jnp.bfloat16
NT_DIMS = (((1,), (1,)), ((), ()))


def passed_along(block, axis, distance):
    devices = range(lax.axis_size(axis))
    route = [((i - distance) % len(devices), i) for i in devices]
    return lax.ppermute(block, axis, route)


def split_two(value):
    high = value.astype(BF16)
    return high, (value - high.astype(F32)).astype(BF16)


def iota(shape, axis):
    return lax.broadcasted_iota(jnp.int32, shape, axis)


def pack_kernel(
    block_z,
    block_x,
    weight_ref,
    offset_ref,
    up_ref,
    down_ref,
    lengths_ref,
    separations_ref,
    owners_ref,
    out_ref,
    request_ref,
    table_ref,
):
    codes = lengths_ref[...] * (2 * NT) + separations_ref[...]
    request_ref[...] = owners_ref[...] * LANES + codes
    lane = iota((8, LANES), 1)
    table = jnp.zeros((8, LANES), F32)
    for k in range(8):
        corner = offset_ref[0, k] * 4 + offset_ref[1, k] * 2 + offset_ref[2, k]
        table = jnp.where(lane == corner, weight_ref[k], table)
    table_ref[...] = table
    zh = block_z + 1
    slot_lanes = zh * XH
    width_x = block_x * G
    cells = up_ref.shape[3]
    z_blocks = cells // (block_z * width_x)
    up = up_ref[...].astype(F32)
    down = down_ref[...].astype(F32)

    def cross(a, b, c):
        d, e = (c + 1) % 3, (c + 2) % 3
        return up[a, d] * down[b, e] - up[a, e] * down[b, d]

    planes = [cross(0, 0, c) - cross(1, 1, c) for c in range(3)]
    planes += [cross(0, 1, c) + cross(1, 0, c) for c in range(3)]
    lane = iota((1, 2 * LANES), 1)
    half = lane // LANES
    within = lane % LANES
    slot = within // slot_lanes
    cell = within % slot_lanes
    source_row = iota((LANES, 2 * LANES), 0)
    results = []
    for comp in range(6):
        turned = (slot + 12 - comp - 4 * half) % 6
        source = (cell % zh) * width_x + (block_x * (turned + 4 * half) + cell // zh) % width_x
        source = jnp.where((turned < 4) & (slot < 6), source, -1)
        pick = jnp.where(source_row == source, 1.0, 0.0).astype(BF16)
        wide = jnp.concatenate([planes[comp], planes[comp][:, :LANES]], axis=1)
        rows = []
        for zb in range(z_blocks):
            begin = zb * block_z * width_x
            part = wide[:, begin : begin + LANES]
            high = part.astype(BF16).astype(F32)
            rows += [high, part - high]
        left = jnp.concatenate(rows, axis=0).astype(BF16)
        got = jnp.dot(left, pick, preferred_element_type=F32)
        got = got.reshape(z_blocks, 2, NT, 2 * LANES)
        results.append(got[:, 0] + got[:, 1])
    one_slot = iota((NT, LANES), 1) // slot_lanes
    for zb in range(z_blocks):
        for g in range(G):
            at = (g // 4) * LANES
            value = results[0][zb, :, at : at + LANES]
            for comp in range(1, 6):
                value = jnp.where(
                    one_slot == (comp + g) % 6, results[comp][zb, :, at : at + LANES], value
                )
            out_ref[zb * G + g] = value


def link_times(links, vec):
    real, imag = [], []
    for a in range(3):
        row = [(links[3 * a + b], links[9 + 3 * a + b]) for b in range(3)]
        real.append(sum(row[b][0] * vec[b] - row[b][1] * vec[3 + b] for b in range(3)))
        imag.append(sum(row[b][0] * vec[3 + b] + row[b][1] * vec[b] for b in range(3)))
    return real + imag


def edge_kernel(links_ref, forward_ref, ready_ref, edge_ref):
    edge_ref[0:6] = forward_ref[:, 0]
    links = [links_ref[i, 0].astype(F32) for i in range(18)]
    after = [forward_ref[c, 1].astype(F32) for c in range(6)]
    for c, value in enumerate(link_times(links, after)):
        high, low = split_two(value)
        edge_ref[6 + c] = high
        edge_ref[12 + c] = low


def phases(group, depth_z, block_z, block_x, scale):
    row = iota((CROWS, LANES), 0)
    angle = ((group * block_z + row // block_x) * PMOM % depth_z).astype(F32)
    angle = angle * (2.0 * math.pi / depth_z)
    inside = row < block_z * block_x
    cos_z = jnp.where(inside, jnp.cos(angle) * scale, 0.0)[:, :1]
    sin_z = jnp.where(inside, jnp.sin(angle) * scale, 0.0)[:, :1]
    return cos_z, sin_z


def chain_kernel(
    depth_z,
    scale,
    block_z,
    block_x,
    table_ref,
    request_ref,
    links_ref,
    links_next_ref,
    forward_ref,
    forward_next_ref,
    chain_ref,
    corner_ref,
    picked_ref,
    link_rows,
    field_rows,
):
    place = lax.axis_index("zs")
    rows_y = links_ref.shape[3]
    zh = block_z + 1
    slot_lanes = zh * XH
    count = block_z * block_x
    no_plane = jnp.zeros((block_x, rows_y), F32)

    def fill_links(i, carry):
        for z in range(block_z):
            link_rows[i, block_x * z : block_x * (z + 1)] = links_ref[i, z].astype(F32)
            at = count + block_x * z
            last = z == block_z - 1
            plane = no_plane if last else links_next_ref[i, z].astype(F32)
            link_rows[i, at : at + block_x] = plane
        return carry

    def fill_field(i, carry):
        for z in range(block_z):
            field_rows[i, block_x * z : block_x * (z + 1)] = forward_ref[i, z].astype(F32)
            at = count + block_x * z
            field_rows[i, at : at + block_x] = forward_next_ref[i, z].astype(F32)
        return carry

    lax.fori_loop(0, 18, fill_links, 0)
    lax.fori_loop(0, 6, fill_field, 0)

    cos_z, sin_z = phases(place // G, depth_z, block_z, block_x, scale)
    total_rows = link_rows.shape[1]

    def step(length, carry):
        for at in range(0, rows_y, LANES):
            lanes = slice(at, at + LANES)
            vec = [
                pltpu.roll(field_rows[c, :, lanes], total_rows - block_x, 0) for c in range(6)
            ]
            for a in range(3):
                real = None
                imag = None
                for b in range(3):
                    link_real = link_rows[a * 3 + b, :, lanes]
                    link_imag = link_rows[9 + a * 3 + b, :, lanes]
                    term_real = link_real * vec[b] - link_imag * vec[3 + b]
                    term_imag = link_real * vec[3 + b] + link_imag * vec[b]
                    real = term_real if real is None else real + term_real
                    imag = term_imag if imag is None else imag + term_imag
                field_rows[a, :, lanes] = real
                field_rows[3 + a, :, lanes] = imag
                top_real, top_imag = real[:CROWS], imag[:CROWS]
                chain_ref[length, a * CROWS : (a + 1) * CROWS, lanes] = (
                    top_real * cos_z - top_imag * sin_z
                )
                chain_ref[length, (3 + a) * CROWS : (4 + a) * CROWS, lanes] = (
                    top_real * sin_z + top_imag * cos_z
                )
        return carry

    lax.fori_loop(0, LMAX, step, 0)

    shape = (6 * CROWS, LANES)
    row = iota(shape, 0)
    lane = iota(shape, 1)
    comp = row // CROWS
    z_step = lane % slot_lanes % zh - row % CROWS // block_x
    x_step = lane % slot_lanes // zh - row % block_x
    here = (lane // slot_lanes == (comp + place % G) % 6) & (row % CROWS < count)
    here = here & (x_step >= 0) & (x_step < 2) & (z_step >= 0) & (z_step < 2)
    table = jnp.broadcast_to(table_ref[0:1], shape)
    for y_step in range(2):
        corner = jnp.where(here, 4 * x_step + 2 * y_step + z_step, 0)
        weights = jnp.where(here, jnp.take_along_axis(table, corner, axis=1), 0.0)
        high, low = split_two(weights)
        rows = slice(y_step * 6 * CROWS, (y_step + 1) * 6 * CROWS)
        corner_ref[rows] = jnp.concatenate([high, high, low], axis=1)

    request = request_ref[...]
    mine = request // LANES == place
    codes = (request % LANES).astype(F32)
    member = jnp.where(mine, 1.0, 0.0)
    below = jnp.where(iota((LANES, LANES), 0) < iota((LANES, LANES), 1), 1.0, 0.0)
    earlier = jnp.dot(member.astype(BF16), below.astype(BF16), preferred_element_type=F32)
    running = jnp.zeros((1, 1), F32)
    picked = jnp.zeros((8, LANES), F32)
    slots = iota((LANES, LANES), 0).astype(F32)
    head = iota((8, LANES), 0) == 0
    for i in range(member.shape[0]):
        key = jnp.where(member[i : i + 1] > 0.5, earlier[i : i + 1] + running, -1.0)
        hits = jnp.where(slots == key, 1.0, 0.0).astype(BF16)
        left = jnp.where(head, codes[i : i + 1], 1.0).astype(BF16)
        picked = picked + lax.dot_general(left, hits, NT_DIMS, preferred_element_type=F32)
        running = running + jnp.sum(member[i : i + 1], axis=1, keepdims=True)
    lane_of = picked[0:1].astype(jnp.int32) + iota((8, LANES), 0) % 2 * NT
    picked_ref[...] = jnp.where(picked[1:2] > 0.5, lane_of, -1)


def tail_kernel(
    depth_z, scale, block_z, block_x, links_ref, links_next_ref, edge_ref, corner_ref, extra_ref
):
    cos_z, sin_z = phases(lax.axis_index("zs") // G, depth_z, block_z, block_x, scale)
    extra_ref[...] = jnp.zeros_like(extra_ref)
    planes = edge_ref[...].astype(F32)
    near = [planes[c] for c in range(6)]
    far = [planes[6 + c] + planes[12 + c] for c in range(6)]
    vecs = [near, far]
    for z in range(2 * block_z - 1, block_z - 3, -1):
        ref = links_ref if z < block_z else links_next_ref
        links = [ref[i, z % block_z].astype(F32) for i in range(18)]
        vecs = [link_times(links, vec) for vec in vecs]
        if z < block_z:
            at = z * block_x
            cos_at, sin_at = cos_z[at : at + block_x], sin_z[at : at + block_x]
            for k, vec in enumerate(vecs):
                kept = k + block_z - 1 - z
                for a in range(3):
                    real, imag = vec[a], vec[3 + a]
                    first = a * CROWS + at
                    extra_ref[kept, first : first + block_x] = real * cos_at - imag * sin_at
                    first = (3 + a) * CROWS + at
                    extra_ref[kept, first : first + block_x] = real * sin_at + imag * cos_at
            vecs = vecs[:-1]


def meet_kernel(block_z, block_x, got_ref, corner_ref, chain_ref, extra_ref, seq_ref, table_ref):
    rows_y = got_ref.shape[0] * NT
    got = got_ref[...].reshape(rows_y, LANES)
    high, low = split_two(got)
    terms = jnp.concatenate([high, low, high], axis=1)
    both = lax.dot_general(corner_ref[...], terms, NT_DIMS, preferred_element_type=F32)
    size = 6 * CROWS
    seq = both[:size] + pltpu.roll(both[size:], rows_y - NT, 1)
    for comp in range(6):
        for z in range(block_z):
            at = comp * CROWS + z * block_x
            seq_ref[comp, z] = seq[at : at + block_x]
    turned = jnp.concatenate([-seq[3 * CROWS :], seq[: 3 * CROWS]], axis=0)
    sums = []
    for length in range(LMAX):
        chain = chain_ref[length]
        if length >= block_z:
            chain = chain + extra_ref[length - block_z]
        for field in (seq, turned):
            prod = field * chain
            part = prod[:8]
            for at in range(8, size, 8):
                part = part + prod[at : at + 8]
            narrow = part[:, :LANES]
            for at in range(LANES, rows_y, LANES):
                narrow = narrow + part[:, at : at + LANES]
            sums.append(narrow)
    rows = 2 * LMAX * 8
    high, low = split_two(jnp.concatenate(sums, axis=0))
    same_t = jnp.where(iota((LANES, LANES), 0) % NT == iota((LANES, LANES), 1) % NT, 1.0, 0.0)
    table = jnp.dot(
        jnp.concatenate([high, low], axis=0), same_t.astype(BF16), preferred_element_type=F32
    )
    table = table[:rows] + table[rows:]
    mine = iota((rows, LANES), 1) // NT == iota((rows, LANES), 0) // 8
    flat = jnp.sum(jnp.where(mine, table, 0.0), axis=0, keepdims=True)
    table_ref[...] = jnp.broadcast_to(flat, table_ref.shape)


def final_kernel(tables_ref, picked_ref, out_ref):
    total = jnp.sum(tables_ref[...], axis=0, keepdims=True)
    picked = picked_ref[...]
    value = jnp.take_along_axis(
        jnp.broadcast_to(total, picked.shape), jnp.maximum(picked, 0), axis=1
    )
    value = jnp.where(picked >= 0, value, 0.0)
    out_ref[...] = value[:2, : out_ref.shape[1]]


VMEM = pl.BlockSpec(memory_space=pltpu.VMEM)
SMEM = pl.BlockSpec(memory_space=pltpu.SMEM)


def cost(flops, moved):
    return pl.CostEstimate(flops=flops, bytes_accessed=moved, transcendentals=0)


PARAMS = pltpu.CompilerParams(vmem_limit_bytes=16 * 1024 * 1024)
WIDE_PARAMS = pltpu.CompilerParams(vmem_limit_bytes=60 * 1024 * 1024)


def shards(
    quark_up,
    quark_down,
    forward,
    gauge_links,
    corner_weight,
    corner_offset,
    lengths,
    separations,
    owner_map,
):
    devices = lax.axis_size("zs")
    block_z, block_x, rows_y = forward.shape[3:]
    cells = quark_up.shape[3]
    depth_z = cells // (block_x * G)
    scale = 1.0 / math.sqrt(cells * (rows_y // NT))
    links = gauge_links.reshape(18, block_z, block_x, rows_y)
    field = forward.reshape(6, block_z, block_x, rows_y)

    links_next = passed_along(links, "zs", -G)
    field_next = passed_along(field, "zs", -G)
    requests = (lengths.shape[0] // LANES, LANES)
    payload, request, table = pl.pallas_call(
        functools.partial(pack_kernel, block_z, block_x),
        out_shape=(
            jax.ShapeDtypeStruct((devices, NT, LANES), F32),
            jax.ShapeDtypeStruct(requests, jnp.int32),
            jax.ShapeDtypeStruct((8, LANES), F32),
        ),
        grid=(1,),
        in_specs=[SMEM] * 2
        + [pl.BlockSpec(quark_up.shape, lambda i: (0, 0, 0, 0))] * 2
        + [pl.BlockSpec(requests, lambda i: (0, 0))] * 3,
        out_specs=(
            pl.BlockSpec((devices, NT, LANES), lambda i: (0, 0, 0)),
            pl.BlockSpec(requests, lambda i: (0, 0)),
            pl.BlockSpec((8, LANES), lambda i: (0, 0)),
        ),
        compiler_params=WIDE_PARAMS,
        cost_estimate=cost(2_000_000_000, 400_000),
        name="pack",
    )(
        corner_weight,
        corner_offset.T,
        quark_up,
        quark_down,
        lengths.reshape(requests),
        separations.reshape(requests),
        owner_map.reshape(requests),
    )
    got = lax.all_to_all(payload, "zs", split_axis=0, concat_axis=0, tiled=True)

    past = LMAX - block_z
    edge = pl.pallas_call(
        edge_kernel,
        out_shape=jax.ShapeDtypeStruct((18, block_x, rows_y), BF16),
        in_specs=[VMEM] * 2 + [pl.BlockSpec(memory_space=pl.ANY)],
        out_specs=VMEM,
        compiler_params=PARAMS,
        cost_estimate=cost(50_000_000, 60_000),
        name="edge",
    )(links, field, links_next)
    edge_next = passed_along(edge, "zs", -2 * G)
    chain, corner, picked = pl.pallas_call(
        functools.partial(chain_kernel, depth_z, scale, block_z, block_x),
        out_shape=(
            jax.ShapeDtypeStruct((LMAX, 6 * CROWS, rows_y), F32),
            jax.ShapeDtypeStruct((12 * CROWS, 3 * LANES), BF16),
            jax.ShapeDtypeStruct((8, LANES), jnp.int32),
        ),
        in_specs=[VMEM] * 6,
        out_specs=(VMEM,) * 3,
        scratch_shapes=[
            pltpu.VMEM((18, 2 * block_z * block_x, rows_y), F32),
            pltpu.VMEM((6, 2 * block_z * block_x, rows_y), F32),
        ],
        compiler_params=PARAMS,
        cost_estimate=cost(3_000_000_000, 200_000),
        name="chain",
    )(table, request, links, links_next, field, field_next)

    extra = pl.pallas_call(
        functools.partial(tail_kernel, depth_z, scale, block_z, block_x),
        out_shape=jax.ShapeDtypeStruct((past, 6 * CROWS, rows_y), F32),
        in_specs=[VMEM] * 3 + [pl.BlockSpec(memory_space=pl.ANY)],
        out_specs=VMEM,
        compiler_params=PARAMS,
        cost_estimate=cost(400_000_000, 200_000),
        name="tail",
    )(links, links_next, edge_next, corner)

    seq, partial = pl.pallas_call(
        functools.partial(meet_kernel, block_z, block_x),
        out_shape=(
            jax.ShapeDtypeStruct((6, block_z, block_x, rows_y), F32),
            jax.ShapeDtypeStruct((devices, LANES), F32),
        ),
        in_specs=[VMEM] * 4,
        out_specs=(VMEM, VMEM),
        compiler_params=PARAMS,
        cost_estimate=cost(2_000_000_000, 1_000_000),
        name="meet",
    )(got, corner, chain, extra)
    tables = lax.all_to_all(
        partial.reshape(devices, 1, LANES), "zs", split_axis=0, concat_axis=0, tiled=True
    ).reshape(devices, LANES)
    owned = pl.pallas_call(
        final_kernel,
        out_shape=jax.ShapeDtypeStruct((2, MOST), F32),
        in_specs=[VMEM] * 2,
        out_specs=VMEM,
        compiler_params=PARAMS,
        name="final",
    )(tables, picked)
    return (seq.reshape(2, 3, 1, block_z, block_x, rows_y), owned.T)


def solution(mesh):
    in_specs = (
        P(None, None, "zs", "grp"),
        P(None, None, "zs", "grp"),
        P(None, None, "zs", None, None, "grp"),
        P(None, None, None, "zs", None, None, "grp"),
        P(),
        P(),
        P("grp"),
        P("grp"),
        P("grp", None),
    )
    out_specs = (P(None, None, "zs", None, None, "grp"), P("zs", "grp"))
    return jax.shard_map(shards, mesh=mesh, in_specs=in_specs, out_specs=out_specs, check_vma=False)
```
